512 devices in a mesh: replica: 32 (over x_lo, z), brick: 16 (over y, x_hi, core).
Axes of the slice: x: 4 (x_hi: 2, x_lo: 2; x = x_hi * 2 + x_lo), y: 4, z: 16, core: 2. Of those that a mesh axis runs over, the one named last changes fastest.
Arguments:
- atom_locations: float32 [32, 3, 12288], P('replica', None, 'brick'), may hold values from 0 to 160, as said below
- atom_speeds_vector: float32 [32, 3, 12288], P('replica', None, 'brick'), may hold values from -7 to 7
- inertial_amounts: float32 [12288], P('brick'), may hold values from 1 to 4
- electric_loads: float32 [12288], P('brick'), may hold values from -4 to 4
- scatter_strengths: float32 [12288], P('brick'), may hold values from 0.5 to 2
- gaussian_spreads_sigma: float32 [12288], P('brick'), may hold values from 0.7 to 1.4
- atom_present_flags: int32 [12288], P('brick'), may hold values 0 or 1
- observed_volume_values: float32 [160, 128, 128], P('brick'), may hold values from 0 to 2
- voxel_reciprocal_spread: float32 [160, 128, 128], P('brick'), may hold values from 0.5 to 4
- paired_partner_lists: int32 [96, 14], P('brick'), may hold values from 0 to 9
- cell_usage_tally: int32 [96], P('brick'), may hold values from 1 to 14, as said below
- halo_sender_spots: int32 [2, 4096], P(None, 'brick'), may hold values from 0 to 767
- target_warmth_levels: int32 [32], P('replica'), may hold values from 280 to 399
Outputs:
- new_positions: float32 [32, 3, 12288], P('replica', None, 'brick')
- new_velocities: float32 [32, 3, 12288], P('replica', None, 'brick')
- deviation: float32 [160, 128, 128], P('brick', 'replica')
The draws below stay inside these ranges and needn't reach their ends.
Inputs may be any that keep to these rules, and one draw needn't show every extreme that they name: `atom_locations`: atoms in the slots of brick b have x in [b * 10, (b + 1) * 10), y in [0, 128), z in [0, 128). Only the first cell_usage_tally[c] slots of cell c count; some cell uses all 14 slots.
All inputs are finite; a program needn't handle non-finite values. No bound on the sum of `atom_present_flags` on one device may be relied on, other than what follows from the above.
Results may differ from the reference program's by a relative error of at most 0.00062.
Values may be sent and summed in bfloat16 or wider, within the bound.
A program may use at most 64 MiB of HBM per device.

```python
import math
import jax
import jax.numpy as jnp
from jax import lax

SX = 10
GY = 128
GZ = 128
ATOM_DEV = 768
HALO = 2
CELL = 128
NBR = 14
CELLS = 6
GHOST = 256
BLOCKS = 10
REPLICA_MEMBERS = 32
NX = 160
ATOMS = 12288
N_BRICK = 16


def brick_of(count):
    return (jnp.arange(count, dtype=jnp.int32) // ATOM_DEV).astype(jnp.float32)


def draw_atom_locations(key, part):
    keys = jax.random.split(jax.random.fold_in(key, 11), 1)
    frac = jax.random.uniform(keys[0], (REPLICA_MEMBERS, 3, ATOMS), jnp.float32)
    xpart = (brick_of(ATOMS)[None, :] + frac[:, 0]) * SX
    ypart = frac[:, 1] * GY
    zpart = frac[:, 2] * GZ
    return jnp.stack([xpart, ypart, zpart], axis=1)


def draw_atom_speeds_vector(key, part):
    slabs = ATOMS // ATOM_DEV
    ramp = brick_of(ATOMS) / max(slabs - 1, 1)
    inner = jax.random.fold_in(key, 23)
    base = jnp.clip(jax.random.normal(inner, (REPLICA_MEMBERS, 3, ATOMS), jnp.float32), -4.0, 4.0)
    spread_scale = 1.0 + 0.732 * ramp
    return base * spread_scale[None, None, :]


def draw_cell_usage_tally(key, part):
    keys = jax.random.split(jax.random.fold_in(key, 37), 4)
    slabs = ATOMS // ATOM_DEV
    cells = ATOM_DEV // CELL
    ceiling = jax.random.randint(keys[0], (slabs,), 2, NBR + 1)
    chosen = jax.random.randint(keys[1], (), 0, slabs)
    ceiling = jnp.where(jnp.arange(slabs, dtype=jnp.int32) == chosen, NBR, ceiling)
    counts = jax.random.randint(keys[2], (slabs, cells), ceiling[:, None] // 2 + 1, ceiling[:, None] + 1)
    spot = jax.random.randint(keys[3], (slabs,), 0, cells)
    counts = jnp.where(jnp.arange(cells, dtype=jnp.int32)[None, :] == spot[:, None], ceiling[:, None], counts)
    return counts.reshape(-1).astype(jnp.int32)


def touch_ends(values, own_key, low, top_value):
    extent = values.shape
    spot = [jax.random.randint(jax.random.fold_in(own_key, axis), (), 0, extent[axis]) for axis in range(len(extent))]
    values = values.at[tuple(spot)].set(low)
    longest = extent.index(max(extent))
    spot[longest] = (spot[longest] + 1) % extent[longest]
    return values.at[tuple(spot)].set(top_value)


def shard_levels(stream_key, extent, shards, least, largest):
    loudness, own = 1.0, jax.random.fold_in(stream_key, 6)
    for axis_at, shards_of in shards:
        steps = jnp.exp(jax.random.uniform(jax.random.fold_in(own, axis_at), (shards_of,), jnp.float32, least / len(shards), largest / len(shards)))
        loudness = loudness * jnp.repeat(steps, extent[axis_at] // shards_of).reshape([-1 if axis == axis_at else 1 for axis in range(len(extent))])
    return loudness


def bell_draw(stream_key, extent, scale, most, pieces=(), held_as=jnp.bfloat16):
    loudness = shard_levels(stream_key, extent, pieces, -0.22, 0.18) if pieces else 1.0
    drawn = jax.random.normal(stream_key, extent, jnp.float32) * scale * loudness
    return jnp.minimum(jnp.maximum(drawn, -most), most).astype(held_as)


def setup_inputs(seed: int = 0) -> dict:
    seeds = jax.random.split(jax.random.key(seed), 14)
    atom_locations = draw_atom_locations(jax.random.fold_in(seeds[13], 71), 0)
    atom_speeds_vector = draw_atom_speeds_vector(jax.random.fold_in(seeds[13], 71), 0)
    inertial_amounts = jnp.clip(jnp.exp(math.log(4.0) - 1.3862944 * jax.random.uniform(seeds[2], (ATOMS,), jnp.float32) ** shard_levels(seeds[2], (ATOMS,), ((0, 16),), -0.2, 0.2)), 1.0, 4.0)
    electric_loads = bell_draw(seeds[3], (ATOMS,), 1.0, 4.0, ((0, 16),), jnp.float32)
    scatter_strengths = jnp.clip(jnp.exp(math.log(2.0) - 1.3862944 * jax.random.uniform(seeds[4], (ATOMS,), jnp.float32) ** shard_levels(seeds[4], (ATOMS,), ((0, 16),), -0.2, 0.2)), 0.5, 2.0)
    gaussian_spreads_sigma = jnp.clip(jnp.exp(math.log(1.4) - 0.6931472 * jax.random.uniform(seeds[5], (ATOMS,), jnp.float32) ** shard_levels(seeds[5], (ATOMS,), ((0, 16),), -0.2, 0.2)), 0.7, 1.4)
    atom_present_flags = touch_ends((jax.random.randint(seeds[6], (ATOMS,), 0, 8) < 7).astype(jnp.int32), jax.random.fold_in(seeds[6], 1), 0, 1)
    observed_volume_values = jnp.clip(2.0 * jax.random.uniform(seeds[7], (NX, GY, GZ), jnp.float32) ** shard_levels(seeds[7], (NX, GY, GZ), ((0, 16),), -0.2, 0.2), 0.0, 2.0)
    voxel_reciprocal_spread = jnp.clip(jnp.exp(math.log(4.0) - 2.0794415 * jax.random.uniform(seeds[8], (NX, GY, GZ), jnp.float32) ** shard_levels(seeds[8], (NX, GY, GZ), ((0, 16),), -0.2, 0.2)), 0.5, 4.0)
    paired_partner_lists = touch_ends(jax.random.randint(seeds[9], (N_BRICK * CELLS, NBR), 0, BLOCKS), jax.random.fold_in(seeds[9], 1), 0, BLOCKS - 1).astype(jnp.int32)
    cell_usage_tally = draw_cell_usage_tally(jax.random.fold_in(seeds[13], 71), 0)
    halo_sender_spots = touch_ends(jax.random.randint(seeds[11], (2, N_BRICK * GHOST), 0, ATOM_DEV), jax.random.fold_in(seeds[11], 1), 0, ATOM_DEV - 1).astype(jnp.int32)
    target_warmth_levels = touch_ends(jax.random.randint(seeds[12], (REPLICA_MEMBERS,), 280, 400), jax.random.fold_in(seeds[12], 1), 280, 399).astype(jnp.int32)
    return dict(atom_locations=atom_locations, atom_speeds_vector=atom_speeds_vector, inertial_amounts=inertial_amounts, electric_loads=electric_loads, scatter_strengths=scatter_strengths, gaussian_spreads_sigma=gaussian_spreads_sigma, atom_present_flags=atom_present_flags, observed_volume_values=observed_volume_values, voxel_reciprocal_spread=voxel_reciprocal_spread, paired_partner_lists=paired_partner_lists, cell_usage_tally=cell_usage_tally, halo_sender_spots=halo_sender_spots, target_warmth_levels=target_warmth_levels)


restraint = 0.1
coupling = 5.0
softening = 1.0
timestep = 0.5
boltzmann = 0.015
heat_bath_damping = 0.5

def wrapped(delta, period):
    return delta - period * jnp.floor(delta / period + 0.5)

def factors(grid, coord, inv_var, period):
    delta = wrapped(grid[:, None] - coord[None, :], period)
    value = jnp.exp(-0.5 * delta * delta * inv_var[None, :])
    return (value, delta * inv_var[None, :] * value)

def spread(x_val, y_val, z_fac, amp):

    def one_plane(row):
        left = ((amp * row)[None, :] * y_val).astype(jnp.bfloat16)
        return lax.dot_general(left, z_fac, (((1,), (1,)), ((), ())), preferred_element_type=jnp.float32)
    return lax.map(one_plane, x_val)

def map_forces(grad_ext, x_val, x_der, y_val, y_der, z_pair, amp):
    count = amp.shape[0]

    def one_plane(carry, inputs):
        plane, x_one, x_slope = inputs
        product = jnp.dot(plane, z_pair, preferred_element_type=jnp.float32)
        along = product[:, :count]
        across = product[:, count:]
        first = lax.optimization_barrier(jnp.sum(y_val * along, axis=0))
        second = lax.optimization_barrier(jnp.sum(y_der * along, axis=0))
        third = lax.optimization_barrier(jnp.sum(y_val * across, axis=0))
        return (carry + jnp.stack([x_slope * first, x_one * second, x_one * third]), None)
    total, _ = lax.scan(one_plane, jnp.zeros((3, count), jnp.float32), (grad_ext, x_val, x_der))
    return -amp[None, :] * total

def pair_forces(coords, charge, ghost_low, ghost_high, paired_partner_lists, live, periods, limit):
    own = jnp.concatenate([coords, charge[None, :]], 0).reshape(4, -1, CELL)
    blocks = jnp.concatenate([own, ghost_low.reshape(4, -1, CELL), ghost_high.reshape(4, -1, CELL)], axis=1)
    period = jnp.array([float(p) for p in periods], jnp.float32)[:, None, None, None]

    def slot(index, total):
        partner = jnp.take(blocks, paired_partner_lists[:, index], axis=1)
        delta = wrapped(own[:3, :, :, None] - partner[:3, :, None, :], period)
        dist = lax.optimization_barrier(jnp.sum(delta * delta, axis=0)) + softening
        active = (index < live).astype(jnp.float32)
        scale = coupling * own[3][:, :, None] * partner[3][:, None, :] * active[:, None, None] / (dist * jnp.sqrt(dist))
        return total + lax.optimization_barrier(jnp.sum(scale[None] * delta, axis=3))
    total = lax.fori_loop(0, limit, slot, jnp.zeros((3, own.shape[1], CELL), jnp.float32))
    return total.reshape(3, -1)

def grids(coords, inv_var, brick):
    planes = SX + 2 * HALO
    plane_grid = (brick * SX - HALO + jnp.arange(planes, dtype=jnp.int32)).astype(jnp.float32)
    x_val, x_der = factors(plane_grid, coords[0], inv_var, NX)
    y_val, y_der = factors(jnp.arange(GY, dtype=jnp.int32).astype(jnp.float32), coords[1], inv_var, GY)
    z_val, z_der = factors(jnp.arange(GZ, dtype=jnp.int32).astype(jnp.float32), coords[2], inv_var, GZ)
    z_pair = jnp.concatenate([z_val, z_der], axis=1).astype(jnp.bfloat16)
    return (x_val, x_der, y_val, y_der, z_pair)

def reference(atom_locations, atom_speeds_vector, inertial_amounts, electric_loads, scatter_strengths, gaussian_spreads_sigma, atom_present_flags, observed_volume_values, voxel_reciprocal_spread, paired_partner_lists, cell_usage_tally, halo_sender_spots, target_warmth_levels):
    occupancy = atom_present_flags.astype(jnp.float32)
    amp_b = (occupancy * scatter_strengths).reshape(N_BRICK, ATOM_DEV)
    charge_b = (occupancy * electric_loads).reshape(N_BRICK, ATOM_DEV)
    inv_b = (1.0 / (gaussian_spreads_sigma * gaussian_spreads_sigma)).reshape(N_BRICK, ATOM_DEV)
    bricks = jnp.arange(N_BRICK, dtype=jnp.int32)
    coords_b = atom_locations.reshape(REPLICA_MEMBERS, 3, N_BRICK, ATOM_DEV)

    def spread_one(inputs):
        coords, inv_var, amp, brick = inputs
        x_val, x_der, y_val, y_der, z_pair = grids(coords, inv_var, brick)
        return spread(x_val, y_val, z_pair[:, :ATOM_DEV], amp)

    def spread_member(coords):
        return lax.map(spread_one, (jnp.moveaxis(coords, 1, 0), inv_b, amp_b, bricks))
    partial_value = lax.map(spread_member, coords_b)
    own = partial_value[:, :, HALO:HALO + SX]
    from_lower = jnp.roll(partial_value[:, :, SX + HALO:], 1, axis=1)
    from_upper = jnp.roll(partial_value[:, :, :HALO], -1, axis=1)
    pad_low = jnp.pad(from_lower, ((0, 0), (0, 0), (0, SX - HALO), (0, 0), (0, 0)))
    pad_high = jnp.pad(from_upper, ((0, 0), (0, 0), (SX - HALO, 0), (0, 0), (0, 0)))
    maps = own + pad_low + pad_high
    summed = lax.optimization_barrier(jnp.sum(maps, axis=0)).reshape(NX, GY, GZ)
    deviation = summed / REPLICA_MEMBERS - observed_volume_values
    grad = (restraint * voxel_reciprocal_spread * deviation).astype(jnp.bfloat16)
    ghost_b = halo_sender_spots.reshape(2, N_BRICK, GHOST)
    nbr_b = paired_partner_lists.reshape(N_BRICK, CELLS, NBR)
    live_b = cell_usage_tally.reshape(N_BRICK, CELLS)
    planes = SX + 2 * HALO

    def force_one(inputs):
        coords, inv_var, amp, charge, brick, nbr, live, low, high = inputs
        x_val, x_der, y_val, y_der, z_pair = grids(coords, inv_var, brick)
        plane_ids = jnp.mod(brick * SX - HALO + jnp.arange(planes, dtype=jnp.int32), NX).astype(jnp.int32)
        grad_ext = jnp.take(grad, plane_ids, axis=0)
        restraint_force = map_forces(grad_ext, x_val, x_der, y_val, y_der, z_pair, amp)
        short = pair_forces(coords, charge, low, high, nbr, live, (NX, GY, GZ), NBR)
        return restraint_force + short

    def force_member(coords):
        packets = []
        for side in range(2):
            chosen = ghost_b[side]
            place = jnp.take_along_axis(coords, chosen[None], axis=2)
            charge_part = jnp.take_along_axis(charge_b, chosen, axis=1)
            packets.append(jnp.moveaxis(jnp.concatenate([place, charge_part[None]], 0), 1, 0))
        low = jnp.roll(packets[0], 1, axis=0)
        high = jnp.roll(packets[1], -1, axis=0)
        return lax.map(force_one, (jnp.moveaxis(coords, 1, 0), inv_b, amp_b, charge_b, bricks, nbr_b, live_b, low, high))
    forces = lax.map(force_member, coords_b)
    forces = jnp.moveaxis(forces, 1, 2).reshape(REPLICA_MEMBERS, 3, ATOMS)
    v_half = atom_speeds_vector + timestep * forces / inertial_amounts[None, None, :]
    kinetic = lax.optimization_barrier(jnp.sum(inertial_amounts[None, None, :] * v_half * v_half, axis=(1, 2)))
    present_moment = kinetic / (3 * ATOMS * boltzmann) + 1e-06
    rescale_ratio = jnp.sqrt(1.0 + heat_bath_damping * (target_warmth_levels.astype(jnp.float32) / present_moment - 1.0))
    new_velocities = rescale_ratio[:, None, None] * v_half
    new_positions = atom_locations + timestep * new_velocities
    return (new_positions, new_velocities, deviation)
```

```python
import functools
import math

import jax
import jax.numpy as jnp
from jax import lax
from jax.experimental import pallas as pl
from jax.experimental.pallas import tpu as pltpu
from jax.sharding import PartitionSpec as P

MESH = pl.DeviceIdType.MESH

HALO = 2
CELL = 128
GHOST = 256
LOG2E = 1.4426950408889634

restraint = 0.1
coupling = 5.0
softening = 1.0
timestep = 0.5
boltzmann = 0.015
heat_bath_damping = 0.5

B_STEPS = ((0, 0), (0, 1), (1, 0), (1, 1))


def fixed(coord, period):
    scale = 2.0**31 / period
    return (coord * scale).astype(jnp.int32) << 1


def dot_t(a, b):
    return lax.dot_general(a, b, (((1,), (1,)), ((), ())), preferred_element_type=jnp.float32)


def kernel(
    dims,
    loc,
    vel,
    mass_ref,
    load_ref,
    strength_ref,
    sigma_ref,
    flag_ref,
    spots,
    lists,
    tally,
    warm,
    obs,
    vrs,
    pos_out,
    vel_out,
    dev_out,
    crd,
    zz,
    gxs,
    gxds,
    gys,
    gyds,
    acc,
    rs,
    lo,
    hi,
    obst,
    vrst,
    grd,
    frc,
    frcin,
    gsend,
    glo,
    ghi,
    bx,
    bq,
    by,
    bz,
    colx,
    coly,
    colz,
    pacc,
    kin,
    loc_sem,
    crd_ss,
    crd_rs,
    gh_ss,
    gh_rs,
    ob_ss,
    ob_rs,
    rs_ss,
    rs_rs,
    lo_ss,
    lo_rs,
    hi_ss,
    hi_rs,
    gr_ss,
    gr_rs,
    fr_ss,
    fr_rs,
    kn_ss,
    kn_rs,
):
    members, bricks, thick, rows, depth, atoms = dims
    half = members // 2
    na = half // 2
    planes = thick + 2 * HALO
    wide = planes * 8
    cells = atoms // CELL
    slots = lists.shape[1]
    r = lax.axis_index("replica")
    b = lax.axis_index("brick")
    x, z = r // half, r % half
    zh, zp = z // 2, z % 2
    up, down = (b + 1) % bricks, (b + bricks - 1) % bricks

    def a_peer(d):
        return (x * half + ((zh + d) % na) * 2 + zp, b)

    def b_rep(k):
        dx, dp = B_STEPS[k]
        return ((x + dx) % 2) * half + zh * 2 + (zp + dp) % 2

    barrier = pltpu.get_barrier_semaphore()
    partners = [a_peer(d) for d in range(1, na)]
    partners += [(b_rep(k), b) for k in range(1, 4)]
    partners += [(b_rep(k), n) for k in range(1, 4) for n in (up, down)]
    partners += [(r, (b + d) % bricks) for d in range(1, bricks)]
    for p in partners:
        pl.semaphore_signal(barrier, inc=1, device_id=p, device_id_type=MESH)

    row0 = pl.multiple_of(x * (rows // 2) + zh * 8, 8)
    tile = pl.ds(row0, 8)
    local_copies = [
        pltpu.make_async_copy(src.at[:, tile, :], dst.at[pl.ds(HALO, thick)], loc_sem.at[i])
        for i, (src, dst) in enumerate(((obs, obst), (vrs, vrst)))
    ]
    for c in local_copies:
        c.start()
    occ = flag_ref[...].astype(jnp.float32)
    amp = occ * strength_ref[...]
    q = occ * load_ref[...]
    sigma = sigma_ref[...]
    iv = 1.0 / (sigma * sigma)
    for i in range(3):
        crd[0, i] = loc[0, i : i + 1, :]

    sends = []

    def remote(src, dst, ss, rsem, device):
        c = pltpu.make_async_remote_copy(
            src_ref=src, dst_ref=dst, send_sem=ss, recv_sem=rsem, device_id=device, device_id_type=MESH
        )
        c.start()
        sends.append(c)
        return c

    near = []
    for t in range(1, na):
        near.append((t + 1) // 2 if t % 2 else na - t // 2)

    pl.semaphore_wait(barrier, len(partners))
    crd_in = {}
    for d in reversed(near):
        crd_in[d] = remote(crd.at[0], crd.at[d], crd_ss.at[d], crd_rs.at[d], a_peer(d))
    ob_in = []
    for i, (src, dst) in enumerate(((obs, obst), (vrs, vrst))):
        ob_in.append(
            remote(
                src.at[pl.ds(thick - HALO, HALO), tile, :],
                dst.at[pl.ds(0, HALO)],
                ob_ss.at[2 * i],
                ob_rs.at[2 * i],
                (r, up),
            )
        )
        ob_in.append(
            remote(
                src.at[pl.ds(0, HALO), tile, :],
                dst.at[pl.ds(thick + HALO, HALO)],
                ob_ss.at[2 * i + 1],
                ob_rs.at[2 * i + 1],
                (r, down),
            )
        )

    four = jnp.concatenate([loc[0], q], axis=0)
    first = four.astype(jnp.bfloat16).astype(jnp.float32)
    rest = four - first
    second = rest.astype(jnp.bfloat16).astype(jnp.float32)
    third = rest - second
    pieces = jnp.concatenate([first, second, third, jnp.zeros_like(four)], axis=0).astype(jnp.bfloat16)
    slot_of = lax.broadcasted_iota(jnp.int32, (atoms, GHOST), 0)
    gh_in = []
    for side, (dst, device) in enumerate(((glo, (r, up)), (ghi, (r, down)))):
        chosen = jnp.where(slot_of == spots[side : side + 1, :], 1.0, 0.0).astype(jnp.bfloat16)
        got = jnp.dot(pieces, chosen, preferred_element_type=jnp.float32)
        got = got[0:4] + got[4:8] + got[8:12]
        for i in range(4):
            gsend[side, i] = got[i : i + 1]
        gh_in.append(remote(gsend.at[side], dst, gh_ss.at[side], gh_rs.at[side], device))

    shift_y, shift_z = 32 - int(math.log2(rows)), 32 - int(math.log2(depth))
    unit_y, unit_z = 2.0**-shift_y, 2.0**-shift_z
    ivc = iv * (-0.5 * LOG2E)
    plane_at = (b * thick - HALO + lax.broadcasted_iota(jnp.int32, (16, atoms), 0)).astype(jnp.float32)
    row_in = lax.broadcasted_iota(jnp.int32, (16, atoms), 0)
    row_at = (zh * 8 + (row_in // 8) * (rows // 2) + row_in % 8) << shift_y

    def spread(d, start):
        dx = plane_at - crd[d, 0]
        gx = jnp.exp2(dx * dx * ivc)
        gxs[d] = gx
        gxds[d] = dx * iv * gx
        dy = (row_at - fixed(crd[d, 1], rows)).astype(jnp.float32)
        gy = jnp.exp2(dy * dy * (ivc * unit_y**2))
        gys[d] = gy
        gyds[d] = dy * (iv * unit_y) * gy
        level = lax.broadcasted_iota(jnp.int32, (depth, atoms), 0) << shift_z
        dz = (level - fixed(crd[d, 2], depth)).astype(jnp.float32)
        gz = jnp.exp2(dz * dz * (ivc * unit_z**2))
        zz[d, :, atoms:] = (dz * (iv * unit_z) * gz).astype(jnp.bfloat16)
        gzb = gz.astype(jnp.bfloat16)
        zz[d, :, :atoms] = gzb
        ax = (amp * gx)[:planes]
        for t in range(2):
            left = ax[:, None, :] * gy[None, 8 * t : 8 * t + 8, :]
            part = dot_t(left.reshape(wide, atoms).astype(jnp.bfloat16), gzb)
            if start:
                acc[t] = part
            else:
                acc[t] += part

    spread(0, True)

    for c in range(cells):
        at = slice(c * CELL, (c + 1) * CELL)
        for i, col in enumerate((colx, coly, colz)):
            v = jnp.broadcast_to(loc[0, i : i + 1, at], (CELL, CELL)).T
            col[at] = v * 2.0**shift_z if i == 0 else fixed(v, (rows, depth)[i - 1])

    for t, d in enumerate(near):
        crd_in[d].wait_recv()
        spread(d, False)

    rs_in, lo_in, hi_in = [], [], []
    edge = 2 * HALO * 8
    for k in (3, 2, 1, 0):
        dx, dp = B_STEPS[k]
        t = (x + dx) % 2
        if k:
            rs_in.append(remote(acc.at[t], rs.at[k - 1], rs_ss.at[k], rs_rs.at[k], (b_rep(k), b)))
        lo_in.append(
            remote(acc.at[t, pl.ds(wide - edge, edge)], lo.at[k], lo_ss.at[k], lo_rs.at[k], (b_rep(k), up))
        )
        hi_in.append(remote(acc.at[t, pl.ds(0, edge)], hi.at[k], hi_ss.at[k], hi_rs.at[k], (b_rep(k), down)))

    scale_x = 2.0**shift_z
    for c in range(cells):
        at = slice(c * CELL, (c + 1) * CELL)
        bx[c] = loc[0, 0:1, at] * scale_x
        by[c] = fixed(loc[0, 1:2, at], rows)
        bz[c] = fixed(loc[0, 2:3, at], depth)
        bq[c] = q[:, at]
    zero = jnp.zeros((1, CELL), jnp.float32)
    none = cells + 4
    bx[none] = zero
    bq[none] = zero
    by[none] = jnp.zeros((1, CELL), jnp.int32)
    bz[none] = jnp.zeros((1, CELL), jnp.int32)
    for c in gh_in:
        c.wait_recv()
    period_x = float(thick * bricks)
    for side, src in enumerate((glo, ghi)):
        if side == 0:
            move = jnp.where(b == 0, -period_x, 0.0)
        else:
            move = jnp.where(b == bricks - 1, period_x, 0.0)
        for g in range(2):
            at = slice(g * CELL, (g + 1) * CELL)
            n = cells + 2 * side + g
            bx[n] = (src[0, :, at] + move) * scale_x
            by[n] = fixed(src[1, :, at], rows)
            bz[n] = fixed(src[2, :, at], depth)
            bq[n] = src[3, :, at]

    part_rows = 32
    parts = CELL // part_rows

    def pair(u, _):
        c = u // parts
        at = pl.ds(pl.multiple_of(u * part_rows, part_rows), part_rows)
        xi, yi, zi = colx[at], coly[at], colz[at]
        total = [jnp.zeros((part_rows, CELL), jnp.float32)] * 3
        for s in range(slots):
            n = jnp.where(s < tally[0, c], lists[c, s], none)
            dx = xi - bx[n]
            dy = (yi - by[n]).astype(jnp.float32)
            dz = (zi - bz[n]).astype(jnp.float32)
            if shift_y != shift_z:
                dy = dy * 2.0 ** (shift_z - shift_y)
            inv = lax.rsqrt(dx * dx + dy * dy + dz * dz + softening * 4.0**shift_z)
            pull = inv * inv * inv * bq[n]
            total = [total[0] + pull * dx, total[1] + pull * dy, total[2] + pull * dz]
        for i in range(3):
            pacc[i, at] = total[i]
        return 0

    units = cells * parts
    lax.fori_loop(0, units // 3, pair, 0)

    for c in local_copies:
        c.wait()
    for c in ob_in + rs_in + lo_in + hi_in:
        c.wait_recv()
    total = acc[x] + rs[0] + rs[1] + rs[2]
    low = lo[0] + lo[1] + lo[2] + lo[3]
    high = hi[0] + hi[1] + hi[2] + hi[3]
    total = jnp.concatenate(
        [total[:edge] + low, total[edge : wide - edge], total[wide - edge :] + high], axis=0
    )
    dev = total.reshape(planes, 8, depth) / members - obst[...]
    grad = (restraint * vrst[...] * dev).astype(jnp.bfloat16)
    grd[x] = grad.reshape(wide, depth)
    gr_in = remote(grd.at[x], grd.at[x], gr_ss.at[0], gr_rs.at[0], (b_rep(2), b))
    own = dev[HALO : HALO + thick]
    dev_out[...] = jnp.where(zp == 0, own[:, :4], own[:, 4:])

    lax.fori_loop(units // 3, 2 * units // 3, pair, 0)
    gr_in.wait_recv()

    lanes = 256

    def force(d):
        for c in range(atoms // lanes):
            at = slice(c * lanes, (c + 1) * lanes)
            after = slice(atoms + c * lanes, atoms + (c + 1) * lanes)
            f = [0.0, 0.0, 0.0]
            for t in range(2):
                along = jnp.dot(grd[t], zz[d, :, at], preferred_element_type=jnp.float32)
                across = jnp.dot(grd[t], zz[d, :, after], preferred_element_type=jnp.float32)
                sums = [0.0, 0.0, 0.0]
                for i in range(planes):
                    p = along[8 * i : 8 * i + 8]
                    g = gxs[d, i : i + 1, at]
                    sums[0] += gxds[d, i : i + 1, at] * p
                    sums[1] += g * p
                    sums[2] += g * across[8 * i : 8 * i + 8]
                y = gys[d, 8 * t : 8 * t + 8, at]
                f[0] += y * sums[0]
                f[1] += gyds[d, 8 * t : 8 * t + 8, at] * sums[1]
                f[2] += y * sums[2]
            for i in range(3):
                frc[d, i, :, at] = jnp.sum(f[i], axis=0, keepdims=True)

    fr_in = []
    for d in reversed(near):
        force(d)
        fr_in.append(remote(frc.at[d], frcin.at[d], fr_ss.at[d], fr_rs.at[d], a_peer(na - d)))
    force(0)

    lax.fori_loop(2 * units // 3, units, pair, 0)
    short = []
    gain = coupling * 4.0**shift_z
    for i in range(3):
        line = [
            jnp.sum(pacc[i, c * CELL : (c + 1) * CELL].T, axis=0, keepdims=True) for c in range(cells)
        ]
        short.append((gain * q) * jnp.concatenate(line, axis=1))

    for c in fr_in:
        c.wait_recv()
    mass = mass_ref[...]
    v_half = []
    square = jnp.zeros((1, atoms), jnp.float32)
    for i in range(3):
        f = frc[0, i]
        for d in range(1, na):
            f = f + frcin[d, i]
        v = vel[0, i : i + 1, :] + timestep * (short[i] - amp * f) / mass
        square = square + mass * v * v
        v_half.append(v)
    row = square[:, :CELL]
    for c in range(1, cells):
        row = row + square[:, c * CELL : (c + 1) * CELL]
    kin[0] = row
    kn_in = [
        remote(kin.at[0], kin.at[d], kn_ss.at[d], kn_rs.at[d], (r, (b + d) % bricks))
        for d in range(1, bricks)
    ]
    for c in kn_in:
        c.wait_recv()
    for d in range(1, bricks):
        row = row + kin[d]
    kinetic = jnp.sum(row, axis=1, keepdims=True)
    present = kinetic / (3 * atoms * bricks * boltzmann) + 1e-06
    wanted = jnp.full((1, 1), warm[0, 0].astype(jnp.float32))
    ratio = jnp.sqrt(1.0 + heat_bath_damping * (wanted / present - 1.0))
    for i in range(3):
        v = ratio * v_half[i]
        vel_out[0, i : i + 1, :] = v
        pos_out[0, i : i + 1, :] = loc[0, i : i + 1, :] + timestep * v
    for c in sends:
        c.wait_send()


def local(
    atom_locations,
    atom_speeds_vector,
    inertial_amounts,
    electric_loads,
    scatter_strengths,
    gaussian_spreads_sigma,
    atom_present_flags,
    observed_volume_values,
    voxel_reciprocal_spread,
    paired_partner_lists,
    cell_usage_tally,
    halo_sender_spots,
    target_warmth_levels,
):
    thick, rows, depth = observed_volume_values.shape
    atoms = atom_locations.shape[2]
    members, bricks = lax.axis_size("replica"), lax.axis_size("brick")
    na = members // 4
    planes = thick + 2 * HALO
    wide = planes * 8
    cells = atoms // CELL
    blocks = cells + 5
    f32, bf16, i32 = jnp.float32, jnp.bfloat16, jnp.int32
    vmem = pl.BlockSpec(memory_space=pltpu.VMEM)
    smem = pl.BlockSpec(memory_space=pltpu.SMEM)
    anywhere = pl.BlockSpec(memory_space=pl.ANY)
    edge = 2 * HALO * 8
    scratch = [
        pltpu.VMEM((na, 3, 1, atoms), f32),
        pltpu.VMEM((na, depth, 2 * atoms), bf16),
        pltpu.VMEM((na, 16, atoms), f32),
        pltpu.VMEM((na, 16, atoms), f32),
        pltpu.VMEM((na, 16, atoms), f32),
        pltpu.VMEM((na, 16, atoms), f32),
        pltpu.VMEM((2, wide, depth), f32),
        pltpu.VMEM((3, wide, depth), f32),
        pltpu.VMEM((4, edge, depth), f32),
        pltpu.VMEM((4, edge, depth), f32),
        pltpu.VMEM((planes, 8, depth), f32),
        pltpu.VMEM((planes, 8, depth), f32),
        pltpu.VMEM((2, wide, depth), bf16),
        pltpu.VMEM((na, 3, 1, atoms), f32),
        pltpu.VMEM((na, 3, 1, atoms), f32),
        pltpu.VMEM((2, 4, 1, GHOST), f32),
        pltpu.VMEM((4, 1, GHOST), f32),
        pltpu.VMEM((4, 1, GHOST), f32),
        pltpu.VMEM((blocks, 1, CELL), f32),
        pltpu.VMEM((blocks, 1, CELL), f32),
        pltpu.VMEM((blocks, 1, CELL), i32),
        pltpu.VMEM((blocks, 1, CELL), i32),
        pltpu.VMEM((atoms, CELL), f32),
        pltpu.VMEM((atoms, CELL), i32),
        pltpu.VMEM((atoms, CELL), i32),
        pltpu.VMEM((3, atoms, CELL), f32),
        pltpu.VMEM((bricks, 1, CELL), f32),
        pltpu.SemaphoreType.DMA((2,)),
    ]
    for count in (na, 2, 4, 4, 4, 4, 1, na, bricks):
        scratch += [pltpu.SemaphoreType.DMA((count,))] * 2
    flat = lambda v: v.reshape(1, -1)
    return pl.pallas_call(
        functools.partial(kernel, (members, bricks, thick, rows, depth, atoms)),
        out_shape=(
            jax.ShapeDtypeStruct((1, 3, atoms), f32),
            jax.ShapeDtypeStruct((1, 3, atoms), f32),
            jax.ShapeDtypeStruct((thick, rows // members, depth), f32),
        ),
        in_specs=[vmem] * 8 + [smem] * 3 + [anywhere] * 2,
        out_specs=(vmem, vmem, vmem),
        scratch_shapes=scratch,
        compiler_params=pltpu.CompilerParams(
            collective_id=0, has_side_effects=True, vmem_limit_bytes=40 * 2**20
        ),
        cost_estimate=pl.CostEstimate(
            flops=1_200_000_000, bytes_accessed=400_000, transcendentals=4_000_000
        ),
    )(
        atom_locations,
        atom_speeds_vector,
        flat(inertial_amounts),
        flat(electric_loads),
        flat(scatter_strengths),
        flat(gaussian_spreads_sigma),
        flat(atom_present_flags),
        halo_sender_spots,
        paired_partner_lists,
        flat(cell_usage_tally),
        flat(target_warmth_levels),
        observed_volume_values,
        voxel_reciprocal_spread,
    )


def solution(mesh):
    return jax.shard_map(
        local,
        mesh=mesh,
        in_specs=(
            P("replica", None, "brick"),
            P("replica", None, "brick"),
            P("brick"),
            P("brick"),
            P("brick"),
            P("brick"),
            P("brick"),
            P("brick", None, None),
            P("brick", None, None),
            P("brick", None),
            P("brick"),
            P(None, "brick"),
            P("replica"),
        ),
        out_specs=(
            P("replica", None, "brick"),
            P("replica", None, "brick"),
            P("brick", "replica", None),
        ),
        check_vma=False,
    )
```

```python
import functools
import math

import jax
import jax.numpy as jnp
from jax import lax
from jax.experimental import pallas as pl
from jax.experimental.pallas import tpu as pltpu
from jax.sharding import PartitionSpec as P

MESH = pl.DeviceIdType.MESH

HALO = 2
CELL = 128
GHOST = 256
LOG2E = 1.4426950408889634

restraint = 0.1
coupling = 5.0
softening = 1.0
timestep = 0.5
boltzmann = 0.015
heat_bath_damping = 0.5

B_STEPS = ((0, 0), (0, 1), (1, 0), (1, 1))


def fixed(coord, period):
    scale = 2.0**31 / period
    return (coord * scale).astype(jnp.int32) << 1


def dot_t(a, b):
    return lax.dot_general(a, b, (((1,), (1,)), ((), ())), preferred_element_type=jnp.float32)


def kernel(
    dims,
    loc_at,
    vel_at,
    mass_at,
    load_at,
    strength_at,
    sigma_at,
    flag_at,
    spots_at,
    lists_at,
    tally_at,
    warm_at,
    obs,
    vrs,
    pos_out,
    vel_out,
    dev_out,
    vel,
    mass_ref,
    load_ref,
    strength_ref,
    sigma_ref,
    flag_ref,
    spots,
    lists,
    tally,
    warm,
    crd,
    zz,
    gxs,
    gxds,
    gys,
    gyds,
    acc,
    rs,
    lo,
    hi,
    obst,
    vrst,
    grd,
    frc,
    frcin,
    gsend,
    glo,
    ghi,
    bx,
    bq,
    by,
    bz,
    colx,
    coly,
    colz,
    pacc,
    kin,
    loc_sem,
    crd_ss,
    crd_rs,
    gh_ss,
    gh_rs,
    ob_ss,
    ob_rs,
    rs_ss,
    rs_rs,
    lo_ss,
    lo_rs,
    hi_ss,
    hi_rs,
    gr_ss,
    gr_rs,
    fr_ss,
    fr_rs,
    kn_ss,
    kn_rs,
):
    members, bricks, thick, rows, depth, atoms = dims
    half = members // 2
    na = half // 2
    planes = thick + 2 * HALO
    wide = planes * 8
    cells = atoms // CELL
    slots = lists.shape[1]
    r = lax.axis_index("replica")
    b = lax.axis_index("brick")
    x, z = r // half, r % half
    zh, zp = z // 2, z % 2
    up, down = (b + 1) % bricks, (b + bricks - 1) % bricks

    def a_peer(d):
        return (x * half + ((zh + d) % na) * 2 + zp, b)

    def b_rep(k):
        dx, dp = B_STEPS[k]
        return ((x + dx) % 2) * half + zh * 2 + (zp + dp) % 2

    barrier = pltpu.get_barrier_semaphore()
    partners = [a_peer(d) for d in range(1, na)]
    partners += [(b_rep(k), b) for k in range(1, 4)]
    partners += [(b_rep(k), n) for k in range(1, 4) for n in (up, down)]
    partners += [(r, (b + d) % bricks) for d in range(1, bricks)]
    for p in partners:
        pl.semaphore_signal(barrier, inc=1, device_id=p, device_id_type=MESH)

    row0 = pl.multiple_of(x * (rows // 2) + zh * 8, 8)
    tile = pl.ds(row0, 8)
    fetched = {
        "loc": (loc_at, crd.at[0]),
        "flag": (flag_at, flag_ref.at[0]),
        "strength": (strength_at, strength_ref.at[0]),
        "load": (load_at, load_ref.at[0]),
        "sigma": (sigma_at, sigma_ref.at[0]),
        "spots": (spots_at, spots),
        "lists": (lists_at, lists),
        "tally": (tally_at, tally),
        "obs": (obs.at[:, tile, :], obst.at[pl.ds(HALO, thick)]),
        "vrs": (vrs.at[:, tile, :], vrst.at[pl.ds(HALO, thick)]),
        "vel": (vel_at, vel),
        "mass": (mass_at, mass_ref.at[0]),
        "warm": (warm_at, warm),
    }
    copies = {
        name: pltpu.make_async_copy(src, dst, loc_sem.at[i])
        for i, (name, (src, dst)) in enumerate(fetched.items())
    }
    for c in copies.values():
        c.start()
    for name in ("loc", "flag", "strength", "load", "sigma", "spots"):
        copies[name].wait()
    loc = crd.at[0]
    occ = flag_ref[...].astype(jnp.float32)
    amp = occ * strength_ref[...]
    q = occ * load_ref[...]
    sigma = sigma_ref[...]
    iv = 1.0 / (sigma * sigma)

    sends = []

    def remote(src, dst, ss, rsem, device):
        c = pltpu.make_async_remote_copy(
            src_ref=src, dst_ref=dst, send_sem=ss, recv_sem=rsem, device_id=device, device_id_type=MESH
        )
        c.start()
        sends.append(c)
        return c

    near = []
    for t in range(1, na):
        near.append((t + 1) // 2 if t % 2 else na - t // 2)

    pl.semaphore_wait(barrier, len(partners))
    crd_in = {}
    for d in reversed(near):
        crd_in[d] = remote(crd.at[0], crd.at[d], crd_ss.at[d], crd_rs.at[d], a_peer(d))
    ob_in = []
    for i, (src, dst) in enumerate(((obs, obst), (vrs, vrst))):
        ob_in.append(
            remote(
                src.at[pl.ds(thick - HALO, HALO), tile, :],
                dst.at[pl.ds(0, HALO)],
                ob_ss.at[2 * i],
                ob_rs.at[2 * i],
                (r, up),
            )
        )
        ob_in.append(
            remote(
                src.at[pl.ds(0, HALO), tile, :],
                dst.at[pl.ds(thick + HALO, HALO)],
                ob_ss.at[2 * i + 1],
                ob_rs.at[2 * i + 1],
                (r, down),
            )
        )

    four = jnp.concatenate([loc[0], loc[1], loc[2], q], axis=0)
    first = four.astype(jnp.bfloat16).astype(jnp.float32)
    rest = four - first
    second = rest.astype(jnp.bfloat16).astype(jnp.float32)
    third = rest - second
    pieces = jnp.concatenate([first, second, third, jnp.zeros_like(four)], axis=0).astype(jnp.bfloat16)
    slot_of = lax.broadcasted_iota(jnp.int32, (atoms, GHOST), 0)
    gh_in = []
    for side, (dst, device) in enumerate(((glo, (r, up)), (ghi, (r, down)))):
        chosen = jnp.where(slot_of == spots[side : side + 1, :], 1.0, 0.0).astype(jnp.bfloat16)
        got = jnp.dot(pieces, chosen, preferred_element_type=jnp.float32)
        got = got[0:4] + got[4:8] + got[8:12]
        for i in range(4):
            gsend[side, i] = got[i : i + 1]
        gh_in.append(remote(gsend.at[side], dst, gh_ss.at[side], gh_rs.at[side], device))

    shift_y, shift_z = 32 - int(math.log2(rows)), 32 - int(math.log2(depth))
    unit_y, unit_z = 2.0**-shift_y, 2.0**-shift_z
    ivc = iv * (-0.5 * LOG2E)
    plane_at = (b * thick - HALO + lax.broadcasted_iota(jnp.int32, (16, atoms), 0)).astype(jnp.float32)
    row_in = lax.broadcasted_iota(jnp.int32, (16, atoms), 0)
    row_at = (zh * 8 + (row_in // 8) * (rows // 2) + row_in % 8) << shift_y

    def spread(d, start):
        dx = plane_at - crd[d, 0]
        gx = jnp.exp2(dx * dx * ivc)
        gxs[d] = gx
        gxds[d] = dx * iv * gx
        dy = (row_at - fixed(crd[d, 1], rows)).astype(jnp.float32)
        gy = jnp.exp2(dy * dy * (ivc * unit_y**2))
        gys[d] = gy
        gyds[d] = dy * (iv * unit_y) * gy
        level = lax.broadcasted_iota(jnp.int32, (depth, atoms), 0) << shift_z
        dz = (level - fixed(crd[d, 2], depth)).astype(jnp.float32)
        gz = jnp.exp2(dz * dz * (ivc * unit_z**2))
        zz[d, :, atoms:] = (dz * (iv * unit_z) * gz).astype(jnp.bfloat16)
        gzb = gz.astype(jnp.bfloat16)
        zz[d, :, :atoms] = gzb
        ax = (amp * gx)[:planes]
        for t in range(2):
            left = ax[:, None, :] * gy[None, 8 * t : 8 * t + 8, :]
            part = dot_t(left.reshape(wide, atoms).astype(jnp.bfloat16), gzb)
            if start:
                acc[t] = part
            else:
                acc[t] += part

    spread(0, True)

    for c in range(cells):
        at = slice(c * CELL, (c + 1) * CELL)
        for i, col in enumerate((colx, coly, colz)):
            v = jnp.broadcast_to(loc[i, :, at], (CELL, CELL)).T
            col[at] = v * 2.0**shift_z if i == 0 else fixed(v, (rows, depth)[i - 1])

    for t, d in enumerate(near):
        crd_in[d].wait_recv()
        spread(d, False)

    rs_in, lo_in, hi_in = [], [], []
    edge = 2 * HALO * 8
    for k in (3, 2, 1, 0):
        dx, dp = B_STEPS[k]
        t = (x + dx) % 2
        if k:
            rs_in.append(remote(acc.at[t], rs.at[k - 1], rs_ss.at[k], rs_rs.at[k], (b_rep(k), b)))
        lo_in.append(
            remote(acc.at[t, pl.ds(wide - edge, edge)], lo.at[k], lo_ss.at[k], lo_rs.at[k], (b_rep(k), up))
        )
        hi_in.append(remote(acc.at[t, pl.ds(0, edge)], hi.at[k], hi_ss.at[k], hi_rs.at[k], (b_rep(k), down)))

    scale_x = 2.0**shift_z
    for c in range(cells):
        at = slice(c * CELL, (c + 1) * CELL)
        bx[c] = loc[0, :, at] * scale_x
        by[c] = fixed(loc[1, :, at], rows)
        bz[c] = fixed(loc[2, :, at], depth)
        bq[c] = q[:, at]
    zero = jnp.zeros((1, CELL), jnp.float32)
    none = cells + 4
    bx[none] = zero
    bq[none] = zero
    by[none] = jnp.zeros((1, CELL), jnp.int32)
    bz[none] = jnp.zeros((1, CELL), jnp.int32)
    for c in gh_in:
        c.wait_recv()
    period_x = float(thick * bricks)
    for side, src in enumerate((glo, ghi)):
        if side == 0:
            move = jnp.where(b == 0, -period_x, 0.0)
        else:
            move = jnp.where(b == bricks - 1, period_x, 0.0)
        for g in range(2):
            at = slice(g * CELL, (g + 1) * CELL)
            n = cells + 2 * side + g
            bx[n] = (src[0, :, at] + move) * scale_x
            by[n] = fixed(src[1, :, at], rows)
            bz[n] = fixed(src[2, :, at], depth)
            bq[n] = src[3, :, at]

    part_rows = 32
    parts = CELL // part_rows

    def pair(u, _):
        c = u // parts
        at = pl.ds(pl.multiple_of(u * part_rows, part_rows), part_rows)
        xi, yi, zi = colx[at], coly[at], colz[at]
        total = [jnp.zeros((part_rows, CELL), jnp.float32)] * 3
        for s in range(slots):
            n = jnp.where(s < tally[c], lists[c, s], none)
            dx = xi - bx[n]
            dy = (yi - by[n]).astype(jnp.float32)
            dz = (zi - bz[n]).astype(jnp.float32)
            if shift_y != shift_z:
                dy = dy * 2.0 ** (shift_z - shift_y)
            inv = lax.rsqrt(dx * dx + dy * dy + dz * dz + softening * 4.0**shift_z)
            pull = inv * inv * inv * bq[n]
            total = [total[0] + pull * dx, total[1] + pull * dy, total[2] + pull * dz]
        for i in range(3):
            pacc[i, at] = total[i]
        return 0

    units = cells * parts
    copies["lists"].wait()
    copies["tally"].wait()
    lax.fori_loop(0, units // 3, pair, 0)

    copies["obs"].wait()
    copies["vrs"].wait()
    for c in ob_in + rs_in + lo_in + hi_in:
        c.wait_recv()
    total = acc[x] + rs[0] + rs[1] + rs[2]
    low = lo[0] + lo[1] + lo[2] + lo[3]
    high = hi[0] + hi[1] + hi[2] + hi[3]
    total = jnp.concatenate(
        [total[:edge] + low, total[edge : wide - edge], total[wide - edge :] + high], axis=0
    )
    dev = total.reshape(planes, 8, depth) / members - obst[...]
    grad = (restraint * vrst[...] * dev).astype(jnp.bfloat16)
    grd[x] = grad.reshape(wide, depth)
    gr_in = remote(grd.at[x], grd.at[x], gr_ss.at[0], gr_rs.at[0], (b_rep(2), b))
    own = dev[HALO : HALO + thick]
    dev_out[...] = jnp.where(zp == 0, own[:, :4], own[:, 4:])

    lax.fori_loop(units // 3, 2 * units // 3, pair, 0)
    gr_in.wait_recv()

    lanes = 256

    def force(d):
        for c in range(atoms // lanes):
            at = slice(c * lanes, (c + 1) * lanes)
            after = slice(atoms + c * lanes, atoms + (c + 1) * lanes)
            f = [0.0, 0.0, 0.0]
            for t in range(2):
                along = jnp.dot(grd[t], zz[d, :, at], preferred_element_type=jnp.float32)
                across = jnp.dot(grd[t], zz[d, :, after], preferred_element_type=jnp.float32)
                sums = [0.0, 0.0, 0.0]
                for i in range(planes):
                    p = along[8 * i : 8 * i + 8]
                    g = gxs[d, i : i + 1, at]
                    sums[0] += gxds[d, i : i + 1, at] * p
                    sums[1] += g * p
                    sums[2] += g * across[8 * i : 8 * i + 8]
                y = gys[d, 8 * t : 8 * t + 8, at]
                f[0] += y * sums[0]
                f[1] += gyds[d, 8 * t : 8 * t + 8, at] * sums[1]
                f[2] += y * sums[2]
            for i in range(3):
                frc[d, i, :, at] = jnp.sum(f[i], axis=0, keepdims=True)

    fr_in = []
    for d in reversed(near):
        force(d)
        fr_in.append(remote(frc.at[d], frcin.at[d], fr_ss.at[d], fr_rs.at[d], a_peer(na - d)))
    force(0)

    lax.fori_loop(2 * units // 3, units, pair, 0)
    short = []
    gain = coupling * 4.0**shift_z
    for i in range(3):
        line = [
            jnp.sum(pacc[i, c * CELL : (c + 1) * CELL].T, axis=0, keepdims=True) for c in range(cells)
        ]
        short.append((gain * q) * jnp.concatenate(line, axis=1))

    for c in fr_in:
        c.wait_recv()
    for name in ("vel", "mass", "warm"):
        copies[name].wait()
    mass = mass_ref[...]
    v_half = []
    square = jnp.zeros((1, atoms), jnp.float32)
    for i in range(3):
        f = frc[0, i]
        for d in range(1, na):
            f = f + frcin[d, i]
        v = vel[i] + timestep * (short[i] - amp * f) / mass
        square = square + mass * v * v
        v_half.append(v)
    row = square[:, :CELL]
    for c in range(1, cells):
        row = row + square[:, c * CELL : (c + 1) * CELL]
    kin[0] = row
    kn_in = [
        remote(kin.at[0], kin.at[d], kn_ss.at[d], kn_rs.at[d], (r, (b + d) % bricks))
        for d in range(1, bricks)
    ]
    for c in kn_in:
        c.wait_recv()
    for d in range(1, bricks):
        row = row + kin[d]
    kinetic = jnp.sum(row, axis=1, keepdims=True)
    present = kinetic / (3 * atoms * bricks * boltzmann) + 1e-06
    wanted = jnp.full((1, 1), warm[0].astype(jnp.float32))
    ratio = jnp.sqrt(1.0 + heat_bath_damping * (wanted / present - 1.0))
    for i in range(3):
        v = ratio * v_half[i]
        vel_out[i] = v
        pos_out[i] = loc[i] + timestep * v
    for c in sends:
        c.wait_send()


def local(
    atom_locations,
    atom_speeds_vector,
    inertial_amounts,
    electric_loads,
    scatter_strengths,
    gaussian_spreads_sigma,
    atom_present_flags,
    observed_volume_values,
    voxel_reciprocal_spread,
    paired_partner_lists,
    cell_usage_tally,
    halo_sender_spots,
    target_warmth_levels,
):
    thick, rows, depth = observed_volume_values.shape
    atoms = atom_locations.shape[2]
    members, bricks = lax.axis_size("replica"), lax.axis_size("brick")
    na = members // 4
    planes = thick + 2 * HALO
    wide = planes * 8
    cells = atoms // CELL
    blocks = cells + 5
    f32, bf16, i32 = jnp.float32, jnp.bfloat16, jnp.int32
    vmem = pl.BlockSpec(memory_space=pltpu.VMEM)
    hbm = pl.BlockSpec(memory_space=pltpu.HBM)
    edge = 2 * HALO * 8
    scratch = [
        pltpu.VMEM((3, 1, atoms), f32),
        pltpu.VMEM((1, atoms), f32),
        pltpu.VMEM((1, atoms), f32),
        pltpu.VMEM((1, atoms), f32),
        pltpu.VMEM((1, atoms), f32),
        pltpu.VMEM((1, atoms), i32),
        pltpu.VMEM((2, GHOST), i32),
        pltpu.SMEM(paired_partner_lists.shape, i32),
        pltpu.SMEM((cells,), i32),
        pltpu.SMEM((1,), i32),
        pltpu.VMEM((na, 3, 1, atoms), f32),
        pltpu.VMEM((na, depth, 2 * atoms), bf16),
        pltpu.VMEM((na, 16, atoms), f32),
        pltpu.VMEM((na, 16, atoms), f32),
        pltpu.VMEM((na, 16, atoms), f32),
        pltpu.VMEM((na, 16, atoms), f32),
        pltpu.VMEM((2, wide, depth), f32),
        pltpu.VMEM((3, wide, depth), f32),
        pltpu.VMEM((4, edge, depth), f32),
        pltpu.VMEM((4, edge, depth), f32),
        pltpu.VMEM((planes, 8, depth), f32),
        pltpu.VMEM((planes, 8, depth), f32),
        pltpu.VMEM((2, wide, depth), bf16),
        pltpu.VMEM((na, 3, 1, atoms), f32),
        pltpu.VMEM((na, 3, 1, atoms), f32),
        pltpu.VMEM((2, 4, 1, GHOST), f32),
        pltpu.VMEM((4, 1, GHOST), f32),
        pltpu.VMEM((4, 1, GHOST), f32),
        pltpu.VMEM((blocks, 1, CELL), f32),
        pltpu.VMEM((blocks, 1, CELL), f32),
        pltpu.VMEM((blocks, 1, CELL), i32),
        pltpu.VMEM((blocks, 1, CELL), i32),
        pltpu.VMEM((atoms, CELL), f32),
        pltpu.VMEM((atoms, CELL), i32),
        pltpu.VMEM((atoms, CELL), i32),
        pltpu.VMEM((3, atoms, CELL), f32),
        pltpu.VMEM((bricks, 1, CELL), f32),
        pltpu.SemaphoreType.DMA((13,)),
    ]
    for count in (na, 2, 4, 4, 4, 4, 1, na, bricks):
        scratch += [pltpu.SemaphoreType.DMA((count,))] * 2
    tall = lambda v: v.reshape(3, 1, atoms)
    new_positions, new_velocities, deviation = pl.pallas_call(
        functools.partial(kernel, (members, bricks, thick, rows, depth, atoms)),
        out_shape=(
            jax.ShapeDtypeStruct((3, 1, atoms), f32),
            jax.ShapeDtypeStruct((3, 1, atoms), f32),
            jax.ShapeDtypeStruct((thick, rows // members, depth), f32),
        ),
        in_specs=[hbm] * 13,
        out_specs=(vmem, vmem, vmem),
        scratch_shapes=scratch,
        compiler_params=pltpu.CompilerParams(
            collective_id=0, has_side_effects=True, vmem_limit_bytes=40 * 2**20
        ),
        cost_estimate=pl.CostEstimate(
            flops=1_200_000_000, bytes_accessed=400_000, transcendentals=4_000_000
        ),
    )(
        *(
            pltpu.with_memory_space_constraint(v, pltpu.HBM)
            for v in (
                tall(atom_locations),
                tall(atom_speeds_vector),
                inertial_amounts,
                electric_loads,
                scatter_strengths,
                gaussian_spreads_sigma,
                atom_present_flags,
                halo_sender_spots,
                paired_partner_lists,
                cell_usage_tally,
            )
        ),
        target_warmth_levels,
        pltpu.with_memory_space_constraint(observed_volume_values, pltpu.HBM),
        pltpu.with_memory_space_constraint(voxel_reciprocal_spread, pltpu.HBM),
    )
    return (
        new_positions.reshape(1, 3, atoms),
        new_velocities.reshape(1, 3, atoms),
        deviation,
    )


def solution(mesh):
    return jax.shard_map(
        local,
        mesh=mesh,
        in_specs=(
            P("replica", None, "brick"),
            P("replica", None, "brick"),
            P("brick"),
            P("brick"),
            P("brick"),
            P("brick"),
            P("brick"),
            P("brick", None, None),
            P("brick", None, None),
            P("brick", None),
            P("brick"),
            P(None, "brick"),
            P("replica"),
        ),
        out_specs=(
            P("replica", None, "brick"),
            P("replica", None, "brick"),
            P("brick", "replica", None),
        ),
        check_vma=False,
    )
```

```python
import functools
import math

import jax
import jax.numpy as jnp
from jax import lax
from jax.experimental import pallas as pl
from jax.experimental.pallas import tpu as pltpu
from jax.sharding import PartitionSpec as P

MESH = pl.DeviceIdType.MESH

HALO = 2
CELL = 128
GHOST = 256
LOG2E = 1.4426950408889634

restraint = 0.1
coupling = 5.0
softening = 1.0
timestep = 0.5
boltzmann = 0.015
heat_bath_damping = 0.5


def fixed(coord, period):
    scale = 2.0**31 / period
    return (coord * scale).astype(jnp.int32) << 1


def dot_t(a, b):
    return lax.dot_general(a, b, (((1,), (1,)), ((), ())), preferred_element_type=jnp.float32)


def kernel(
    dims,
    loc_at,
    vel_at,
    mass_at,
    load_at,
    strength_at,
    sigma_at,
    flag_at,
    spots_at,
    lists_at,
    tally_at,
    warm_at,
    obs,
    vrs,
    pos_out,
    vel_out,
    dev_out,
    vel,
    mass_ref,
    load_ref,
    strength_ref,
    sigma_ref,
    flag_ref,
    spots,
    lists,
    tally,
    warm,
    crd,
    zz,
    gxs,
    gxds,
    gys,
    gyds,
    acc,
    rs,
    lo,
    hi,
    obv,
    amps,
    ivs,
    grd,
    frc,
    frcin,
    gsend,
    glo,
    ghi,
    bx,
    bq,
    by,
    bz,
    colx,
    coly,
    colz,
    pacc,
    kin,
    loc_sem,
    crd_ss,
    crd_rs,
    gh_ss,
    gh_rs,
    ob_ss,
    ob_rs,
    rs_ss,
    rs_rs,
    lo_ss,
    lo_rs,
    hi_ss,
    hi_rs,
    fr_ss,
    fr_rs,
    kn_ss,
    kn_rs,
):
    members, bricks, thick, rows, depth, atoms = dims
    na = members // 2
    share = rows // members
    planes = thick + 2 * HALO
    wide = planes * 8
    edge = 2 * HALO * 8
    cells = atoms // CELL
    slots = lists.shape[1]
    r = lax.axis_index("replica")
    b = lax.axis_index("brick")
    x, z = r // na, r % na
    up, down = (b + 1) % bricks, (b + bricks - 1) % bricks
    across = ((1 - x) * na + z, b)

    def a_peer(d):
        return (x * na + (z + d) % na, b)

    def nearest(t):
        odd = t % 2
        return odd * ((t + 1) // 2) + (1 - odd) * ((na - t // 2) % na)

    barrier = pltpu.get_barrier_semaphore()
    partners = [a_peer(d) for d in range(1, na)] + [across]
    partners += [(across[0], up), (across[0], down)]
    partners += [(r, (b + d) % bricks) for d in range(1, bricks)]
    for p in partners:
        pl.semaphore_signal(barrier, inc=1, device_id=p, device_id_type=MESH)

    fetched = {
        "loc": (loc_at, crd.at[0]),
        "flag": (flag_at, flag_ref.at[0]),
        "strength": (strength_at, strength_ref.at[0]),
        "load": (load_at, load_ref.at[0]),
        "sigma": (sigma_at, sigma_ref.at[0]),
        "spots": (spots_at, spots),
        "lists": (lists_at, lists),
        "tally": (tally_at, tally),
        "vel": (vel_at, vel),
        "mass": (mass_at, mass_ref.at[0]),
        "warm": (warm_at, warm),
    }
    for t in range(2):
        tile = pl.ds(pl.multiple_of(t * (rows // 2) + (z // 2) * 8, 8), 8)
        for i, src in enumerate((obs, vrs)):
            fetched["map", t, i] = (src.at[:, tile, :], obv.at[pl.ds(HALO, thick), i, t])
    copies = {
        name: pltpu.make_async_copy(src, dst, loc_sem.at[i])
        for i, (name, (src, dst)) in enumerate(fetched.items())
    }
    for c in copies.values():
        c.start()
    for name in ("loc", "flag", "strength", "load", "sigma", "spots"):
        copies[name].wait()
    loc = crd.at[0]
    occ = flag_ref[...].astype(jnp.float32)
    amp = occ * strength_ref[...]
    q = occ * load_ref[...]
    sigma = sigma_ref[...]
    iv = 1.0 / (sigma * sigma)

    four = jnp.concatenate([loc[0], loc[1], loc[2], q], axis=0)
    first = four.astype(jnp.bfloat16).astype(jnp.float32)
    rest = four - first
    second = rest.astype(jnp.bfloat16).astype(jnp.float32)
    third = rest - second
    pieces = jnp.concatenate([first, second, third, jnp.zeros_like(four)], axis=0).astype(jnp.bfloat16)
    slot_of = lax.broadcasted_iota(jnp.int32, (atoms, GHOST), 0)
    for side in range(2):
        chosen = jnp.where(slot_of == spots[side : side + 1, :], 1.0, 0.0).astype(jnp.bfloat16)
        got = jnp.dot(pieces, chosen, preferred_element_type=jnp.float32)
        got = got[0:4] + got[4:8] + got[8:12]
        for i in range(4):
            gsend[side, i] = got[i : i + 1]

    shift_y, shift_z = 32 - int(math.log2(rows)), 32 - int(math.log2(depth))
    unit_y, unit_z = 2.0**-shift_y, 2.0**-shift_z
    amps[...] = amp
    ivs[...] = iv

    def spread(d):
        amp, iv = amps[...], ivs[...]
        ivc = iv * (-0.5 * LOG2E)
        plane_at = (b * thick - HALO + lax.broadcasted_iota(jnp.int32, (16, atoms), 0)).astype(jnp.float32)
        row_in = lax.broadcasted_iota(jnp.int32, (8, atoms), 0)
        row_at = (z * share + (row_in // share) * (rows // 2) + row_in % share) << shift_y
        dx = plane_at - crd[d, 0]
        gx = jnp.exp2(dx * dx * ivc)
        gxs[d] = gx
        gxds[d] = dx * iv * gx
        dy = (row_at - fixed(crd[d, 1], rows)).astype(jnp.float32)
        gy = jnp.exp2(dy * dy * (ivc * unit_y**2))
        gys[d] = gy
        gyds[d] = dy * (iv * unit_y) * gy
        level = lax.broadcasted_iota(jnp.int32, (depth, atoms), 0) << shift_z
        dz = (level - fixed(crd[d, 2], depth)).astype(jnp.float32)
        gz = jnp.exp2(dz * dz * (ivc * unit_z**2))
        zz[d, :, atoms:] = (dz * (iv * unit_z) * gz).astype(jnp.bfloat16)
        gzb = gz.astype(jnp.bfloat16)
        zz[d, :, :atoms] = gzb
        left = (amp * gx)[:planes, None, :] * gy[None]
        acc[...] += dot_t(left.reshape(wide, atoms).astype(jnp.bfloat16), gzb)

    acc[...] = jnp.zeros_like(acc)

    for c in range(cells):
        at = slice(c * CELL, (c + 1) * CELL)
        for i, col in enumerate((colx, coly, colz)):
            v = jnp.broadcast_to(loc[i, :, at], (CELL, CELL)).T
            col[at] = v * 2.0**shift_z if i == 0 else fixed(v, (rows, depth)[i - 1])

    scale_x = 2.0**shift_z
    for c in range(cells):
        at = slice(c * CELL, (c + 1) * CELL)
        bx[c] = loc[0, :, at] * scale_x
        by[c] = fixed(loc[1, :, at], rows)
        bz[c] = fixed(loc[2, :, at], depth)
        bq[c] = q[:, at]
    none = cells + 4
    for ref in (bx, bq, by, bz):
        ref[none] = jnp.zeros((1, CELL), ref.dtype)

    sends = []

    def remote(src, dst, ss, rsem, device):
        return pltpu.make_async_remote_copy(
            src_ref=src, dst_ref=dst, send_sem=ss, recv_sem=rsem, device_id=device, device_id_type=MESH
        )

    def post(*a):
        c = remote(*a)
        c.start()
        sends.append(c)
        return c

    def crd_copy(d):
        return remote(crd.at[0], crd.at[d], crd_ss.at[d], crd_rs.at[d], a_peer(d))

    pl.semaphore_wait(barrier, len(partners))
    for t in range(na - 1, 0, -1):
        crd_copy(nearest(t)).start()
    gh_in = [
        post(gsend.at[0], glo, gh_ss.at[0], gh_rs.at[0], (r, up)),
        post(gsend.at[1], ghi, gh_ss.at[1], gh_rs.at[1], (r, down)),
    ]
    for t in range(2):
        for i in range(2):
            copies["map", t, i].wait()
    ob_in = [
        post(obv.at[pl.ds(thick, HALO)], obv.at[pl.ds(0, HALO)], ob_ss.at[0], ob_rs.at[0], (r, up)),
        post(
            obv.at[pl.ds(HALO, HALO)],
            obv.at[pl.ds(thick + HALO, HALO)],
            ob_ss.at[1],
            ob_rs.at[1],
            (r, down),
        ),
    ]

    def collect(t, _):
        d = nearest(t)

        @pl.when(t > 0)
        def _():
            crd_copy(d).wait_recv()

        spread(d)
        return 0

    lax.fori_loop(0, na, collect, 0)

    lower, upper = acc.at[pl.ds(0, edge)], acc.at[pl.ds(wide - edge, edge)]
    map_in = [
        post(upper, lo.at[0], lo_ss.at[0], lo_rs.at[0], (across[0], up)),
        post(lower, hi.at[0], hi_ss.at[0], hi_rs.at[0], (across[0], down)),
        post(upper, lo.at[1], lo_ss.at[1], lo_rs.at[1], (r, up)),
        post(lower, hi.at[1], hi_ss.at[1], hi_rs.at[1], (r, down)),
        post(acc, rs, rs_ss.at[0], rs_rs.at[0], across),
    ]

    for c in gh_in:
        c.wait_recv()
    period_x = float(thick * bricks)
    for side, src in enumerate((glo, ghi)):
        if side == 0:
            move = jnp.where(b == 0, -period_x, 0.0)
        else:
            move = jnp.where(b == bricks - 1, period_x, 0.0)
        for g in range(2):
            at = slice(g * CELL, (g + 1) * CELL)
            n = cells + 2 * side + g
            bx[n] = (src[0, :, at] + move) * scale_x
            by[n] = fixed(src[1, :, at], rows)
            bz[n] = fixed(src[2, :, at], depth)
            bq[n] = src[3, :, at]

    part_rows = 32
    parts = CELL // part_rows

    def pair(u, _):
        c = u // parts
        at = pl.ds(pl.multiple_of(u * part_rows, part_rows), part_rows)
        xi, yi, zi = colx[at], coly[at], colz[at]
        total = [jnp.zeros((part_rows, CELL), jnp.float32)] * 3
        for s in range(slots):
            n = jnp.where(s < tally[c], lists[c, s], none)
            dx = xi - bx[n]
            dy = (yi - by[n]).astype(jnp.float32)
            dz = (zi - bz[n]).astype(jnp.float32)
            if shift_y != shift_z:
                dy = dy * 2.0 ** (shift_z - shift_y)
            inv = lax.rsqrt(dx * dx + dy * dy + dz * dz + softening * 4.0**shift_z)
            pull = inv * inv * inv * bq[n]
            total = [total[0] + pull * dx, total[1] + pull * dy, total[2] + pull * dz]
        for i in range(3):
            pacc[i, at] = total[i]
        return 0

    units = cells * parts
    copies["lists"].wait()
    copies["tally"].wait()
    lax.fori_loop(0, units // 2, pair, 0)

    for c in ob_in + map_in:
        c.wait_recv()
    total = acc[...] + rs[...]
    low = lo[0] + lo[1]
    high = hi[0] + hi[1]
    total = jnp.concatenate(
        [total[:edge] + low, total[edge : wide - edge], total[wide - edge :] + high], axis=0
    ).reshape(planes, 8, depth)
    row_in = lax.broadcasted_iota(jnp.int32, (planes, 8, depth), 1)

    def own_rows(i):
        one, two = obv[:, i, 0], obv[:, i, 1]
        turn = lambda v: jnp.concatenate([v[:, share:], v[:, :share]], axis=1)
        even = jnp.where(row_in < share, one, turn(two))
        odd = jnp.where(row_in < share, turn(one), two)
        return jnp.where(z % 2 == 0, even, odd)

    dev = total / members - own_rows(0)
    grad = (restraint * own_rows(1) * dev).astype(jnp.bfloat16)
    grd[...] = grad.reshape(wide, depth)
    own = dev[HALO : HALO + thick]
    dev_out[...] = jnp.where(x == 0, own[:, :share], own[:, share:])

    lanes = 256

    def force(d):
        for c in range(atoms // lanes):
            at = slice(c * lanes, (c + 1) * lanes)
            after = slice(atoms + c * lanes, atoms + (c + 1) * lanes)
            along = jnp.dot(grd[...], zz[d, :, at], preferred_element_type=jnp.float32)
            slope = jnp.dot(grd[...], zz[d, :, after], preferred_element_type=jnp.float32)
            sums = [0.0, 0.0, 0.0]
            for i in range(planes):
                p = along[8 * i : 8 * i + 8]
                g = gxs[d, i : i + 1, at]
                sums[0] += gxds[d, i : i + 1, at] * p
                sums[1] += g * p
                sums[2] += g * slope[8 * i : 8 * i + 8]
            y = gys[d, :, at]
            f = (y * sums[0], gyds[d, :, at] * sums[1], y * sums[2])
            for i in range(3):
                frc[d, i, :, at] = jnp.sum(f[i], axis=0, keepdims=True)

    def fr_copy(d):
        return remote(frc.at[d], frcin.at[d], fr_ss.at[d], fr_rs.at[d], a_peer((na - d) % na))

    def give(t, _):
        d = nearest(na - 1 - t)
        force(d)

        @pl.when(t < na - 1)
        def _():
            fr_copy(d).start()

        return 0

    lax.fori_loop(0, na, give, 0)

    lax.fori_loop(units // 2, units, pair, 0)
    for name in ("vel", "mass", "warm"):
        copies[name].wait()
    mass = mass_ref[...]
    light = timestep / mass
    gain = (coupling * 4.0**shift_z) * q * light
    push = amps[...] * light
    v_half = []
    for i in range(3):
        line = [
            jnp.sum(pacc[i, c * CELL : (c + 1) * CELL].T, axis=0, keepdims=True) for c in range(cells)
        ]
        v_half.append(vel[i] + gain * jnp.concatenate(line, axis=1))

    for d in range(1, na):
        fr_copy(d).wait_recv()
    square = jnp.zeros((1, atoms), jnp.float32)
    for i in range(3):
        f = frc[0, i]
        for d in range(1, na):
            f = f + frcin[d, i]
        v_half[i] = v_half[i] - push * f
        square = square + v_half[i] * v_half[i]
    square = mass * square
    row = square[:, :CELL]
    for c in range(1, cells):
        row = row + square[:, c * CELL : (c + 1) * CELL]
    kin[0] = row
    kn_in = [
        post(kin.at[0], kin.at[d], kn_ss.at[d], kn_rs.at[d], (r, (b + d) % bricks)) for d in range(1, bricks)
    ]
    for c in kn_in:
        c.wait_recv()
    for d in range(1, bricks):
        row = row + kin[d]
    kinetic = jnp.sum(row, axis=1, keepdims=True)
    present = kinetic / (3 * atoms * bricks * boltzmann) + 1e-06
    wanted = jnp.full((1, 1), warm[0].astype(jnp.float32))
    ratio = jnp.sqrt(1.0 + heat_bath_damping * (wanted / present - 1.0))
    for i in range(3):
        v = ratio * v_half[i]
        vel_out[i] = v
        pos_out[i] = loc[i] + timestep * v
    for d in range(1, na):
        crd_copy(d).wait_send()
        fr_copy(d).wait_send()
    for c in sends:
        c.wait_send()


def local(
    atom_locations,
    atom_speeds_vector,
    inertial_amounts,
    electric_loads,
    scatter_strengths,
    gaussian_spreads_sigma,
    atom_present_flags,
    observed_volume_values,
    voxel_reciprocal_spread,
    paired_partner_lists,
    cell_usage_tally,
    halo_sender_spots,
    target_warmth_levels,
):
    thick, rows, depth = observed_volume_values.shape
    atoms = atom_locations.shape[2]
    members, bricks = lax.axis_size("replica"), lax.axis_size("brick")
    na = members // 2
    planes = thick + 2 * HALO
    wide = planes * 8
    cells = atoms // CELL
    blocks = cells + 5
    f32, bf16, i32 = jnp.float32, jnp.bfloat16, jnp.int32
    vmem = pl.BlockSpec(memory_space=pltpu.VMEM)
    hbm = pl.BlockSpec(memory_space=pltpu.HBM)
    edge = 2 * HALO * 8
    scratch = [
        pltpu.VMEM((3, 1, atoms), f32),
        pltpu.VMEM((1, atoms), f32),
        pltpu.VMEM((1, atoms), f32),
        pltpu.VMEM((1, atoms), f32),
        pltpu.VMEM((1, atoms), f32),
        pltpu.VMEM((1, atoms), i32),
        pltpu.VMEM((2, GHOST), i32),
        pltpu.SMEM(paired_partner_lists.shape, i32),
        pltpu.SMEM((cells,), i32),
        pltpu.SMEM((1,), i32),
        pltpu.VMEM((na, 3, 1, atoms), f32),
        pltpu.VMEM((na, depth, 2 * atoms), bf16),
        pltpu.VMEM((na, 16, atoms), f32),
        pltpu.VMEM((na, 16, atoms), f32),
        pltpu.VMEM((na, 8, atoms), f32),
        pltpu.VMEM((na, 8, atoms), f32),
        pltpu.VMEM((wide, depth), f32),
        pltpu.VMEM((wide, depth), f32),
        pltpu.VMEM((2, edge, depth), f32),
        pltpu.VMEM((2, edge, depth), f32),
        pltpu.VMEM((planes, 2, 2, 8, depth), f32),
        pltpu.VMEM((1, atoms), f32),
        pltpu.VMEM((1, atoms), f32),
        pltpu.VMEM((wide, depth), bf16),
        pltpu.VMEM((na, 3, 1, atoms), f32),
        pltpu.VMEM((na, 3, 1, atoms), f32),
        pltpu.VMEM((2, 4, 1, GHOST), f32),
        pltpu.VMEM((4, 1, GHOST), f32),
        pltpu.VMEM((4, 1, GHOST), f32),
        pltpu.VMEM((blocks, 1, CELL), f32),
        pltpu.VMEM((blocks, 1, CELL), f32),
        pltpu.VMEM((blocks, 1, CELL), i32),
        pltpu.VMEM((blocks, 1, CELL), i32),
        pltpu.VMEM((atoms, CELL), f32),
        pltpu.VMEM((atoms, CELL), i32),
        pltpu.VMEM((atoms, CELL), i32),
        pltpu.VMEM((3, atoms, CELL), f32),
        pltpu.VMEM((bricks, 1, CELL), f32),
        pltpu.SemaphoreType.DMA((15,)),
    ]
    for count in (na, 2, 2, 1, 2, 2, na, bricks):
        scratch += [pltpu.SemaphoreType.DMA((count,))] * 2
    tall = lambda v: v.reshape(3, 1, atoms)
    new_positions, new_velocities, deviation = pl.pallas_call(
        functools.partial(kernel, (members, bricks, thick, rows, depth, atoms)),
        out_shape=(
            jax.ShapeDtypeStruct((3, 1, atoms), f32),
            jax.ShapeDtypeStruct((3, 1, atoms), f32),
            jax.ShapeDtypeStruct((thick, rows // members, depth), f32),
        ),
        in_specs=[hbm] * 13,
        out_specs=(vmem, vmem, vmem),
        scratch_shapes=scratch,
        compiler_params=pltpu.CompilerParams(
            collective_id=0, has_side_effects=True, vmem_limit_bytes=40 * 2**20
        ),
        cost_estimate=pl.CostEstimate(
            flops=1_200_000_000, bytes_accessed=400_000, transcendentals=4_000_000
        ),
    )(
        *(
            pltpu.with_memory_space_constraint(v, pltpu.HBM)
            for v in (
                tall(atom_locations),
                tall(atom_speeds_vector),
                inertial_amounts,
                electric_loads,
                scatter_strengths,
                gaussian_spreads_sigma,
                atom_present_flags,
                halo_sender_spots,
                paired_partner_lists,
                cell_usage_tally,
            )
        ),
        target_warmth_levels,
        pltpu.with_memory_space_constraint(observed_volume_values, pltpu.HBM),
        pltpu.with_memory_space_constraint(voxel_reciprocal_spread, pltpu.HBM),
    )
    return (
        new_positions.reshape(1, 3, atoms),
        new_velocities.reshape(1, 3, atoms),
        deviation,
    )


def solution(mesh):
    return jax.shard_map(
        local,
        mesh=mesh,
        in_specs=(
            P("replica", None, "brick"),
            P("replica", None, "brick"),
            P("brick"),
            P("brick"),
            P("brick"),
            P("brick"),
            P("brick"),
            P("brick", None, None),
            P("brick", None, None),
            P("brick", None),
            P("brick"),
            P(None, "brick"),
            P("replica"),
        ),
        out_specs=(
            P("replica", None, "brick"),
            P("replica", None, "brick"),
            P("brick", "replica", None),
        ),
        check_vma=False,
    )
```

```python
import functools
import math

import jax
import jax.numpy as jnp
from jax import lax
from jax.experimental import pallas as pl
from jax.experimental.pallas import tpu as pltpu
from jax.sharding import PartitionSpec as P

MESH = pl.DeviceIdType.MESH

HALO = 2
CELL = 128
GHOST = 256
LOG2E = 1.4426950408889634
B_STEPS = ((0, 0), (0, 1), (1, 0), (1, 1))

restraint = 0.1
coupling = 5.0
softening = 1.0
timestep = 0.5
boltzmann = 0.015
heat_bath_damping = 0.5


def fixed(coord, period):
    scale = 2.0**31 / period
    return (coord * scale).astype(jnp.int32) << 1


def dot_t(a, b):
    return lax.dot_general(a, b, (((1,), (1,)), ((), ())), preferred_element_type=jnp.float32)


def kernel(
    dims,
    loc_at,
    vel_at,
    mass_at,
    load_at,
    strength_at,
    sigma_at,
    flag_at,
    spots_at,
    lists_at,
    tally_at,
    warm_at,
    obs,
    vrs,
    pos_out,
    vel_out,
    dev_out,
    vel,
    mass_ref,
    load_ref,
    strength_ref,
    sigma_ref,
    flag_ref,
    spots,
    lists,
    tally,
    warm,
    crd,
    zz,
    gxs,
    gxds,
    gys,
    gyds,
    acc,
    mine,
    rs,
    lo,
    hi,
    obv,
    amps,
    ivs,
    grd,
    frc,
    frcin,
    gsend,
    glo,
    ghi,
    bx,
    bq,
    by,
    bz,
    colx,
    coly,
    colz,
    pacc,
    kin,
    loc_sem,
    crd_ss,
    crd_rs,
    gh_ss,
    gh_rs,
    ob_ss,
    ob_rs,
    rs_ss,
    rs_rs,
    lo_ss,
    lo_rs,
    hi_ss,
    hi_rs,
    fr_ss,
    fr_rs,
    kn_ss,
    kn_rs,
):
    members, bricks, thick, rows, depth, atoms = dims
    half = members // 2
    na = half // 2
    share = rows // members
    planes = thick + 2 * HALO
    wide = planes * 16
    edge = 2 * HALO * 16
    cells = atoms // CELL
    slots = lists.shape[1]
    r = lax.axis_index("replica")
    b = lax.axis_index("brick")
    x, z = r // half, r % half
    zh, zp = z // 2, z % 2
    up, down = (b + 1) % bricks, (b + bricks - 1) % bricks

    def a_peer(d):
        return (x * half + ((zh + d) % na) * 2 + zp, b)

    def b_rep(k):
        dx, dp = B_STEPS[k]
        return ((x + dx) % 2) * half + zh * 2 + (zp + dp) % 2

    def nearest(t):
        odd = t % 2
        return odd * ((t + 1) // 2) + (1 - odd) * ((na - t // 2) % na)

    direct = [nearest(t) for t in range(1, na)]
    relayed = {}
    if na == 8:
        direct = direct[:4]
        relayed = {1: (3, 2), 7: (5, 6), 2: (4, 2)}

    barrier = pltpu.get_barrier_semaphore()
    partners = [a_peer(d) for d in direct]
    partners += [(b_rep(k), n) for k in range(1, 4) for n in (b, up, down)]
    partners += [(r, (b + d) % bricks) for d in range(1, bricks)]
    for p in partners:
        pl.semaphore_signal(barrier, inc=1, device_id=p, device_id_type=MESH)

    fetched = {
        "loc": (loc_at, crd.at[0]),
        "flag": (flag_at, flag_ref.at[0]),
        "strength": (strength_at, strength_ref.at[0]),
        "load": (load_at, load_ref.at[0]),
        "sigma": (sigma_at, sigma_ref.at[0]),
        "spots": (spots_at, spots),
        "lists": (lists_at, lists),
        "tally": (tally_at, tally),
        "vel": (vel_at, vel),
        "mass": (mass_at, mass_ref.at[0]),
        "warm": (warm_at, warm),
    }
    for t in range(2):
        tile = pl.ds(pl.multiple_of(t * (rows // 2) + zh * 8, 8), 8)
        for i, src in enumerate((obs, vrs)):
            fetched["map", t, i] = (src.at[:, tile, :], obv.at[pl.ds(HALO, thick), i, pl.ds(8 * t, 8)])
    copies = {
        name: pltpu.make_async_copy(src, dst, loc_sem.at[i])
        for i, (name, (src, dst)) in enumerate(fetched.items())
    }
    for c in copies.values():
        c.start()
    for name in ("loc", "flag", "strength", "load", "sigma", "spots"):
        copies[name].wait()
    loc = crd.at[0]
    occ = flag_ref[...].astype(jnp.float32)
    amp = occ * strength_ref[...]
    q = occ * load_ref[...]
    sigma = sigma_ref[...]
    iv = 1.0 / (sigma * sigma)

    four = jnp.concatenate([loc[0], loc[1], loc[2], q], axis=0)
    first = four.astype(jnp.bfloat16).astype(jnp.float32)
    rest = four - first
    second = rest.astype(jnp.bfloat16).astype(jnp.float32)
    third = rest - second
    pieces = jnp.concatenate([first, second, third, jnp.zeros_like(four)], axis=0).astype(jnp.bfloat16)
    slot_of = lax.broadcasted_iota(jnp.int32, (atoms, GHOST), 0)
    for side in range(2):
        chosen = jnp.where(slot_of == spots[side : side + 1, :], 1.0, 0.0).astype(jnp.bfloat16)
        got = jnp.dot(pieces, chosen, preferred_element_type=jnp.float32)
        got = got[0:4] + got[4:8] + got[8:12]
        for i in range(4):
            gsend[side, i] = got[i : i + 1]

    shift_y, shift_z = 32 - int(math.log2(rows)), 32 - int(math.log2(depth))
    unit_y, unit_z = 2.0**-shift_y, 2.0**-shift_z
    amps[...] = amp
    ivs[...] = iv

    def spread(d):
        amp, iv = amps[...], ivs[...]
        ivc = iv * (-0.5 * LOG2E)
        plane_at = (b * thick - HALO + lax.broadcasted_iota(jnp.int32, (16, atoms), 0)).astype(jnp.float32)
        row_in = lax.broadcasted_iota(jnp.int32, (16, atoms), 0)
        row_at = (zh * 8 + (row_in // 8) * (rows // 2) + row_in % 8) << shift_y
        dx = plane_at - crd[d, 0]
        gx = jnp.exp2(dx * dx * ivc)
        gxs[d] = gx
        gxds[d] = dx * iv * gx
        dy = (row_at - fixed(crd[d, 1], rows)).astype(jnp.float32)
        gy = jnp.exp2(dy * dy * (ivc * unit_y**2))
        gys[d] = gy
        gyds[d] = dy * (iv * unit_y) * gy
        level = lax.broadcasted_iota(jnp.int32, (depth, atoms), 0) << shift_z
        dz = (level - fixed(crd[d, 2], depth)).astype(jnp.float32)
        gz = jnp.exp2(dz * dz * (ivc * unit_z**2))
        zz[d, :, atoms:] = (dz * (iv * unit_z) * gz).astype(jnp.bfloat16)
        gzb = gz.astype(jnp.bfloat16)
        zz[d, :, :atoms] = gzb
        left = (amp * gx)[:planes, None, :] * gy[None]
        part = dot_t(left.reshape(wide, atoms).astype(jnp.bfloat16), gzb)
        if d == 0:
            acc[...] = part
        else:
            acc[...] += part

    spread(0)

    for c in range(cells):
        at = slice(c * CELL, (c + 1) * CELL)
        for i, col in enumerate((colx, coly, colz)):
            v = jnp.broadcast_to(loc[i, :, at], (CELL, CELL)).T
            col[at] = v * 2.0**shift_z if i == 0 else fixed(v, (rows, depth)[i - 1])

    scale_x = 2.0**shift_z
    for c in range(cells):
        at = slice(c * CELL, (c + 1) * CELL)
        bx[c] = loc[0, :, at] * scale_x
        by[c] = fixed(loc[1, :, at], rows)
        bz[c] = fixed(loc[2, :, at], depth)
        bq[c] = q[:, at]
    none = cells + 4
    for ref in (bx, bq, by, bz):
        ref[none] = jnp.zeros((1, CELL), ref.dtype)

    sends = []

    def remote(src, dst, ss, rsem, device):
        return pltpu.make_async_remote_copy(
            src_ref=src, dst_ref=dst, send_sem=ss, recv_sem=rsem, device_id=device, device_id_type=MESH
        )

    def post(*a):
        c = remote(*a)
        c.start()
        sends.append(c)
        return c

    pl.semaphore_wait(barrier, len(partners))
    crd_in = {}
    for d in reversed(direct):
        crd_in[d] = post(crd.at[0], crd.at[d], crd_ss.at[d], crd_rs.at[d], a_peer(d))
    gh_in = [
        post(gsend.at[0], glo, gh_ss.at[0], gh_rs.at[0], (r, up)),
        post(gsend.at[1], ghi, gh_ss.at[1], gh_rs.at[1], (r, down)),
    ]
    for t in range(2):
        for i in range(2):
            copies["map", t, i].wait()
    ob_in = [
        post(obv.at[pl.ds(thick, HALO)], obv.at[pl.ds(0, HALO)], ob_ss.at[0], ob_rs.at[0], (r, up)),
        post(
            obv.at[pl.ds(HALO, HALO)],
            obv.at[pl.ds(thick + HALO, HALO)],
            ob_ss.at[1],
            ob_rs.at[1],
            (r, down),
        ),
    ]

    def await_crd(d):
        crd_in[d].wait_recv()
        if d in relayed:
            far, to = relayed[d]
            crd_in[far] = post(crd.at[d], crd.at[far], crd_ss.at[far], crd_rs.at[far], a_peer(to))

    if na == 8:
        for ready, then in (((1, 7), (1,)), ((2,), (7, 2)), ((6,), (6,)), ((3,), (3,)), ((5,), (5,)), ((4,), (4,))):
            for d in ready:
                await_crd(d)
            for d in then:
                spread(d)
    else:
        for d in direct:
            await_crd(d)
            spread(d)

    mine[...] = acc[...].astype(jnp.bfloat16)
    lower, upper = mine.at[pl.ds(0, edge)], mine.at[pl.ds(wide - edge, edge)]
    map_in = []
    for k in (3, 2, 1, 0):
        map_in.append(post(upper, lo.at[k], lo_ss.at[k], lo_rs.at[k], (b_rep(k), up)))
        map_in.append(post(lower, hi.at[k], hi_ss.at[k], hi_rs.at[k], (b_rep(k), down)))
        if k:
            map_in.append(post(mine, rs.at[k - 1], rs_ss.at[k], rs_rs.at[k], (b_rep(k), b)))

    for c in gh_in:
        c.wait_recv()
    period_x = float(thick * bricks)
    for side, src in enumerate((glo, ghi)):
        if side == 0:
            move = jnp.where(b == 0, -period_x, 0.0)
        else:
            move = jnp.where(b == bricks - 1, period_x, 0.0)
        for g in range(2):
            at = slice(g * CELL, (g + 1) * CELL)
            n = cells + 2 * side + g
            bx[n] = (src[0, :, at] + move) * scale_x
            by[n] = fixed(src[1, :, at], rows)
            bz[n] = fixed(src[2, :, at], depth)
            bq[n] = src[3, :, at]

    part_rows = 32
    parts = CELL // part_rows

    def pair(u, _):
        c = u // parts
        at = pl.ds(pl.multiple_of(u * part_rows, part_rows), part_rows)
        xi, yi, zi = colx[at], coly[at], colz[at]
        total = [jnp.zeros((part_rows, CELL), jnp.float32)] * 3
        for s in range(slots):
            n = jnp.where(s < tally[c], lists[c, s], none)
            dx = xi - bx[n]
            dy = (yi - by[n]).astype(jnp.float32)
            dz = (zi - bz[n]).astype(jnp.float32)
            if shift_y != shift_z:
                dy = dy * 2.0 ** (shift_z - shift_y)
            inv = lax.rsqrt(dx * dx + dy * dy + dz * dz + softening * 4.0**shift_z)
            pull = inv * inv * inv * bq[n]
            total = [total[0] + pull * dx, total[1] + pull * dy, total[2] + pull * dz]
        for i in range(3):
            pacc[i, at] = total[i]
        return 0

    units = cells * parts
    copies["lists"].wait()
    copies["tally"].wait()
    lax.fori_loop(0, units // 2, pair, 0)

    for c in ob_in + map_in:
        c.wait_recv()
    wider = lambda v: v.astype(jnp.float32)
    total = acc[...] + wider(rs[0]) + wider(rs[1]) + wider(rs[2])
    low = wider(lo[0]) + wider(lo[1]) + wider(lo[2]) + wider(lo[3])
    high = wider(hi[0]) + wider(hi[1]) + wider(hi[2]) + wider(hi[3])
    total = jnp.concatenate(
        [total[:edge] + low, total[edge : wide - edge], total[wide - edge :] + high], axis=0
    ).reshape(planes, 16, depth)
    dev = total / members - obv[:, 0]
    grad = (restraint * obv[:, 1] * dev).astype(jnp.bfloat16)
    grd[...] = grad.reshape(wide, depth)
    own = dev[HALO : HALO + thick]
    own = jnp.where(x == 0, own[:, :8], own[:, 8:])
    dev_out[...] = jnp.where(zp == 0, own[:, :share], own[:, share:])

    lanes = 256

    def force(d):
        for c in range(atoms // lanes):
            at = slice(c * lanes, (c + 1) * lanes)
            after = slice(atoms + c * lanes, atoms + (c + 1) * lanes)
            along = jnp.dot(grd[...], zz[d, :, at], preferred_element_type=jnp.float32)
            slope = jnp.dot(grd[...], zz[d, :, after], preferred_element_type=jnp.float32)
            sums = [0.0, 0.0, 0.0]
            for i in range(planes):
                p = along[16 * i : 16 * i + 16]
                g = gxs[d, i : i + 1, at]
                sums[0] += gxds[d, i : i + 1, at] * p
                sums[1] += g * p
                sums[2] += g * slope[16 * i : 16 * i + 16]
            y = gys[d, :, at]
            f = (y * sums[0], gyds[d, :, at] * sums[1], y * sums[2])
            for i in range(3):
                frc[d, i, :, at] = jnp.sum(f[i], axis=0, keepdims=True)

    def fr_copy(d):
        return remote(frc.at[d], frcin.at[d], fr_ss.at[d], fr_rs.at[d], a_peer((na - d) % na))

    def give(t, _):
        d = nearest(na - 1 - t)
        force(d)

        @pl.when(t < na - 1)
        def _():
            fr_copy(d).start()

        return 0

    lax.fori_loop(0, na, give, 0)

    lax.fori_loop(units // 2, units, pair, 0)
    for name in ("vel", "mass", "warm"):
        copies[name].wait()
    mass = mass_ref[...]
    light = timestep / mass
    gain = (coupling * 4.0**shift_z) * q * light
    push = amps[...] * light
    v_half = []
    for i in range(3):
        line = [
            jnp.sum(pacc[i, c * CELL : (c + 1) * CELL].T, axis=0, keepdims=True) for c in range(cells)
        ]
        v_half.append(vel[i] + gain * jnp.concatenate(line, axis=1))

    for d in range(1, na):
        fr_copy(d).wait_recv()
    square = jnp.zeros((1, atoms), jnp.float32)
    for i in range(3):
        f = frc[0, i]
        for d in range(1, na):
            f = f + frcin[d, i]
        v_half[i] = v_half[i] - push * f
        square = square + v_half[i] * v_half[i]
    square = mass * square
    row = square[:, :CELL]
    for c in range(1, cells):
        row = row + square[:, c * CELL : (c + 1) * CELL]
    kin[0] = row
    kn_in = [
        post(kin.at[0], kin.at[d], kn_ss.at[d], kn_rs.at[d], (r, (b + d) % bricks)) for d in range(1, bricks)
    ]
    for c in kn_in:
        c.wait_recv()
    for d in range(1, bricks):
        row = row + kin[d]
    kinetic = jnp.sum(row, axis=1, keepdims=True)
    present = kinetic / (3 * atoms * bricks * boltzmann) + 1e-06
    wanted = jnp.full((1, 1), warm[0].astype(jnp.float32))
    ratio = jnp.sqrt(1.0 + heat_bath_damping * (wanted / present - 1.0))
    for i in range(3):
        v = ratio * v_half[i]
        vel_out[i] = v
        pos_out[i] = loc[i] + timestep * v
    for d in range(1, na):
        fr_copy(d).wait_send()
    for c in sends:
        c.wait_send()


def local(
    atom_locations,
    atom_speeds_vector,
    inertial_amounts,
    electric_loads,
    scatter_strengths,
    gaussian_spreads_sigma,
    atom_present_flags,
    observed_volume_values,
    voxel_reciprocal_spread,
    paired_partner_lists,
    cell_usage_tally,
    halo_sender_spots,
    target_warmth_levels,
):
    thick, rows, depth = observed_volume_values.shape
    atoms = atom_locations.shape[2]
    members, bricks = lax.axis_size("replica"), lax.axis_size("brick")
    na = members // 4
    planes = thick + 2 * HALO
    wide = planes * 16
    cells = atoms // CELL
    blocks = cells + 5
    f32, bf16, i32 = jnp.float32, jnp.bfloat16, jnp.int32
    vmem = pl.BlockSpec(memory_space=pltpu.VMEM)
    hbm = pl.BlockSpec(memory_space=pltpu.HBM)
    edge = 2 * HALO * 16
    scratch = [
        pltpu.VMEM((3, 1, atoms), f32),
        pltpu.VMEM((1, atoms), f32),
        pltpu.VMEM((1, atoms), f32),
        pltpu.VMEM((1, atoms), f32),
        pltpu.VMEM((1, atoms), f32),
        pltpu.VMEM((1, atoms), i32),
        pltpu.VMEM((2, GHOST), i32),
        pltpu.SMEM(paired_partner_lists.shape, i32),
        pltpu.SMEM((cells,), i32),
        pltpu.SMEM((1,), i32),
        pltpu.VMEM((na, 3, 1, atoms), f32),
        pltpu.VMEM((na, depth, 2 * atoms), bf16),
        pltpu.VMEM((na, 16, atoms), f32),
        pltpu.VMEM((na, 16, atoms), f32),
        pltpu.VMEM((na, 16, atoms), f32),
        pltpu.VMEM((na, 16, atoms), f32),
        pltpu.VMEM((wide, depth), f32),
        pltpu.VMEM((wide, depth), bf16),
        pltpu.VMEM((3, wide, depth), bf16),
        pltpu.VMEM((4, edge, depth), bf16),
        pltpu.VMEM((4, edge, depth), bf16),
        pltpu.VMEM((planes, 2, 16, depth), f32),
        pltpu.VMEM((1, atoms), f32),
        pltpu.VMEM((1, atoms), f32),
        pltpu.VMEM((wide, depth), bf16),
        pltpu.VMEM((na, 3, 1, atoms), f32),
        pltpu.VMEM((na, 3, 1, atoms), f32),
        pltpu.VMEM((2, 4, 1, GHOST), f32),
        pltpu.VMEM((4, 1, GHOST), f32),
        pltpu.VMEM((4, 1, GHOST), f32),
        pltpu.VMEM((blocks, 1, CELL), f32),
        pltpu.VMEM((blocks, 1, CELL), f32),
        pltpu.VMEM((blocks, 1, CELL), i32),
        pltpu.VMEM((blocks, 1, CELL), i32),
        pltpu.VMEM((atoms, CELL), f32),
        pltpu.VMEM((atoms, CELL), i32),
        pltpu.VMEM((atoms, CELL), i32),
        pltpu.VMEM((3, atoms, CELL), f32),
        pltpu.VMEM((bricks, 1, CELL), f32),
        pltpu.SemaphoreType.DMA((15,)),
    ]
    for count in (na, 2, 2, 4, 4, 4, na, bricks):
        scratch += [pltpu.SemaphoreType.DMA((count,))] * 2
    tall = lambda v: v.reshape(3, 1, atoms)
    new_positions, new_velocities, deviation = pl.pallas_call(
        functools.partial(kernel, (members, bricks, thick, rows, depth, atoms)),
        out_shape=(
            jax.ShapeDtypeStruct((3, 1, atoms), f32),
            jax.ShapeDtypeStruct((3, 1, atoms), f32),
            jax.ShapeDtypeStruct((thick, rows // members, depth), f32),
        ),
        in_specs=[hbm] * 13,
        out_specs=(vmem, vmem, vmem),
        scratch_shapes=scratch,
        compiler_params=pltpu.CompilerParams(
            collective_id=0, has_side_effects=True, vmem_limit_bytes=40 * 2**20
        ),
        cost_estimate=pl.CostEstimate(
            flops=1_200_000_000, bytes_accessed=400_000, transcendentals=4_000_000
        ),
    )(
        *(
            pltpu.with_memory_space_constraint(v, pltpu.HBM)
            for v in (
                tall(atom_locations),
                tall(atom_speeds_vector),
                inertial_amounts,
                electric_loads,
                scatter_strengths,
                gaussian_spreads_sigma,
                atom_present_flags,
                halo_sender_spots,
                paired_partner_lists,
                cell_usage_tally,
            )
        ),
        target_warmth_levels,
        pltpu.with_memory_space_constraint(observed_volume_values, pltpu.HBM),
        pltpu.with_memory_space_constraint(voxel_reciprocal_spread, pltpu.HBM),
    )
    return (
        new_positions.reshape(1, 3, atoms),
        new_velocities.reshape(1, 3, atoms),
        deviation,
    )


def solution(mesh):
    return jax.shard_map(
        local,
        mesh=mesh,
        in_specs=(
            P("replica", None, "brick"),
            P("replica", None, "brick"),
            P("brick"),
            P("brick"),
            P("brick"),
            P("brick"),
            P("brick"),
            P("brick", None, None),
            P("brick", None, None),
            P("brick", None),
            P("brick"),
            P(None, "brick"),
            P("replica"),
        ),
        out_specs=(
            P("replica", None, "brick"),
            P("replica", None, "brick"),
            P("brick", "replica", None),
        ),
        check_vma=False,
    )
```

```python
import functools
import math

import jax
import jax.numpy as jnp
from jax import lax
from jax.experimental import pallas as pl
from jax.experimental.pallas import tpu as pltpu
from jax.sharding import PartitionSpec as P

MESH = pl.DeviceIdType.MESH

HALO = 2
CELL = 128
GHOST = 256
LOG2E = 1.4426950408889634
B_STEPS = ((0, 0), (0, 1), (1, 0), (1, 1))

restraint = 0.1
coupling = 5.0
softening = 1.0
timestep = 0.5
boltzmann = 0.015
heat_bath_damping = 0.5


def fixed(coord, period):
    scale = 2.0**31 / period
    return (coord * scale).astype(jnp.int32) << 1


def dot_t(a, b):
    return lax.dot_general(a, b, (((1,), (1,)), ((), ())), preferred_element_type=jnp.float32)


def kernel(
    dims,
    loc_at,
    vel_at,
    mass_at,
    load_at,
    strength_at,
    sigma_at,
    flag_at,
    spots_at,
    lists_at,
    tally_at,
    warm_at,
    obs,
    vrs,
    pos_out,
    vel_out,
    dev_out,
    vel,
    mass_ref,
    load_ref,
    strength_ref,
    sigma_ref,
    flag_ref,
    spots,
    lists,
    tally,
    warm,
    crd,
    zz,
    gxs,
    gxds,
    gys,
    gyds,
    acc,
    mine,
    rs,
    lo,
    hi,
    obv,
    amps,
    ivs,
    grd,
    frc,
    frcin,
    gsend,
    glo,
    ghi,
    bx,
    bq,
    by,
    bz,
    colx,
    coly,
    colz,
    pacc,
    kin,
    loc_sem,
    crd_ss,
    crd_rs,
    gh_ss,
    gh_rs,
    ob_ss,
    ob_rs,
    rs_ss,
    rs_rs,
    lo_ss,
    lo_rs,
    hi_ss,
    hi_rs,
    fr_ss,
    fr_rs,
    kn_ss,
    kn_rs,
):
    members, bricks, thick, rows, depth, atoms = dims
    half = members // 2
    na = half // 2
    share = rows // members
    planes = thick + 2 * HALO
    wide = planes * 16
    edge = 2 * HALO * 16
    cells = atoms // CELL
    slots = lists.shape[1]
    r = lax.axis_index("replica")
    b = lax.axis_index("brick")
    x, z = r // half, r % half
    zh, zp = z // 2, z % 2
    up, down = (b + 1) % bricks, (b + bricks - 1) % bricks

    def a_peer(d):
        return (x * half + ((zh + d) % na) * 2 + zp, b)

    def b_rep(k):
        dx, dp = B_STEPS[k]
        return ((x + dx) % 2) * half + zh * 2 + (zp + dp) % 2

    def brick_at(n):
        y, xh, core = n // 4, n // 2 % 2, n % 2
        return (b // 4 + y) % (bricks // 4) * 4 + (b // 2 + xh) % 2 * 2 + (b + core) % 2

    def nearest(t):
        odd = t % 2
        return odd * ((t + 1) // 2) + (1 - odd) * ((na - t // 2) % na)

    direct = [nearest(t) for t in range(1, na)]
    relayed = {}
    if na == 8:
        direct = direct[:4]
        relayed = {1: (3, 2), 7: (5, 6), 2: (4, 2)}

    barrier = pltpu.get_barrier_semaphore()
    partners = [a_peer(d) for d in direct]
    partners += [(b_rep(k), n) for k in range(1, 4) for n in (b, up, down)]
    partners += [(r, brick_at(n)) for n in range(1, bricks)]
    for p in partners:
        pl.semaphore_signal(barrier, inc=1, device_id=p, device_id_type=MESH)

    fetched = {
        "loc": (loc_at, crd.at[0]),
        "flag": (flag_at, flag_ref.at[0]),
        "strength": (strength_at, strength_ref.at[0]),
        "load": (load_at, load_ref.at[0]),
        "sigma": (sigma_at, sigma_ref.at[0]),
        "spots": (spots_at, spots),
        "lists": (lists_at, lists),
        "tally": (tally_at, tally),
        "vel": (vel_at, vel),
        "mass": (mass_at, mass_ref.at[0]),
        "warm": (warm_at, warm),
    }
    for t in range(2):
        tile = pl.ds(pl.multiple_of(t * (rows // 2) + zh * 8, 8), 8)
        for i, src in enumerate((obs, vrs)):
            fetched["map", t, i] = (src.at[:, tile, :], obv.at[pl.ds(HALO, thick), i, pl.ds(8 * t, 8)])
    copies = {
        name: pltpu.make_async_copy(src, dst, loc_sem.at[i])
        for i, (name, (src, dst)) in enumerate(fetched.items())
    }
    for c in copies.values():
        c.start()
    copies["loc"].wait()
    sends = []

    def remote(src, dst, ss, rsem, device):
        return pltpu.make_async_remote_copy(
            src_ref=src, dst_ref=dst, send_sem=ss, recv_sem=rsem, device_id=device, device_id_type=MESH
        )

    def post(*a):
        c = remote(*a)
        c.start()
        sends.append(c)
        return c

    pl.semaphore_wait(barrier, len(partners))
    crd_in = {}
    for d in reversed(direct):
        crd_in[d] = post(crd.at[0], crd.at[d], crd_ss.at[d], crd_rs.at[d], a_peer(d))
    for name in ("flag", "strength", "load", "sigma", "spots"):
        copies[name].wait()
    loc = crd.at[0]
    occ = flag_ref[...].astype(jnp.float32)
    amp = occ * strength_ref[...]
    q = occ * load_ref[...]
    sigma = sigma_ref[...]
    iv = 1.0 / (sigma * sigma)

    four = jnp.concatenate([loc[0], loc[1], loc[2], q], axis=0)
    first = four.astype(jnp.bfloat16).astype(jnp.float32)
    rest = four - first
    second = rest.astype(jnp.bfloat16).astype(jnp.float32)
    third = rest - second
    pieces = jnp.concatenate([first, second, third, jnp.zeros_like(four)], axis=0).astype(jnp.bfloat16)
    slot_of = lax.broadcasted_iota(jnp.int32, (atoms, GHOST), 0)
    for side in range(2):
        chosen = jnp.where(slot_of == spots[side : side + 1, :], 1.0, 0.0).astype(jnp.bfloat16)
        got = jnp.dot(pieces, chosen, preferred_element_type=jnp.float32)
        got = got[0:4] + got[4:8] + got[8:12]
        for i in range(4):
            gsend[side, i] = got[i : i + 1]

    shift_y, shift_z = 32 - int(math.log2(rows)), 32 - int(math.log2(depth))
    unit_y, unit_z = 2.0**-shift_y, 2.0**-shift_z
    amps[...] = amp
    ivs[...] = iv

    def spread(d):
        amp, iv = amps[...], ivs[...]
        ivc = iv * (-0.5 * LOG2E)
        plane_at = (b * thick - HALO + lax.broadcasted_iota(jnp.int32, (16, atoms), 0)).astype(jnp.float32)
        row_in = lax.broadcasted_iota(jnp.int32, (16, atoms), 0)
        row_at = (zh * 8 + (row_in // 8) * (rows // 2) + row_in % 8) << shift_y
        dx = plane_at - crd[d, 0]
        gx = jnp.exp2(dx * dx * ivc)
        gxs[d] = gx
        gxds[d] = dx * iv * gx
        dy = (row_at - fixed(crd[d, 1], rows)).astype(jnp.float32)
        gy = jnp.exp2(dy * dy * (ivc * unit_y**2))
        gys[d] = gy
        gyds[d] = dy * (iv * unit_y) * gy
        level = lax.broadcasted_iota(jnp.int32, (depth, atoms), 0) << shift_z
        dz = (level - fixed(crd[d, 2], depth)).astype(jnp.float32)
        gz = jnp.exp2(dz * dz * (ivc * unit_z**2))
        zz[d, :, atoms:] = (dz * (iv * unit_z) * gz).astype(jnp.bfloat16)
        gzb = gz.astype(jnp.bfloat16)
        zz[d, :, :atoms] = gzb
        left = (amp * gx)[:planes, None, :] * gy[None]
        part = dot_t(left.reshape(wide, atoms).astype(jnp.bfloat16), gzb)
        if d == 0:
            acc[...] = part
        else:
            acc[...] += part

    spread(0)

    for c in range(cells):
        at = slice(c * CELL, (c + 1) * CELL)
        for i, col in enumerate((colx, coly, colz)):
            v = jnp.broadcast_to(loc[i, :, at], (CELL, CELL)).T
            col[at] = v * 2.0**shift_z if i == 0 else fixed(v, (rows, depth)[i - 1])

    scale_x = 2.0**shift_z
    for c in range(cells):
        at = slice(c * CELL, (c + 1) * CELL)
        bx[c] = loc[0, :, at] * scale_x
        by[c] = fixed(loc[1, :, at], rows)
        bz[c] = fixed(loc[2, :, at], depth)
        bq[c] = q[:, at]
    none = cells + 4
    for ref in (bx, bq, by, bz):
        ref[none] = jnp.zeros((1, CELL), ref.dtype)

    gh_in = [
        post(gsend.at[0], glo, gh_ss.at[0], gh_rs.at[0], (r, up)),
        post(gsend.at[1], ghi, gh_ss.at[1], gh_rs.at[1], (r, down)),
    ]
    for t in range(2):
        for i in range(2):
            copies["map", t, i].wait()
    ob_in = [
        post(obv.at[pl.ds(thick, HALO)], obv.at[pl.ds(0, HALO)], ob_ss.at[0], ob_rs.at[0], (r, up)),
        post(
            obv.at[pl.ds(HALO, HALO)],
            obv.at[pl.ds(thick + HALO, HALO)],
            ob_ss.at[1],
            ob_rs.at[1],
            (r, down),
        ),
    ]

    def await_crd(d):
        crd_in[d].wait_recv()
        if d in relayed:
            far, to = relayed[d]
            crd_in[far] = post(crd.at[d], crd.at[far], crd_ss.at[far], crd_rs.at[far], a_peer(to))

    if na == 8:
        for ready, then in (((1, 7), (1,)), ((2,), (7, 2)), ((6,), (6,)), ((3,), (3,)), ((5,), (5,)), ((4,), (4,))):
            for d in ready:
                await_crd(d)
            for d in then:
                spread(d)
    else:
        for d in direct:
            await_crd(d)
            spread(d)

    mine[...] = acc[...].astype(jnp.bfloat16)
    lower, upper = mine.at[pl.ds(0, edge)], mine.at[pl.ds(wide - edge, edge)]
    map_in = []
    for k in (1, 3, 0, 2):
        map_in.append(post(upper, lo.at[k], lo_ss.at[k], lo_rs.at[k], (b_rep(k), up)))
        map_in.append(post(lower, hi.at[k], hi_ss.at[k], hi_rs.at[k], (b_rep(k), down)))
    for k in (3, 1, 2):
        map_in.append(post(mine, rs.at[k - 1], rs_ss.at[k], rs_rs.at[k], (b_rep(k), b)))

    for c in gh_in:
        c.wait_recv()
    period_x = float(thick * bricks)
    for side, src in enumerate((glo, ghi)):
        if side == 0:
            move = jnp.where(b == 0, -period_x, 0.0)
        else:
            move = jnp.where(b == bricks - 1, period_x, 0.0)
        for g in range(2):
            at = slice(g * CELL, (g + 1) * CELL)
            n = cells + 2 * side + g
            bx[n] = (src[0, :, at] + move) * scale_x
            by[n] = fixed(src[1, :, at], rows)
            bz[n] = fixed(src[2, :, at], depth)
            bq[n] = src[3, :, at]

    part_rows = 32
    parts = CELL // part_rows

    def pair(u, _):
        c = u // parts
        at = pl.ds(pl.multiple_of(u * part_rows, part_rows), part_rows)
        xi, yi, zi = colx[at], coly[at], colz[at]
        total = [jnp.zeros((part_rows, CELL), jnp.float32)] * 3
        for s in range(slots):
            n = jnp.where(s < tally[c], lists[c, s], none)
            dx = xi - bx[n]
            dy = (yi - by[n]).astype(jnp.float32)
            dz = (zi - bz[n]).astype(jnp.float32)
            if shift_y != shift_z:
                dy = dy * 2.0 ** (shift_z - shift_y)
            inv = lax.rsqrt(dx * dx + dy * dy + dz * dz + softening * 4.0**shift_z)
            pull = inv * inv * inv * bq[n]
            total = [total[0] + pull * dx, total[1] + pull * dy, total[2] + pull * dz]
        for i in range(3):
            pacc[i, at] = total[i]
        return 0

    units = cells * parts
    copies["lists"].wait()
    copies["tally"].wait()
    lax.fori_loop(0, units // 2, pair, 0)

    for c in ob_in + map_in:
        c.wait_recv()
    wider = lambda v: v.astype(jnp.float32)
    total = acc[...] + wider(rs[0]) + wider(rs[1]) + wider(rs[2])
    low = wider(lo[0]) + wider(lo[1]) + wider(lo[2]) + wider(lo[3])
    high = wider(hi[0]) + wider(hi[1]) + wider(hi[2]) + wider(hi[3])
    total = jnp.concatenate(
        [total[:edge] + low, total[edge : wide - edge], total[wide - edge :] + high], axis=0
    ).reshape(planes, 16, depth)
    dev = total / members - obv[:, 0]
    grad = (restraint * obv[:, 1] * dev).astype(jnp.bfloat16)
    grd[...] = grad.reshape(wide, depth)
    own = dev[HALO : HALO + thick]
    own = jnp.where(x == 0, own[:, :8], own[:, 8:])
    dev_out[...] = jnp.where(zp == 0, own[:, :share], own[:, share:])

    lanes = 256

    def force(d):
        for c in range(atoms // lanes):
            at = slice(c * lanes, (c + 1) * lanes)
            after = slice(atoms + c * lanes, atoms + (c + 1) * lanes)
            along = jnp.dot(grd[...], zz[d, :, at], preferred_element_type=jnp.float32)
            slope = jnp.dot(grd[...], zz[d, :, after], preferred_element_type=jnp.float32)
            sums = [0.0, 0.0, 0.0]
            for i in range(planes):
                p = along[16 * i : 16 * i + 16]
                g = gxs[d, i : i + 1, at]
                sums[0] += gxds[d, i : i + 1, at] * p
                sums[1] += g * p
                sums[2] += g * slope[16 * i : 16 * i + 16]
            y = gys[d, :, at]
            f = (y * sums[0], gyds[d, :, at] * sums[1], y * sums[2])
            for i in range(3):
                frc[d, i, :, at] = jnp.sum(f[i], axis=0, keepdims=True)

    def fr_copy(d):
        return remote(frc.at[d], frcin.at[d], fr_ss.at[d], fr_rs.at[d], a_peer((na - d) % na))

    def give(t, _):
        d = nearest(na - 1 - t)
        force(d)

        @pl.when(t < na - 1)
        def _():
            fr_copy(d).start()

        return 0

    lax.fori_loop(0, na, give, 0)

    lax.fori_loop(units // 2, units, pair, 0)
    for name in ("vel", "mass", "warm"):
        copies[name].wait()
    mass = mass_ref[...]
    light = timestep / mass
    gain = (coupling * 4.0**shift_z) * q * light
    push = amps[...] * light
    v_half = []
    for i in range(3):
        line = [
            jnp.sum(pacc[i, c * CELL : (c + 1) * CELL].T, axis=0, keepdims=True) for c in range(cells)
        ]
        v_half.append(vel[i] + gain * jnp.concatenate(line, axis=1))

    for d in range(1, na):
        fr_copy(d).wait_recv()
    square = jnp.zeros((1, atoms), jnp.float32)
    for i in range(3):
        f = frc[0, i]
        for d in range(1, na):
            f = f + frcin[d, i]
        v_half[i] = v_half[i] - push * f
        square = square + v_half[i] * v_half[i]
    square = mass * square
    row = square[:, :CELL]
    for c in range(1, cells):
        row = row + square[:, c * CELL : (c + 1) * CELL]
    kin[0] = row
    kn_in = [
        post(kin.at[0], kin.at[n], kn_ss.at[n], kn_rs.at[n], (r, brick_at(n)))
        for n in sorted(range(1, bricks), key=lambda n: -(min(n // 4, 4 - n // 4) + n // 2 % 2 * 2 + n % 2))
    ]
    for c in kn_in:
        c.wait_recv()
    for d in range(1, bricks):
        row = row + kin[d]
    kinetic = jnp.sum(row, axis=1, keepdims=True)
    present = kinetic / (3 * atoms * bricks * boltzmann) + 1e-06
    wanted = jnp.full((1, 1), warm[0].astype(jnp.float32))
    ratio = jnp.sqrt(1.0 + heat_bath_damping * (wanted / present - 1.0))
    for i in range(3):
        v = ratio * v_half[i]
        vel_out[i] = v
        pos_out[i] = loc[i] + timestep * v
    for d in range(1, na):
        fr_copy(d).wait_send()
    for c in sends:
        c.wait_send()


def write(count, *refs):
    sources, targets, sem = refs[:count], refs[count:-1], refs[-1]
    copies = [pltpu.make_async_copy(a, c, sem.at[i]) for i, (a, c) in enumerate(zip(sources, targets))]
    for c in copies:
        c.start()
    for c in copies:
        c.wait()


def local(
    atom_locations,
    atom_speeds_vector,
    inertial_amounts,
    electric_loads,
    scatter_strengths,
    gaussian_spreads_sigma,
    atom_present_flags,
    observed_volume_values,
    voxel_reciprocal_spread,
    paired_partner_lists,
    cell_usage_tally,
    halo_sender_spots,
    target_warmth_levels,
):
    thick, rows, depth = observed_volume_values.shape
    atoms = atom_locations.shape[2]
    members, bricks = lax.axis_size("replica"), lax.axis_size("brick")
    na = members // 4
    planes = thick + 2 * HALO
    wide = planes * 16
    cells = atoms // CELL
    blocks = cells + 5
    f32, bf16, i32 = jnp.float32, jnp.bfloat16, jnp.int32
    vmem = pl.BlockSpec(memory_space=pltpu.VMEM)
    hbm = pl.BlockSpec(memory_space=pltpu.HBM)
    edge = 2 * HALO * 16
    scratch = [
        pltpu.VMEM((3, 1, atoms), f32),
        pltpu.VMEM((1, atoms), f32),
        pltpu.VMEM((1, atoms), f32),
        pltpu.VMEM((1, atoms), f32),
        pltpu.VMEM((1, atoms), f32),
        pltpu.VMEM((1, atoms), i32),
        pltpu.VMEM((2, GHOST), i32),
        pltpu.SMEM(paired_partner_lists.shape, i32),
        pltpu.SMEM((cells,), i32),
        pltpu.SMEM((1,), i32),
        pltpu.VMEM((na, 3, 1, atoms), f32),
        pltpu.VMEM((na, depth, 2 * atoms), bf16),
        pltpu.VMEM((na, 16, atoms), f32),
        pltpu.VMEM((na, 16, atoms), f32),
        pltpu.VMEM((na, 16, atoms), f32),
        pltpu.VMEM((na, 16, atoms), f32),
        pltpu.VMEM((wide, depth), f32),
        pltpu.VMEM((wide, depth), bf16),
        pltpu.VMEM((3, wide, depth), bf16),
        pltpu.VMEM((4, edge, depth), bf16),
        pltpu.VMEM((4, edge, depth), bf16),
        pltpu.VMEM((planes, 2, 16, depth), f32),
        pltpu.VMEM((1, atoms), f32),
        pltpu.VMEM((1, atoms), f32),
        pltpu.VMEM((wide, depth), bf16),
        pltpu.VMEM((na, 3, 1, atoms), f32),
        pltpu.VMEM((na, 3, 1, atoms), f32),
        pltpu.VMEM((2, 4, 1, GHOST), f32),
        pltpu.VMEM((4, 1, GHOST), f32),
        pltpu.VMEM((4, 1, GHOST), f32),
        pltpu.VMEM((blocks, 1, CELL), f32),
        pltpu.VMEM((blocks, 1, CELL), f32),
        pltpu.VMEM((blocks, 1, CELL), i32),
        pltpu.VMEM((blocks, 1, CELL), i32),
        pltpu.VMEM((atoms, CELL), f32),
        pltpu.VMEM((atoms, CELL), i32),
        pltpu.VMEM((atoms, CELL), i32),
        pltpu.VMEM((3, atoms, CELL), f32),
        pltpu.VMEM((bricks, 1, CELL), f32),
        pltpu.SemaphoreType.DMA((15,)),
    ]
    for count in (na, 2, 2, 4, 4, 4, na, bricks):
        scratch += [pltpu.SemaphoreType.DMA((count,))] * 2
    tall = lambda v: v.reshape(3, 1, atoms)
    new_positions, new_velocities, deviation = pl.pallas_call(
        functools.partial(kernel, (members, bricks, thick, rows, depth, atoms)),
        out_shape=(
            jax.ShapeDtypeStruct((3, 1, atoms), f32),
            jax.ShapeDtypeStruct((3, 1, atoms), f32),
            jax.ShapeDtypeStruct((thick, rows // members, depth), f32),
        ),
        in_specs=[hbm] * 13,
        out_specs=(vmem, vmem, vmem),
        scratch_shapes=scratch,
        compiler_params=pltpu.CompilerParams(
            collective_id=0, has_side_effects=True, vmem_limit_bytes=40 * 2**20
        ),
        cost_estimate=pl.CostEstimate(
            flops=1_200_000_000, bytes_accessed=400_000, transcendentals=4_000_000
        ),
    )(
        *(
            pltpu.with_memory_space_constraint(v, pltpu.HBM)
            for v in (
                tall(atom_locations),
                tall(atom_speeds_vector),
                inertial_amounts,
                electric_loads,
                scatter_strengths,
                gaussian_spreads_sigma,
                atom_present_flags,
                halo_sender_spots,
                paired_partner_lists,
                cell_usage_tally,
            )
        ),
        target_warmth_levels,
        pltpu.with_memory_space_constraint(observed_volume_values, pltpu.HBM),
        pltpu.with_memory_space_constraint(voxel_reciprocal_spread, pltpu.HBM),
    )
    made = (new_positions, new_velocities, deviation)
    new_positions, new_velocities, deviation = pl.pallas_call(
        functools.partial(write, len(made)),
        out_shape=tuple(jax.ShapeDtypeStruct(v.shape, v.dtype) for v in made),
        in_specs=[vmem] * len(made),
        out_specs=tuple(hbm for _ in made),
        scratch_shapes=[pltpu.SemaphoreType.DMA((len(made),))],
    )(*(pltpu.with_memory_space_constraint(v, pltpu.VMEM) for v in made))
    return (
        new_positions.reshape(1, 3, atoms),
        new_velocities.reshape(1, 3, atoms),
        deviation,
    )


def solution(mesh):
    return jax.shard_map(
        local,
        mesh=mesh,
        in_specs=(
            P("replica", None, "brick"),
            P("replica", None, "brick"),
            P("brick"),
            P("brick"),
            P("brick"),
            P("brick"),
            P("brick"),
            P("brick", None, None),
            P("brick", None, None),
            P("brick", None),
            P("brick"),
            P(None, "brick"),
            P("replica"),
        ),
        out_specs=(
            P("replica", None, "brick"),
            P("replica", None, "brick"),
            P("brick", "replica", None),
        ),
        check_vma=False,
    )
```

```python
import functools
import math

import jax
import jax.numpy as jnp
from jax import lax
from jax.experimental import pallas as pl
from jax.experimental.pallas import tpu as pltpu
from jax.sharding import PartitionSpec as P

MESH = pl.DeviceIdType.MESH

HALO = 2
CELL = 128
GHOST = 256
LOG2E = 1.4426950408889634
B_STEPS = ((0, 0), (0, 1), (1, 0), (1, 1))

restraint = 0.1
coupling = 5.0
softening = 1.0
timestep = 0.5
boltzmann = 0.015
heat_bath_damping = 0.5


def fixed(coord, period):
    scale = 2.0**31 / period
    return (coord * scale).astype(jnp.int32) << 1


def dot_t(a, b):
    return lax.dot_general(a, b, (((1,), (1,)), ((), ())), preferred_element_type=jnp.float32)


def kernel(
    dims,
    loc_at,
    vel_at,
    mass_at,
    load_at,
    strength_at,
    sigma_at,
    flag_at,
    spots_at,
    lists_at,
    tally_at,
    warm,
    obs,
    vrs,
    pos_out,
    vel_out,
    dev_out,
    vel,
    mass_ref,
    load_ref,
    strength_ref,
    sigma_ref,
    flag_ref,
    spots,
    lists,
    tally,
    crd,
    zz,
    gxs,
    gxds,
    gys,
    gyds,
    acc,
    mine,
    rs,
    lo,
    hi,
    obv,
    amps,
    ivs,
    grd,
    frc,
    frcin,
    gsend,
    glo,
    ghi,
    bx,
    bq,
    by,
    bz,
    colx,
    coly,
    colz,
    pacc,
    kin,
    loc_sem,
    crd_ss,
    crd_rs,
    gh_ss,
    gh_rs,
    ob_ss,
    ob_rs,
    rs_ss,
    rs_rs,
    lo_ss,
    lo_rs,
    hi_ss,
    hi_rs,
    fr_ss,
    fr_rs,
    kn_ss,
    kn_rs,
):
    members, bricks, thick, rows, depth, atoms = dims
    half = members // 2
    na = half // 2
    share = rows // members
    planes = thick + 2 * HALO
    wide = planes * 16
    edge = 2 * HALO * 16
    cells = atoms // CELL
    slots = lists.shape[1]
    r = lax.axis_index("replica")
    b = lax.axis_index("brick")
    x, z = r // half, r % half
    zh, zp = z // 2, z % 2
    up, down = (b + 1) % bricks, (b + bricks - 1) % bricks

    def a_peer(d):
        return (x * half + ((zh + d) % na) * 2 + zp, b)

    def b_rep(k):
        dx, dp = B_STEPS[k]
        return ((x + dx) % 2) * half + zh * 2 + (zp + dp) % 2

    def brick_at(n):
        y, xh, core = n // 4, n // 2 % 2, n % 2
        return (b // 4 + y) % (bricks // 4) * 4 + (b // 2 + xh) % 2 * 2 + (b + core) % 2

    far_first = sorted(
        range(1, bricks), key=lambda n: -(min(n // 4, 4 - n // 4) + n // 2 % 2 * 2 + n % 2)
    )

    def nearest(t):
        odd = t % 2
        return odd * ((t + 1) // 2) + (1 - odd) * ((na - t // 2) % na)

    direct = [nearest(t) for t in range(1, na)]
    relayed = {}
    if na == 8:
        direct = direct[:4]
        relayed = {1: (3, 2), 7: (5, 6), 2: (4, 2)}

    barrier = pltpu.get_barrier_semaphore()
    partners = [a_peer(d) for d in reversed(direct)]
    partners += [(r, brick_at(n)) for n in far_first]
    partners += [(b_rep(k), n) for n in (up, down, b) for k in range(1, 4)]
    for p in partners:
        pl.semaphore_signal(barrier, inc=1, device_id=p, device_id_type=MESH)

    fetched = {
        "loc": (loc_at, crd.at[0]),
        "flag": (flag_at, flag_ref.at[0]),
        "strength": (strength_at, strength_ref.at[0]),
        "load": (load_at, load_ref.at[0]),
        "sigma": (sigma_at, sigma_ref.at[0]),
        "spots": (spots_at, spots),
        "lists": (lists_at, lists),
        "tally": (tally_at, tally),
        "vel": (vel_at, vel),
        "mass": (mass_at, mass_ref.at[0]),
    }
    for t in range(2):
        tile = pl.ds(pl.multiple_of(t * (rows // 2) + zh * 8, 8), 8)
        for i, src in enumerate((obs, vrs)):
            fetched["map", t, i] = (src.at[:, tile, :], obv.at[pl.ds(HALO, thick), i, pl.ds(8 * t, 8)])
    copies = {
        name: pltpu.make_async_copy(src, dst, loc_sem.at[i])
        for i, (name, (src, dst)) in enumerate(fetched.items())
    }
    for c in copies.values():
        c.start()
    copies["loc"].wait()
    sends = []

    def remote(src, dst, ss, rsem, device):
        return pltpu.make_async_remote_copy(
            src_ref=src, dst_ref=dst, send_sem=ss, recv_sem=rsem, device_id=device, device_id_type=MESH
        )

    def post(*a):
        c = remote(*a)
        c.start()
        sends.append(c)
        return c

    for name in ("flag", "strength", "load", "sigma", "spots"):
        copies[name].wait()
    loc = crd.at[0]
    occ = flag_ref[...].astype(jnp.float32)
    amp = occ * strength_ref[...]
    q = occ * load_ref[...]
    sigma = sigma_ref[...]
    iv = 1.0 / (sigma * sigma)

    four = jnp.concatenate([loc[0], loc[1], loc[2], q], axis=0)
    first = four.astype(jnp.bfloat16).astype(jnp.float32)
    rest = four - first
    second = rest.astype(jnp.bfloat16).astype(jnp.float32)
    third = rest - second
    pieces = jnp.concatenate([first, second, third, jnp.zeros_like(four)], axis=0).astype(jnp.bfloat16)
    slot_of = lax.broadcasted_iota(jnp.int32, (atoms, GHOST), 0)
    for side in range(2):
        chosen = jnp.where(slot_of == spots[side : side + 1, :], 1.0, 0.0).astype(jnp.bfloat16)
        got = jnp.dot(pieces, chosen, preferred_element_type=jnp.float32)
        got = got[0:4] + got[4:8] + got[8:12]
        for i in range(4):
            gsend[side, i] = got[i : i + 1]

    shift_y, shift_z = 32 - int(math.log2(rows)), 32 - int(math.log2(depth))
    unit_y, unit_z = 2.0**-shift_y, 2.0**-shift_z
    amps[...] = amp
    ivs[...] = iv

    def spread(d):
        amp, iv = amps[...], ivs[...]
        ivc = iv * (-0.5 * LOG2E)
        plane_at = (b * thick - HALO + lax.broadcasted_iota(jnp.int32, (16, atoms), 0)).astype(jnp.float32)
        row_in = lax.broadcasted_iota(jnp.int32, (16, atoms), 0)
        row_at = (zh * 8 + (row_in // 8) * (rows // 2) + row_in % 8) << shift_y
        dx = plane_at - crd[d, 0]
        gx = jnp.exp2(dx * dx * ivc)
        gxs[d] = gx
        gxds[d] = dx * iv * gx
        dy = (row_at - fixed(crd[d, 1], rows)).astype(jnp.float32)
        gy = jnp.exp2(dy * dy * (ivc * unit_y**2))
        gys[d] = gy
        gyds[d] = dy * (iv * unit_y) * gy
        level = lax.broadcasted_iota(jnp.int32, (depth, atoms), 0) << shift_z
        dz = (level - fixed(crd[d, 2], depth)).astype(jnp.float32)
        gz = jnp.exp2(dz * dz * (ivc * unit_z**2))
        zz[d, :, atoms:] = (dz * (iv * unit_z) * gz).astype(jnp.bfloat16)
        gzb = gz.astype(jnp.bfloat16)
        zz[d, :, :atoms] = gzb
        left = (amp * gx)[:planes, None, :] * gy[None]
        part = dot_t(left.reshape(wide, atoms).astype(jnp.bfloat16), gzb)
        if d == 0:
            acc[...] = part
        else:
            acc[...] += part

    spread(0)

    pl.semaphore_wait(barrier, len(partners))
    crd_in = {}
    for d in reversed(direct):
        crd_in[d] = post(crd.at[0], crd.at[d], crd_ss.at[d], crd_rs.at[d], a_peer(d))
    gh_in = [
        post(gsend.at[0], glo, gh_ss.at[0], gh_rs.at[0], (r, up)),
        post(gsend.at[1], ghi, gh_ss.at[1], gh_rs.at[1], (r, down)),
    ]
    for t in range(2):
        for i in range(2):
            copies["map", t, i].wait()
    ob_in = [
        post(obv.at[pl.ds(thick, HALO)], obv.at[pl.ds(0, HALO)], ob_ss.at[0], ob_rs.at[0], (r, up)),
        post(
            obv.at[pl.ds(HALO, HALO)],
            obv.at[pl.ds(thick + HALO, HALO)],
            ob_ss.at[1],
            ob_rs.at[1],
            (r, down),
        ),
    ]


    for c in range(cells):
        at = slice(c * CELL, (c + 1) * CELL)
        for i, col in enumerate((colx, coly, colz)):
            v = jnp.broadcast_to(loc[i, :, at], (CELL, CELL)).T
            col[at] = v * 2.0**shift_z if i == 0 else fixed(v, (rows, depth)[i - 1])

    scale_x = 2.0**shift_z
    for c in range(cells):
        at = slice(c * CELL, (c + 1) * CELL)
        bx[c] = loc[0, :, at] * scale_x
        by[c] = fixed(loc[1, :, at], rows)
        bz[c] = fixed(loc[2, :, at], depth)
        bq[c] = q[:, at]
    none = cells + 4
    for ref in (bx, bq, by, bz):
        ref[none] = jnp.zeros((1, CELL), ref.dtype)

    def await_crd(d):
        crd_in[d].wait_recv()
        if d in relayed:
            far, to = relayed[d]
            crd_in[far] = post(crd.at[d], crd.at[far], crd_ss.at[far], crd_rs.at[far], a_peer(to))

    if na == 8:
        for ready, then in (((1, 7, 2), (1, 7, 2)), ((6,), (6,)), ((3,), (3,)), ((5,), (5,)), ((4,), (4,))):
            for d in ready:
                await_crd(d)
            for d in then:
                spread(d)
    else:
        for d in direct:
            await_crd(d)
            spread(d)

    mine[...] = acc[...].astype(jnp.bfloat16)
    lower, upper = mine.at[pl.ds(0, edge)], mine.at[pl.ds(wide - edge, edge)]
    map_in = []
    for k in (1, 3, 0, 2):
        map_in.append(post(upper, lo.at[k], lo_ss.at[k], lo_rs.at[k], (b_rep(k), up)))
        map_in.append(post(lower, hi.at[k], hi_ss.at[k], hi_rs.at[k], (b_rep(k), down)))
    for k in (3, 1, 2):
        map_in.append(post(mine, rs.at[k - 1], rs_ss.at[k], rs_rs.at[k], (b_rep(k), b)))

    for c in gh_in:
        c.wait_recv()
    period_x = float(thick * bricks)
    for side, src in enumerate((glo, ghi)):
        if side == 0:
            move = jnp.where(b == 0, -period_x, 0.0)
        else:
            move = jnp.where(b == bricks - 1, period_x, 0.0)
        for g in range(2):
            at = slice(g * CELL, (g + 1) * CELL)
            n = cells + 2 * side + g
            bx[n] = (src[0, :, at] + move) * scale_x
            by[n] = fixed(src[1, :, at], rows)
            bz[n] = fixed(src[2, :, at], depth)
            bq[n] = src[3, :, at]

    part_rows = 32
    parts = CELL // part_rows

    def pair(u, _):
        c = u // parts
        at = pl.ds(pl.multiple_of(u * part_rows, part_rows), part_rows)
        xi, yi, zi = colx[at], coly[at], colz[at]
        total = [jnp.zeros((part_rows, CELL), jnp.float32)] * 3
        for s in range(slots):
            n = jnp.where(s < tally[c], lists[c, s], none)
            dx = xi - bx[n]
            dy = (yi - by[n]).astype(jnp.float32)
            dz = (zi - bz[n]).astype(jnp.float32)
            if shift_y != shift_z:
                dy = dy * 2.0 ** (shift_z - shift_y)
            inv = lax.rsqrt(dx * dx + dy * dy + dz * dz + softening * 4.0**shift_z)
            pull = inv * inv * inv * bq[n]
            total = [total[0] + pull * dx, total[1] + pull * dy, total[2] + pull * dz]
        for i in range(3):
            pacc[i, at] = total[i]
        return 0

    units = cells * parts
    copies["lists"].wait()
    copies["tally"].wait()
    lax.fori_loop(0, units // 2, pair, 0)

    for c in ob_in + map_in:
        c.wait_recv()
    wider = lambda v: v.astype(jnp.float32)
    total = acc[...] + wider(rs[0]) + wider(rs[1]) + wider(rs[2])
    low = wider(lo[0]) + wider(lo[1]) + wider(lo[2]) + wider(lo[3])
    high = wider(hi[0]) + wider(hi[1]) + wider(hi[2]) + wider(hi[3])
    total = jnp.concatenate(
        [total[:edge] + low, total[edge : wide - edge], total[wide - edge :] + high], axis=0
    ).reshape(planes, 16, depth)
    dev = total / members - obv[:, 0]
    grad = (restraint * obv[:, 1] * dev).astype(jnp.bfloat16)
    grd[...] = grad.reshape(wide, depth)
    own = dev[HALO : HALO + thick]
    own = jnp.where(x == 0, own[:, :8], own[:, 8:])
    dev_out[...] = jnp.where(zp == 0, own[:, :share], own[:, share:])

    lanes = 256

    def force(d):
        for c in range(atoms // lanes):
            at = slice(c * lanes, (c + 1) * lanes)
            after = slice(atoms + c * lanes, atoms + (c + 1) * lanes)
            along = jnp.dot(grd[...], zz[d, :, at], preferred_element_type=jnp.float32)
            slope = jnp.dot(grd[...], zz[d, :, after], preferred_element_type=jnp.float32)
            sums = [0.0, 0.0, 0.0]
            for i in range(planes):
                p = along[16 * i : 16 * i + 16]
                g = gxs[d, i : i + 1, at]
                sums[0] += gxds[d, i : i + 1, at] * p
                sums[1] += g * p
                sums[2] += g * slope[16 * i : 16 * i + 16]
            y = gys[d, :, at]
            f = (y * sums[0], gyds[d, :, at] * sums[1], y * sums[2])
            for i in range(3):
                frc[d, i, :, at] = jnp.sum(f[i], axis=0, keepdims=True)

    def fr_copy(d):
        return remote(frc.at[d], frcin.at[d], fr_ss.at[d], fr_rs.at[d], a_peer((na - d) % na))

    def give(t, _):
        d = nearest(na - 1 - t)
        force(d)

        @pl.when(t < na - 1)
        def _():
            fr_copy(d).start()

        return 0

    lax.fori_loop(0, na, give, 0)

    lax.fori_loop(units // 2, units, pair, 0)
    for name in ("vel", "mass"):
        copies[name].wait()
    mass = mass_ref[...]
    light = timestep / mass
    gain = (coupling * 4.0**shift_z) * q * light
    push = amps[...] * light
    v_half = []
    for i in range(3):
        line = [
            jnp.sum(pacc[i, c * CELL : (c + 1) * CELL].T, axis=0, keepdims=True) for c in range(cells)
        ]
        v_half.append(vel[i] + gain * jnp.concatenate(line, axis=1))

    for d in range(1, na):
        fr_copy(d).wait_recv()
    square = jnp.zeros((1, atoms), jnp.float32)
    for i in range(3):
        f = frc[0, i]
        for d in range(1, na):
            f = f + frcin[d, i]
        v_half[i] = v_half[i] - push * f
        square = square + v_half[i] * v_half[i]
    square = mass * square
    row = square[:, :CELL]
    for c in range(1, cells):
        row = row + square[:, c * CELL : (c + 1) * CELL]
    kin[0] = row
    kn_in = [
        post(kin.at[0], kin.at[n], kn_ss.at[n], kn_rs.at[n], (r, brick_at(n)))
        for n in far_first
    ]
    for c in kn_in:
        c.wait_recv()
    for d in range(1, bricks):
        row = row + kin[d]
    kinetic = jnp.sum(row, axis=1, keepdims=True)
    present = kinetic / (3 * atoms * bricks * boltzmann) + 1e-06
    wanted = jnp.full((1, 1), warm[0, 0].astype(jnp.float32))
    ratio = jnp.sqrt(1.0 + heat_bath_damping * (wanted / present - 1.0))
    for i in range(3):
        v = ratio * v_half[i]
        vel_out[i] = v
        pos_out[i] = loc[i] + timestep * v
    for d in range(1, na):
        fr_copy(d).wait_send()
    for c in sends:
        c.wait_send()


def write(count, *refs):
    sources, targets, sem = refs[:count], refs[count:-1], refs[-1]
    copies = [pltpu.make_async_copy(a, c, sem.at[i]) for i, (a, c) in enumerate(zip(sources, targets))]
    for c in copies:
        c.start()
    for c in copies:
        c.wait()


def local(
    atom_locations,
    atom_speeds_vector,
    inertial_amounts,
    electric_loads,
    scatter_strengths,
    gaussian_spreads_sigma,
    atom_present_flags,
    observed_volume_values,
    voxel_reciprocal_spread,
    paired_partner_lists,
    cell_usage_tally,
    halo_sender_spots,
    target_warmth_levels,
):
    thick, rows, depth = observed_volume_values.shape
    atoms = atom_locations.shape[2]
    members, bricks = lax.axis_size("replica"), lax.axis_size("brick")
    na = members // 4
    planes = thick + 2 * HALO
    wide = planes * 16
    cells = atoms // CELL
    blocks = cells + 5
    f32, bf16, i32 = jnp.float32, jnp.bfloat16, jnp.int32
    vmem = pl.BlockSpec(memory_space=pltpu.VMEM)
    hbm = pl.BlockSpec(memory_space=pltpu.HBM)
    smem = pl.BlockSpec(memory_space=pltpu.SMEM)
    edge = 2 * HALO * 16
    scratch = [
        pltpu.VMEM((3, 1, atoms), f32),
        pltpu.VMEM((1, atoms), f32),
        pltpu.VMEM((1, atoms), f32),
        pltpu.VMEM((1, atoms), f32),
        pltpu.VMEM((1, atoms), f32),
        pltpu.VMEM((1, atoms), i32),
        pltpu.VMEM((2, GHOST), i32),
        pltpu.SMEM(paired_partner_lists.shape, i32),
        pltpu.SMEM((cells,), i32),
        pltpu.VMEM((na, 3, 1, atoms), f32),
        pltpu.VMEM((na, depth, 2 * atoms), bf16),
        pltpu.VMEM((na, 16, atoms), f32),
        pltpu.VMEM((na, 16, atoms), f32),
        pltpu.VMEM((na, 16, atoms), f32),
        pltpu.VMEM((na, 16, atoms), f32),
        pltpu.VMEM((wide, depth), f32),
        pltpu.VMEM((wide, depth), bf16),
        pltpu.VMEM((3, wide, depth), bf16),
        pltpu.VMEM((4, edge, depth), bf16),
        pltpu.VMEM((4, edge, depth), bf16),
        pltpu.VMEM((planes, 2, 16, depth), f32),
        pltpu.VMEM((1, atoms), f32),
        pltpu.VMEM((1, atoms), f32),
        pltpu.VMEM((wide, depth), bf16),
        pltpu.VMEM((na, 3, 1, atoms), f32),
        pltpu.VMEM((na, 3, 1, atoms), f32),
        pltpu.VMEM((2, 4, 1, GHOST), f32),
        pltpu.VMEM((4, 1, GHOST), f32),
        pltpu.VMEM((4, 1, GHOST), f32),
        pltpu.VMEM((blocks, 1, CELL), f32),
        pltpu.VMEM((blocks, 1, CELL), f32),
        pltpu.VMEM((blocks, 1, CELL), i32),
        pltpu.VMEM((blocks, 1, CELL), i32),
        pltpu.VMEM((atoms, CELL), f32),
        pltpu.VMEM((atoms, CELL), i32),
        pltpu.VMEM((atoms, CELL), i32),
        pltpu.VMEM((3, atoms, CELL), f32),
        pltpu.VMEM((bricks, 1, CELL), f32),
        pltpu.SemaphoreType.DMA((14,)),
    ]
    for count in (na, 2, 2, 4, 4, 4, na, bricks):
        scratch += [pltpu.SemaphoreType.DMA((count,))] * 2
    tall = lambda v: v.reshape(3, 1, atoms)
    new_positions, new_velocities, deviation = pl.pallas_call(
        functools.partial(kernel, (members, bricks, thick, rows, depth, atoms)),
        out_shape=(
            jax.ShapeDtypeStruct((3, 1, atoms), f32),
            jax.ShapeDtypeStruct((3, 1, atoms), f32),
            jax.ShapeDtypeStruct((thick, rows // members, depth), f32),
        ),
        in_specs=[hbm] * 10 + [smem] + [hbm] * 2,
        out_specs=(vmem, vmem, vmem),
        scratch_shapes=scratch,
        compiler_params=pltpu.CompilerParams(
            collective_id=0, has_side_effects=True, vmem_limit_bytes=40 * 2**20
        ),
        cost_estimate=pl.CostEstimate(
            flops=1_200_000_000, bytes_accessed=400_000, transcendentals=4_000_000
        ),
    )(
        *(
            pltpu.with_memory_space_constraint(v, pltpu.HBM)
            for v in (
                tall(atom_locations),
                tall(atom_speeds_vector),
                inertial_amounts,
                electric_loads,
                scatter_strengths,
                gaussian_spreads_sigma,
                atom_present_flags,
                halo_sender_spots,
                paired_partner_lists,
                cell_usage_tally,
            )
        ),
        target_warmth_levels.reshape(1, 1),
        pltpu.with_memory_space_constraint(observed_volume_values, pltpu.HBM),
        pltpu.with_memory_space_constraint(voxel_reciprocal_spread, pltpu.HBM),
    )
    made = (new_positions, new_velocities, deviation)
    new_positions, new_velocities, deviation = pl.pallas_call(
        functools.partial(write, len(made)),
        out_shape=tuple(jax.ShapeDtypeStruct(v.shape, v.dtype) for v in made),
        in_specs=[vmem] * len(made),
        out_specs=tuple(hbm for _ in made),
        scratch_shapes=[pltpu.SemaphoreType.DMA((len(made),))],
    )(*(pltpu.with_memory_space_constraint(v, pltpu.VMEM) for v in made))
    return (
        new_positions.reshape(1, 3, atoms),
        new_velocities.reshape(1, 3, atoms),
        deviation,
    )


def solution(mesh):
    return jax.shard_map(
        local,
        mesh=mesh,
        in_specs=(
            P("replica", None, "brick"),
            P("replica", None, "brick"),
            P("brick"),
            P("brick"),
            P("brick"),
            P("brick"),
            P("brick"),
            P("brick", None, None),
            P("brick", None, None),
            P("brick", None),
            P("brick"),
            P(None, "brick"),
            P("replica"),
        ),
        out_specs=(
            P("replica", None, "brick"),
            P("replica", None, "brick"),
            P("brick", "replica", None),
        ),
        check_vma=False,
    )
```

```python
import functools
import math

import jax
import jax.numpy as jnp
from jax import lax
from jax.experimental import pallas as pl
from jax.experimental.pallas import tpu as pltpu
from jax.sharding import PartitionSpec as P

MESH = pl.DeviceIdType.MESH

HALO = 2
CELL = 128
GHOST = 256
LOG2E = 1.4426950408889634
B_STEPS = ((0, 0), (0, 1), (1, 0), (1, 1))

restraint = 0.1
coupling = 5.0
softening = 1.0
timestep = 0.5
boltzmann = 0.015
heat_bath_damping = 0.5


def fixed(coord, period):
    scale = 2.0**31 / period
    return (coord * scale).astype(jnp.int32) << 1


def dot_t(a, b):
    return lax.dot_general(a, b, (((1,), (1,)), ((), ())), preferred_element_type=jnp.float32)


def kernel(
    dims,
    loc_at,
    vel_at,
    mass_at,
    load_at,
    strength_at,
    sigma_at,
    flag_at,
    spots_at,
    lists_at,
    tally_at,
    warm,
    obs,
    vrs,
    pos_out,
    vel_out,
    dev_out,
    vel,
    mass_ref,
    load_ref,
    strength_ref,
    sigma_ref,
    flag_ref,
    spots,
    lists,
    tally,
    crd,
    zz,
    gxs,
    gxds,
    gys,
    gyds,
    acc,
    mine,
    rs,
    halo,
    obv,
    amps,
    ivs,
    grd,
    frc,
    frcin,
    gsend,
    glo,
    ghi,
    bx,
    bq,
    by,
    bz,
    colx,
    coly,
    colz,
    pacc,
    kin,
    loc_sem,
    crd_ss,
    crd_rs,
    gh_ss,
    gh_rs,
    ob_ss,
    ob_rs,
    rs_ss,
    rs_rs,
    hl_ss,
    hl_rs,
    fr_ss,
    fr_rs,
    kn_ss,
    kn_rs,
):
    members, bricks, thick, rows, depth, atoms = dims
    half = members // 2
    na = half // 2
    share = rows // members
    planes = thick + 2 * HALO
    wide = planes * 16
    edge = 2 * HALO * 16
    cells = atoms // CELL
    slots = lists.shape[1]
    r = lax.axis_index("replica")
    b = lax.axis_index("brick")
    x, z = r // half, r % half
    zh, zp = z // 2, z % 2
    up, down = (b + 1) % bricks, (b + bricks - 1) % bricks

    def a_peer(d):
        return (x * half + ((zh + d) % na) * 2 + zp, b)

    def b_rep(k):
        dx, dp = B_STEPS[k]
        return ((x + dx) % 2) * half + zh * 2 + (zp + dp) % 2

    def brick_at(n):
        y, xh, core = n // 4, n // 2 % 2, n % 2
        return (b // 4 + y) % (bricks // 4) * 4 + (b // 2 + xh) % 2 * 2 + (b + core) % 2

    far_first = sorted(
        range(1, bricks), key=lambda n: -(min(n // 4, 4 - n // 4) + n // 2 % 2 * 2 + n % 2)
    )

    def nearest(t):
        odd = t % 2
        return odd * ((t + 1) // 2) + (1 - odd) * ((na - t // 2) % na)

    direct = [nearest(t) for t in range(1, na)]
    relayed = {}
    if na == 8:
        direct = direct[:4]
        relayed = {1: (3, 2), 7: (5, 6), 2: (4, 2)}

    barrier = pltpu.get_barrier_semaphore()
    partners = [a_peer(d) for d in reversed(direct)]
    partners += [(r, brick_at(n)) for n in far_first]
    partners += [(b_rep(k), n) for n in (up, down, b) for k in range(1, 4)]
    for p in partners:
        pl.semaphore_signal(barrier, inc=1, device_id=p, device_id_type=MESH)

    fetched = {
        "loc": (loc_at, crd.at[0]),
        "flag": (flag_at, flag_ref.at[0]),
        "strength": (strength_at, strength_ref.at[0]),
        "load": (load_at, load_ref.at[0]),
        "sigma": (sigma_at, sigma_ref.at[0]),
        "spots": (spots_at, spots),
        "lists": (lists_at, lists),
        "tally": (tally_at, tally),
        "vel": (vel_at, vel),
        "mass": (mass_at, mass_ref.at[0]),
    }
    for t in range(2):
        tile = pl.ds(pl.multiple_of(t * (rows // 2) + zh * 8, 8), 8)
        for i, src in enumerate((obs, vrs)):
            fetched["map", t, i] = (src.at[:, tile, :], obv.at[pl.ds(HALO, thick), i, pl.ds(8 * t, 8)])
    copies = {
        name: pltpu.make_async_copy(src, dst, loc_sem.at[i])
        for i, (name, (src, dst)) in enumerate(fetched.items())
    }
    for c in copies.values():
        c.start()
    copies["loc"].wait()
    sends = []

    def remote(src, dst, ss, rsem, device):
        return pltpu.make_async_remote_copy(
            src_ref=src, dst_ref=dst, send_sem=ss, recv_sem=rsem, device_id=device, device_id_type=MESH
        )

    def post(*a):
        c = remote(*a)
        c.start()
        sends.append(c)
        return c

    for name in ("flag", "strength", "load", "sigma", "spots"):
        copies[name].wait()
    loc = crd.at[0]
    occ = flag_ref[...].astype(jnp.float32)
    amp = occ * strength_ref[...]
    q = occ * load_ref[...]
    sigma = sigma_ref[...]
    iv = 1.0 / (sigma * sigma)

    four = jnp.concatenate([loc[0], loc[1], loc[2], q], axis=0)
    first = four.astype(jnp.bfloat16).astype(jnp.float32)
    rest = four - first
    second = rest.astype(jnp.bfloat16).astype(jnp.float32)
    third = rest - second
    pieces = jnp.concatenate([first, second, third, jnp.zeros_like(four)], axis=0).astype(jnp.bfloat16)
    slot_of = lax.broadcasted_iota(jnp.int32, (atoms, GHOST), 0)
    for side in range(2):
        chosen = jnp.where(slot_of == spots[side : side + 1, :], 1.0, 0.0).astype(jnp.bfloat16)
        got = jnp.dot(pieces, chosen, preferred_element_type=jnp.float32)
        got = got[0:4] + got[4:8] + got[8:12]
        for i in range(4):
            gsend[side, i] = got[i : i + 1]

    shift_y, shift_z = 32 - int(math.log2(rows)), 32 - int(math.log2(depth))
    unit_y, unit_z = 2.0**-shift_y, 2.0**-shift_z
    amps[...] = amp
    ivs[...] = iv

    def spread(d):
        amp, iv = amps[...], ivs[...]
        ivc = iv * (-0.5 * LOG2E)
        plane_at = (b * thick - HALO + lax.broadcasted_iota(jnp.int32, (16, atoms), 0)).astype(jnp.float32)
        row_in = lax.broadcasted_iota(jnp.int32, (16, atoms), 0)
        row_at = (zh * 8 + (row_in // 8) * (rows // 2) + row_in % 8) << shift_y
        dx = plane_at - crd[d, 0]
        gx = jnp.exp2(dx * dx * ivc)
        gxs[d] = gx
        gxds[d] = dx * iv * gx
        dy = (row_at - fixed(crd[d, 1], rows)).astype(jnp.float32)
        gy = jnp.exp2(dy * dy * (ivc * unit_y**2))
        gys[d] = gy
        gyds[d] = dy * (iv * unit_y) * gy
        level = lax.broadcasted_iota(jnp.int32, (depth, atoms), 0) << shift_z
        dz = (level - fixed(crd[d, 2], depth)).astype(jnp.float32)
        gz = jnp.exp2(dz * dz * (ivc * unit_z**2))
        zz[d, :, atoms:] = (dz * (iv * unit_z) * gz).astype(jnp.bfloat16)
        gzb = gz.astype(jnp.bfloat16)
        zz[d, :, :atoms] = gzb
        left = (amp * gx)[:planes, None, :] * gy[None]
        part = dot_t(left.reshape(wide, atoms).astype(jnp.bfloat16), gzb)
        if isinstance(d, int):
            acc[...] = part
        else:
            acc[...] += part

    spread(0)

    pl.semaphore_wait(barrier, len(partners))
    crd_in = {}
    for d in reversed(direct):
        crd_in[d] = post(crd.at[0], crd.at[d], crd_ss.at[d], crd_rs.at[d], a_peer(d))
    gh_in = [
        post(gsend.at[0], glo, gh_ss.at[0], gh_rs.at[0], (r, up)),
        post(gsend.at[1], ghi, gh_ss.at[1], gh_rs.at[1], (r, down)),
    ]
    for t in range(2):
        for i in range(2):
            copies["map", t, i].wait()
    ob_in = [
        post(obv.at[pl.ds(thick, HALO)], obv.at[pl.ds(0, HALO)], ob_ss.at[0], ob_rs.at[0], (r, up)),
        post(
            obv.at[pl.ds(HALO, HALO)],
            obv.at[pl.ds(thick + HALO, HALO)],
            ob_ss.at[1],
            ob_rs.at[1],
            (r, down),
        ),
    ]


    def column(c, _):
        at = pl.ds(pl.multiple_of(c * CELL, CELL), CELL)
        for i, col in enumerate((colx, coly, colz)):
            v = jnp.broadcast_to(loc[i, :, at], (CELL, CELL)).T
            col[at] = v * 2.0**shift_z if i == 0 else fixed(v, (rows, depth)[i - 1])
        return 0

    lax.fori_loop(0, cells, column, 0)

    scale_x = 2.0**shift_z
    for c in range(cells):
        at = slice(c * CELL, (c + 1) * CELL)
        bx[c] = loc[0, :, at] * scale_x
        by[c] = fixed(loc[1, :, at], rows)
        bz[c] = fixed(loc[2, :, at], depth)
        bq[c] = q[:, at]
    none = cells + 4
    for ref in (bx, bq, by, bz):
        ref[none] = jnp.zeros((1, CELL), ref.dtype)

    def await_crd(d):
        crd_in[d].wait_recv()
        if d in relayed:
            far, to = relayed[d]
            crd_in[far] = post(crd.at[d], crd.at[far], crd_ss.at[far], crd_rs.at[far], a_peer(to))

    early = (1, 7, 2) if na == 8 else ()
    for d in early:
        await_crd(d)

    def collect(t, _):
        d = nearest(t)

        @pl.when(t > len(early))
        def _():
            remote(crd.at[0], crd.at[d], crd_ss.at[d], crd_rs.at[d], a_peer(d)).wait_recv()

        spread(d)
        return 0

    lax.fori_loop(1, na, collect, 0)

    mine[...] = acc[...].astype(jnp.bfloat16)
    core = b % 2

    def post_edge(side, k):
        start = pl.multiple_of((1 - side) * (wide - edge), 16)
        at = side * 4 + k
        post(
            mine.at[pl.ds(start, edge)],
            halo.at[side, k],
            hl_ss.at[at],
            hl_rs.at[at],
            (b_rep(k), (b + bricks + 1 - 2 * side) % bricks),
        )

    map_in = []

    def post_map(k):
        map_in.append(post(mine, rs.at[k - 1], rs_ss.at[k], rs_rs.at[k], (b_rep(k), b)))

    for k in (1, 0, 3, 2):
        post_edge(1 - core, k)
    post_map(3)
    for k in (3, 1):
        post_edge(core, k)
    post_map(1)
    post_edge(core, 2)
    post_map(2)
    post_edge(core, 0)
    for side in range(2):
        for k in range(4):
            at = side * 4 + k
            map_in.append(
                remote(mine.at[pl.ds(0, edge)], halo.at[side, k], hl_ss.at[at], hl_rs.at[at], (b_rep(k), up))
            )

    for c in gh_in:
        c.wait_recv()
    period_x = float(thick * bricks)
    for side, src in enumerate((glo, ghi)):
        if side == 0:
            move = jnp.where(b == 0, -period_x, 0.0)
        else:
            move = jnp.where(b == bricks - 1, period_x, 0.0)
        for g in range(2):
            at = slice(g * CELL, (g + 1) * CELL)
            n = cells + 2 * side + g
            bx[n] = (src[0, :, at] + move) * scale_x
            by[n] = fixed(src[1, :, at], rows)
            bz[n] = fixed(src[2, :, at], depth)
            bq[n] = src[3, :, at]

    part_rows = 32
    parts = CELL // part_rows

    def pair(u, _):
        c = u // parts
        at = pl.ds(pl.multiple_of(u * part_rows, part_rows), part_rows)
        xi, yi, zi = colx[at], coly[at], colz[at]
        total = [jnp.zeros((part_rows, CELL), jnp.float32)] * 3
        for s in range(slots):
            n = jnp.where(s < tally[c], lists[c, s], none)
            dx = xi - bx[n]
            dy = (yi - by[n]).astype(jnp.float32)
            dz = (zi - bz[n]).astype(jnp.float32)
            if shift_y != shift_z:
                dy = dy * 2.0 ** (shift_z - shift_y)
            inv = lax.rsqrt(dx * dx + dy * dy + dz * dz + softening * 4.0**shift_z)
            pull = inv * inv * inv * bq[n]
            total = [total[0] + pull * dx, total[1] + pull * dy, total[2] + pull * dz]
        for i in range(3):
            pacc[i, at] = total[i]
        return 0

    units = cells * parts
    copies["lists"].wait()
    copies["tally"].wait()
    lax.fori_loop(0, units // 2, pair, 0)

    for c in ob_in + map_in:
        c.wait_recv()
    wider = lambda v: v.astype(jnp.float32)
    total = acc[...] + wider(rs[0]) + wider(rs[1]) + wider(rs[2])
    low, high = (
        wider(halo[i, 0]) + wider(halo[i, 1]) + wider(halo[i, 2]) + wider(halo[i, 3]) for i in range(2)
    )
    total = jnp.concatenate(
        [total[:edge] + low, total[edge : wide - edge], total[wide - edge :] + high], axis=0
    ).reshape(planes, 16, depth)
    dev = total / members - obv[:, 0]
    grad = (restraint * obv[:, 1] * dev).astype(jnp.bfloat16)
    grd[...] = grad.reshape(wide, depth)
    own = dev[HALO : HALO + thick]
    own = jnp.where(x == 0, own[:, :8], own[:, 8:])
    dev_out[...] = jnp.where(zp == 0, own[:, :share], own[:, share:])

    lanes = 256

    def force(d):
        for c in range(atoms // lanes):
            at = slice(c * lanes, (c + 1) * lanes)
            after = slice(atoms + c * lanes, atoms + (c + 1) * lanes)
            along = jnp.dot(grd[...], zz[d, :, at], preferred_element_type=jnp.float32)
            slope = jnp.dot(grd[...], zz[d, :, after], preferred_element_type=jnp.float32)
            sums = [0.0, 0.0, 0.0]
            for i in range(planes):
                p = along[16 * i : 16 * i + 16]
                g = gxs[d, i : i + 1, at]
                sums[0] += gxds[d, i : i + 1, at] * p
                sums[1] += g * p
                sums[2] += g * slope[16 * i : 16 * i + 16]
            y = gys[d, :, at]
            f = (y * sums[0], gyds[d, :, at] * sums[1], y * sums[2])
            for i in range(3):
                frc[d, i, :, at] = jnp.sum(f[i], axis=0, keepdims=True)

    def fr_copy(d):
        return remote(frc.at[d], frcin.at[d], fr_ss.at[d], fr_rs.at[d], a_peer((na - d) % na))

    def give(t, _):
        d = nearest(na - 1 - t)
        force(d)

        @pl.when(t < na - 1)
        def _():
            fr_copy(d).start()

        return 0

    lax.fori_loop(0, na, give, 0)

    lax.fori_loop(units // 2, units, pair, 0)
    for name in ("vel", "mass"):
        copies[name].wait()
    mass = mass_ref[...]
    light = timestep / mass
    gain = (coupling * 4.0**shift_z) * q * light
    push = amps[...] * light
    v_half = []
    for i in range(3):
        line = [
            jnp.sum(pacc[i, c * CELL : (c + 1) * CELL].T, axis=0, keepdims=True) for c in range(cells)
        ]
        v_half.append(vel[i] + gain * jnp.concatenate(line, axis=1))

    for d in range(1, na):
        fr_copy(d).wait_recv()
    square = jnp.zeros((1, atoms), jnp.float32)
    for i in range(3):
        f = frc[0, i]
        for d in range(1, na):
            f = f + frcin[d, i]
        v_half[i] = v_half[i] - push * f
        square = square + v_half[i] * v_half[i]
    square = mass * square
    row = square[:, :CELL]
    for c in range(1, cells):
        row = row + square[:, c * CELL : (c + 1) * CELL]
    kin[0] = row
    kn_in = [
        post(kin.at[0], kin.at[n], kn_ss.at[n], kn_rs.at[n], (r, brick_at(n)))
        for n in far_first
    ]
    for c in kn_in:
        c.wait_recv()
    for d in range(1, bricks):
        row = row + kin[d]
    kinetic = jnp.sum(row, axis=1, keepdims=True)
    present = kinetic / (3 * atoms * bricks * boltzmann) + 1e-06
    wanted = jnp.full((1, 1), warm[0, 0].astype(jnp.float32))
    ratio = jnp.sqrt(1.0 + heat_bath_damping * (wanted / present - 1.0))
    for i in range(3):
        v = ratio * v_half[i]
        vel_out[i] = v
        pos_out[i] = loc[i] + timestep * v
    for d in range(1, na):
        fr_copy(d).wait_send()
    for c in sends:
        c.wait_send()


def write(count, *refs):
    sources, targets, sem = refs[:count], refs[count:-1], refs[-1]
    copies = [pltpu.make_async_copy(a, c, sem.at[i]) for i, (a, c) in enumerate(zip(sources, targets))]
    for c in copies:
        c.start()
    for c in copies:
        c.wait()


def local(
    atom_locations,
    atom_speeds_vector,
    inertial_amounts,
    electric_loads,
    scatter_strengths,
    gaussian_spreads_sigma,
    atom_present_flags,
    observed_volume_values,
    voxel_reciprocal_spread,
    paired_partner_lists,
    cell_usage_tally,
    halo_sender_spots,
    target_warmth_levels,
):
    thick, rows, depth = observed_volume_values.shape
    atoms = atom_locations.shape[2]
    members, bricks = lax.axis_size("replica"), lax.axis_size("brick")
    na = members // 4
    planes = thick + 2 * HALO
    wide = planes * 16
    cells = atoms // CELL
    blocks = cells + 5
    f32, bf16, i32 = jnp.float32, jnp.bfloat16, jnp.int32
    vmem = pl.BlockSpec(memory_space=pltpu.VMEM)
    hbm = pl.BlockSpec(memory_space=pltpu.HBM)
    smem = pl.BlockSpec(memory_space=pltpu.SMEM)
    edge = 2 * HALO * 16
    scratch = [
        pltpu.VMEM((3, 1, atoms), f32),
        pltpu.VMEM((1, atoms), f32),
        pltpu.VMEM((1, atoms), f32),
        pltpu.VMEM((1, atoms), f32),
        pltpu.VMEM((1, atoms), f32),
        pltpu.VMEM((1, atoms), i32),
        pltpu.VMEM((2, GHOST), i32),
        pltpu.SMEM(paired_partner_lists.shape, i32),
        pltpu.SMEM((cells,), i32),
        pltpu.VMEM((na, 3, 1, atoms), f32),
        pltpu.VMEM((na, depth, 2 * atoms), bf16),
        pltpu.VMEM((na, 16, atoms), f32),
        pltpu.VMEM((na, 16, atoms), f32),
        pltpu.VMEM((na, 16, atoms), f32),
        pltpu.VMEM((na, 16, atoms), f32),
        pltpu.VMEM((wide, depth), f32),
        pltpu.VMEM((wide, depth), bf16),
        pltpu.VMEM((3, wide, depth), bf16),
        pltpu.VMEM((2, 4, edge, depth), bf16),
        pltpu.VMEM((planes, 2, 16, depth), f32),
        pltpu.VMEM((1, atoms), f32),
        pltpu.VMEM((1, atoms), f32),
        pltpu.VMEM((wide, depth), bf16),
        pltpu.VMEM((na, 3, 1, atoms), f32),
        pltpu.VMEM((na, 3, 1, atoms), f32),
        pltpu.VMEM((2, 4, 1, GHOST), f32),
        pltpu.VMEM((4, 1, GHOST), f32),
        pltpu.VMEM((4, 1, GHOST), f32),
        pltpu.VMEM((blocks, 1, CELL), f32),
        pltpu.VMEM((blocks, 1, CELL), f32),
        pltpu.VMEM((blocks, 1, CELL), i32),
        pltpu.VMEM((blocks, 1, CELL), i32),
        pltpu.VMEM((atoms, CELL), f32),
        pltpu.VMEM((atoms, CELL), i32),
        pltpu.VMEM((atoms, CELL), i32),
        pltpu.VMEM((3, atoms, CELL), f32),
        pltpu.VMEM((bricks, 1, CELL), f32),
        pltpu.SemaphoreType.DMA((14,)),
    ]
    for count in (na, 2, 2, 4, 8, na, bricks):
        scratch += [pltpu.SemaphoreType.DMA((count,))] * 2
    tall = lambda v: v.reshape(3, 1, atoms)
    new_positions, new_velocities, deviation = pl.pallas_call(
        functools.partial(kernel, (members, bricks, thick, rows, depth, atoms)),
        out_shape=(
            jax.ShapeDtypeStruct((3, 1, atoms), f32),
            jax.ShapeDtypeStruct((3, 1, atoms), f32),
            jax.ShapeDtypeStruct((thick, rows // members, depth), f32),
        ),
        in_specs=[hbm] * 10 + [smem] + [hbm] * 2,
        out_specs=(vmem, vmem, vmem),
        scratch_shapes=scratch,
        compiler_params=pltpu.CompilerParams(
            collective_id=0, has_side_effects=True, vmem_limit_bytes=40 * 2**20
        ),
        cost_estimate=pl.CostEstimate(
            flops=1_200_000_000, bytes_accessed=400_000, transcendentals=4_000_000
        ),
    )(
        *(
            pltpu.with_memory_space_constraint(v, pltpu.HBM)
            for v in (
                tall(atom_locations),
                tall(atom_speeds_vector),
                inertial_amounts,
                electric_loads,
                scatter_strengths,
                gaussian_spreads_sigma,
                atom_present_flags,
                halo_sender_spots,
                paired_partner_lists,
                cell_usage_tally,
            )
        ),
        target_warmth_levels.reshape(1, 1),
        pltpu.with_memory_space_constraint(observed_volume_values, pltpu.HBM),
        pltpu.with_memory_space_constraint(voxel_reciprocal_spread, pltpu.HBM),
    )
    made = (new_positions, new_velocities, deviation)
    new_positions, new_velocities, deviation = pl.pallas_call(
        functools.partial(write, len(made)),
        out_shape=tuple(jax.ShapeDtypeStruct(v.shape, v.dtype) for v in made),
        in_specs=[vmem] * len(made),
        out_specs=tuple(hbm for _ in made),
        scratch_shapes=[pltpu.SemaphoreType.DMA((len(made),))],
    )(*(pltpu.with_memory_space_constraint(v, pltpu.VMEM) for v in made))
    return (
        new_positions.reshape(1, 3, atoms),
        new_velocities.reshape(1, 3, atoms),
        deviation,
    )


def solution(mesh):
    return jax.shard_map(
        local,
        mesh=mesh,
        in_specs=(
            P("replica", None, "brick"),
            P("replica", None, "brick"),
            P("brick"),
            P("brick"),
            P("brick"),
            P("brick"),
            P("brick"),
            P("brick", None, None),
            P("brick", None, None),
            P("brick", None),
            P("brick"),
            P(None, "brick"),
            P("replica"),
        ),
        out_specs=(
            P("replica", None, "brick"),
            P("replica", None, "brick"),
            P("brick", "replica", None),
        ),
        check_vma=False,
    )
```

```python
import functools
import math

import jax
import jax.numpy as jnp
from jax import lax
from jax.experimental import pallas as pl
from jax.experimental.pallas import tpu as pltpu
from jax.sharding import PartitionSpec as P

MESH = pl.DeviceIdType.MESH

HALO = 2
CELL = 128
GHOST = 256
LOG2E = 1.4426950408889634
B_STEPS = ((0, 0), (0, 1), (1, 0), (1, 1))

restraint = 0.1
coupling = 5.0
softening = 1.0
timestep = 0.5
boltzmann = 0.015
heat_bath_damping = 0.5


def fixed(coord, period):
    scale = 2.0**31 / period
    return (coord * scale).astype(jnp.int32) << 1


def dot_t(a, b):
    return lax.dot_general(a, b, (((1,), (1,)), ((), ())), preferred_element_type=jnp.float32)


def kernel(
    dims,
    loc_at,
    vel_at,
    mass_at,
    load_at,
    strength_at,
    sigma_at,
    flag_at,
    spots_at,
    lists_at,
    tally_at,
    warm,
    obs,
    vrs,
    pos_out,
    vel_out,
    dev_out,
    vel,
    mass_ref,
    load_ref,
    strength_ref,
    sigma_ref,
    flag_ref,
    spots,
    lists,
    tally,
    crd,
    zz,
    gxs,
    gxds,
    gys,
    gyds,
    acc,
    mine,
    rs,
    halo,
    obv,
    amps,
    ivs,
    grd,
    frc,
    frcin,
    gsend,
    glo,
    ghi,
    bx,
    bq,
    by,
    bz,
    colx,
    coly,
    colz,
    pacc,
    kin,
    loc_sem,
    crd_ss,
    crd_rs,
    gh_ss,
    gh_rs,
    ob_ss,
    ob_rs,
    rs_ss,
    rs_rs,
    hl_ss,
    hl_rs,
    fr_ss,
    fr_rs,
    kn_ss,
    kn_rs,
):
    members, bricks, thick, rows, depth, atoms = dims
    half = members // 2
    na = half // 2
    share = rows // members
    planes = thick + 2 * HALO
    wide = planes * 16
    edge = 2 * HALO * 16
    cells = atoms // CELL
    slots = lists.shape[1]
    r = lax.axis_index("replica")
    b = lax.axis_index("brick")
    x, z = r // half, r % half
    zh, zp = z // 2, z % 2
    up, down = (b + 1) % bricks, (b + bricks - 1) % bricks

    def a_peer(d):
        return (x * half + ((zh + d) % na) * 2 + zp, b)

    def b_rep(k):
        dx, dp = B_STEPS[k]
        return ((x + dx) % 2) * half + zh * 2 + (zp + dp) % 2

    def brick_at(n):
        y, xh, core = n // 4, n // 2 % 2, n % 2
        return (b // 4 + y) % (bricks // 4) * 4 + (b // 2 + xh) % 2 * 2 + (b + core) % 2

    far_first = sorted(
        range(1, bricks), key=lambda n: -(min(n // 4, 4 - n // 4) + n // 2 % 2 * 2 + n % 2)
    )

    def nearest(t):
        odd = t % 2
        return odd * ((t + 1) // 2) + (1 - odd) * ((na - t // 2) % na)

    direct = [nearest(t) for t in range(1, na)]
    relayed = {}
    if na == 8:
        direct = direct[:4]
        relayed = {1: (3, 2), 7: (5, 6), 2: (4, 2)}

    barrier = pltpu.get_barrier_semaphore()
    partners = [a_peer(d) for d in reversed(direct)]
    partners += [(r, brick_at(n)) for n in far_first]
    partners += [(b_rep(k), b) for k in range(1, 4)]
    for p in partners:
        pl.semaphore_signal(barrier, inc=1, device_id=p, device_id_type=MESH)

    fetched = {
        "loc": (loc_at, crd.at[0]),
        "flag": (flag_at, flag_ref.at[0]),
        "strength": (strength_at, strength_ref.at[0]),
        "load": (load_at, load_ref.at[0]),
        "sigma": (sigma_at, sigma_ref.at[0]),
        "spots": (spots_at, spots),
        "lists": (lists_at, lists),
        "tally": (tally_at, tally),
        "vel": (vel_at, vel),
        "mass": (mass_at, mass_ref.at[0]),
    }
    for t in range(2):
        tile = pl.ds(pl.multiple_of(t * (rows // 2) + zh * 8, 8), 8)
        for i, src in enumerate((obs, vrs)):
            fetched["map", t, i] = (src.at[:, tile, :], obv.at[pl.ds(HALO, thick), i, pl.ds(8 * t, 8)])
    copies = {
        name: pltpu.make_async_copy(src, dst, loc_sem.at[i])
        for i, (name, (src, dst)) in enumerate(fetched.items())
    }
    for c in copies.values():
        c.start()
    copies["loc"].wait()
    sends = []

    def remote(src, dst, ss, rsem, device):
        return pltpu.make_async_remote_copy(
            src_ref=src, dst_ref=dst, send_sem=ss, recv_sem=rsem, device_id=device, device_id_type=MESH
        )

    def post(*a):
        c = remote(*a)
        c.start()
        sends.append(c)
        return c

    for name in ("flag", "strength", "load", "sigma", "spots"):
        copies[name].wait()
    loc = crd.at[0]
    occ = flag_ref[...].astype(jnp.float32)
    amp = occ * strength_ref[...]
    q = occ * load_ref[...]
    sigma = sigma_ref[...]
    iv = 1.0 / (sigma * sigma)

    four = jnp.concatenate([loc[0], loc[1], loc[2], q], axis=0)
    first = four.astype(jnp.bfloat16).astype(jnp.float32)
    rest = four - first
    second = rest.astype(jnp.bfloat16).astype(jnp.float32)
    third = rest - second
    pieces = jnp.concatenate([first, second, third, jnp.zeros_like(four)], axis=0).astype(jnp.bfloat16)
    slot_of = lax.broadcasted_iota(jnp.int32, (atoms, GHOST), 0)
    for side in range(2):
        chosen = jnp.where(slot_of == spots[side : side + 1, :], 1.0, 0.0).astype(jnp.bfloat16)
        got = jnp.dot(pieces, chosen, preferred_element_type=jnp.float32)
        got = got[0:4] + got[4:8] + got[8:12]
        for i in range(4):
            gsend[side, i] = got[i : i + 1]

    shift_y, shift_z = 32 - int(math.log2(rows)), 32 - int(math.log2(depth))
    unit_y, unit_z = 2.0**-shift_y, 2.0**-shift_z
    amps[...] = amp
    ivs[...] = iv

    def spread(d):
        amp, iv = amps[...], ivs[...]
        ivc = iv * (-0.5 * LOG2E)
        plane_at = (b * thick - HALO + lax.broadcasted_iota(jnp.int32, (16, atoms), 0)).astype(jnp.float32)
        row_in = lax.broadcasted_iota(jnp.int32, (16, atoms), 0)
        row_at = (zh * 8 + (row_in // 8) * (rows // 2) + row_in % 8) << shift_y
        dx = plane_at - crd[d, 0]
        gx = jnp.exp2(dx * dx * ivc)
        gxs[d] = gx
        gxds[d] = dx * iv * gx
        dy = (row_at - fixed(crd[d, 1], rows)).astype(jnp.float32)
        gy = jnp.exp2(dy * dy * (ivc * unit_y**2))
        gys[d] = gy
        gyds[d] = dy * (iv * unit_y) * gy
        level = lax.broadcasted_iota(jnp.int32, (depth, atoms), 0) << shift_z
        dz = (level - fixed(crd[d, 2], depth)).astype(jnp.float32)
        gz = jnp.exp2(dz * dz * (ivc * unit_z**2))
        zz[d, :, atoms:] = (dz * (iv * unit_z) * gz).astype(jnp.bfloat16)
        gzb = gz.astype(jnp.bfloat16)
        zz[d, :, :atoms] = gzb
        left = (amp * gx)[:planes, None, :] * gy[None]
        part = dot_t(left.reshape(wide, atoms).astype(jnp.bfloat16), gzb)
        if isinstance(d, int):
            acc[...] = part
        else:
            acc[...] += part

    spread(0)

    pl.semaphore_wait(barrier, len(partners))
    crd_in = {}
    for d in reversed(direct):
        crd_in[d] = post(crd.at[0], crd.at[d], crd_ss.at[d], crd_rs.at[d], a_peer(d))
    gh_in = [
        post(gsend.at[0], glo, gh_ss.at[0], gh_rs.at[0], (r, up)),
        post(gsend.at[1], ghi, gh_ss.at[1], gh_rs.at[1], (r, down)),
    ]
    for t in range(2):
        for i in range(2):
            copies["map", t, i].wait()
    ob_in = [
        post(obv.at[pl.ds(thick, HALO)], obv.at[pl.ds(0, HALO)], ob_ss.at[0], ob_rs.at[0], (r, up)),
        post(
            obv.at[pl.ds(HALO, HALO)],
            obv.at[pl.ds(thick + HALO, HALO)],
            ob_ss.at[1],
            ob_rs.at[1],
            (r, down),
        ),
    ]


    def column(c, _):
        at = pl.ds(pl.multiple_of(c * CELL, CELL), CELL)
        for i, col in enumerate((colx, coly, colz)):
            v = jnp.broadcast_to(loc[i, :, at], (CELL, CELL)).T
            col[at] = v * 2.0**shift_z if i == 0 else fixed(v, (rows, depth)[i - 1])
        return 0

    lax.fori_loop(0, cells, column, 0)

    scale_x = 2.0**shift_z
    for c in range(cells):
        at = slice(c * CELL, (c + 1) * CELL)
        bx[c] = loc[0, :, at] * scale_x
        by[c] = fixed(loc[1, :, at], rows)
        bz[c] = fixed(loc[2, :, at], depth)
        bq[c] = q[:, at]
    none = cells + 4
    for ref in (bx, bq, by, bz):
        ref[none] = jnp.zeros((1, CELL), ref.dtype)

    def await_crd(d):
        crd_in[d].wait_recv()
        if d in relayed:
            far, to = relayed[d]
            crd_in[far] = post(crd.at[d], crd.at[far], crd_ss.at[far], crd_rs.at[far], a_peer(to))

    early = (1, 7, 2) if na == 8 else ()
    for d in early:
        await_crd(d)

    def collect(t, _):
        d = nearest(t)

        @pl.when(t > len(early))
        def _():
            remote(crd.at[0], crd.at[d], crd_ss.at[d], crd_rs.at[d], a_peer(d)).wait_recv()

        spread(d)
        return 0

    lax.fori_loop(1, na, collect, 0)

    mine[...] = acc[...].astype(jnp.bfloat16)
    for c in gh_in:
        c.wait_recv()

    core = b % 2

    def post_edge(side, k):
        start = pl.multiple_of((1 - side) * (wide - edge), 16)
        at = side * 4 + k
        post(
            mine.at[pl.ds(start, edge)],
            halo.at[side, k],
            hl_ss.at[at],
            hl_rs.at[at],
            (b_rep(k), (b + bricks + 1 - 2 * side) % bricks),
        )

    map_in = []

    def post_map(k):
        map_in.append(post(mine, rs.at[k - 1], rs_ss.at[k], rs_rs.at[k], (b_rep(k), b)))

    for k in (1, 0, 3, 2):
        post_edge(1 - core, k)
    post_map(3)
    for k in (3, 1):
        post_edge(core, k)
    post_map(1)
    post_edge(core, 2)
    post_map(2)
    post_edge(core, 0)
    for side in range(2):
        for k in range(4):
            at = side * 4 + k
            map_in.append(
                remote(mine.at[pl.ds(0, edge)], halo.at[side, k], hl_ss.at[at], hl_rs.at[at], (b_rep(k), up))
            )

    period_x = float(thick * bricks)
    for side, src in enumerate((glo, ghi)):
        if side == 0:
            move = jnp.where(b == 0, -period_x, 0.0)
        else:
            move = jnp.where(b == bricks - 1, period_x, 0.0)
        for g in range(2):
            at = slice(g * CELL, (g + 1) * CELL)
            n = cells + 2 * side + g
            bx[n] = (src[0, :, at] + move) * scale_x
            by[n] = fixed(src[1, :, at], rows)
            bz[n] = fixed(src[2, :, at], depth)
            bq[n] = src[3, :, at]

    part_rows = 32
    parts = CELL // part_rows

    def pair(u, _):
        c = u // parts
        at = pl.ds(pl.multiple_of(u * part_rows, part_rows), part_rows)
        xi, yi, zi = colx[at], coly[at], colz[at]
        total = [jnp.zeros((part_rows, CELL), jnp.float32)] * 3
        for s in range(slots):
            n = jnp.where(s < tally[c], lists[c, s], none)
            dx = xi - bx[n]
            dy = (yi - by[n]).astype(jnp.float32)
            dz = (zi - bz[n]).astype(jnp.float32)
            if shift_y != shift_z:
                dy = dy * 2.0 ** (shift_z - shift_y)
            inv = lax.rsqrt(dx * dx + dy * dy + dz * dz + softening * 4.0**shift_z)
            pull = inv * inv * inv * bq[n]
            total = [total[0] + pull * dx, total[1] + pull * dy, total[2] + pull * dz]
        for i in range(3):
            pacc[i, at] = total[i]
        return 0

    units = cells * parts
    copies["lists"].wait()
    copies["tally"].wait()
    lax.fori_loop(0, units // 2, pair, 0)

    for c in ob_in + map_in:
        c.wait_recv()
    wider = lambda v: v.astype(jnp.float32)
    total = acc[...] + wider(rs[0]) + wider(rs[1]) + wider(rs[2])
    low, high = (
        wider(halo[i, 0]) + wider(halo[i, 1]) + wider(halo[i, 2]) + wider(halo[i, 3]) for i in range(2)
    )
    total = jnp.concatenate(
        [total[:edge] + low, total[edge : wide - edge], total[wide - edge :] + high], axis=0
    ).reshape(planes, 16, depth)
    dev = total / members - obv[:, 0]
    grad = (restraint * obv[:, 1] * dev).astype(jnp.bfloat16)
    grd[...] = grad.reshape(wide, depth)
    own = dev[HALO : HALO + thick]
    own = jnp.where(x == 0, own[:, :8], own[:, 8:])
    dev_out[...] = jnp.where(zp == 0, own[:, :share], own[:, share:])

    lanes = 256

    def force(d):
        for c in range(atoms // lanes):
            at = slice(c * lanes, (c + 1) * lanes)
            after = slice(atoms + c * lanes, atoms + (c + 1) * lanes)
            along = jnp.dot(grd[...], zz[d, :, at], preferred_element_type=jnp.float32)
            slope = jnp.dot(grd[...], zz[d, :, after], preferred_element_type=jnp.float32)
            sums = [0.0, 0.0, 0.0]
            for i in range(planes):
                p = along[16 * i : 16 * i + 16]
                g = gxs[d, i : i + 1, at]
                sums[0] += gxds[d, i : i + 1, at] * p
                sums[1] += g * p
                sums[2] += g * slope[16 * i : 16 * i + 16]
            y = gys[d, :, at]
            f = (y * sums[0], gyds[d, :, at] * sums[1], y * sums[2])
            for i in range(3):
                frc[d, i, :, at] = jnp.sum(f[i], axis=0, keepdims=True)

    def fr_copy(d):
        return remote(frc.at[d], frcin.at[d], fr_ss.at[d], fr_rs.at[d], a_peer((na - d) % na))

    def give(t, _):
        d = nearest(na - 1 - t)
        force(d)

        @pl.when(t < na - 1)
        def _():
            fr_copy(d).start()

        return 0

    lax.fori_loop(0, na, give, 0)

    lax.fori_loop(units // 2, units, pair, 0)
    for name in ("vel", "mass"):
        copies[name].wait()
    mass = mass_ref[...]
    light = timestep / mass
    gain = (coupling * 4.0**shift_z) * q * light
    push = amps[...] * light
    v_half = []
    for i in range(3):
        line = [
            jnp.sum(pacc[i, c * CELL : (c + 1) * CELL].T, axis=0, keepdims=True) for c in range(cells)
        ]
        v_half.append(vel[i] + gain * jnp.concatenate(line, axis=1))

    for d in range(1, na):
        fr_copy(d).wait_recv()
    square = jnp.zeros((1, atoms), jnp.float32)
    for i in range(3):
        f = frc[0, i]
        for d in range(1, na):
            f = f + frcin[d, i]
        v_half[i] = v_half[i] - push * f
        square = square + v_half[i] * v_half[i]
    square = mass * square
    row = square[:, :CELL]
    for c in range(1, cells):
        row = row + square[:, c * CELL : (c + 1) * CELL]
    kin[0] = row
    kn_in = [
        post(kin.at[0], kin.at[n], kn_ss.at[n], kn_rs.at[n], (r, brick_at(n)))
        for n in far_first
    ]
    for c in kn_in:
        c.wait_recv()
    for d in range(1, bricks):
        row = row + kin[d]
    kinetic = jnp.sum(row, axis=1, keepdims=True)
    present = kinetic / (3 * atoms * bricks * boltzmann) + 1e-06
    wanted = jnp.full((1, 1), warm[0, 0].astype(jnp.float32))
    ratio = jnp.sqrt(1.0 + heat_bath_damping * (wanted / present - 1.0))
    for i in range(3):
        v = ratio * v_half[i]
        vel_out[i] = v
        pos_out[i] = loc[i] + timestep * v
    for d in range(1, na):
        fr_copy(d).wait_send()
    for c in sends:
        c.wait_send()


def write(count, *refs):
    sources, targets, sem = refs[:count], refs[count:-1], refs[-1]
    copies = [pltpu.make_async_copy(a, c, sem.at[i]) for i, (a, c) in enumerate(zip(sources, targets))]
    for c in copies:
        c.start()
    for c in copies:
        c.wait()


def local(
    atom_locations,
    atom_speeds_vector,
    inertial_amounts,
    electric_loads,
    scatter_strengths,
    gaussian_spreads_sigma,
    atom_present_flags,
    observed_volume_values,
    voxel_reciprocal_spread,
    paired_partner_lists,
    cell_usage_tally,
    halo_sender_spots,
    target_warmth_levels,
):
    thick, rows, depth = observed_volume_values.shape
    atoms = atom_locations.shape[2]
    members, bricks = lax.axis_size("replica"), lax.axis_size("brick")
    na = members // 4
    planes = thick + 2 * HALO
    wide = planes * 16
    cells = atoms // CELL
    blocks = cells + 5
    f32, bf16, i32 = jnp.float32, jnp.bfloat16, jnp.int32
    vmem = pl.BlockSpec(memory_space=pltpu.VMEM)
    hbm = pl.BlockSpec(memory_space=pltpu.HBM)
    smem = pl.BlockSpec(memory_space=pltpu.SMEM)
    edge = 2 * HALO * 16
    scratch = [
        pltpu.VMEM((3, 1, atoms), f32),
        pltpu.VMEM((1, atoms), f32),
        pltpu.VMEM((1, atoms), f32),
        pltpu.VMEM((1, atoms), f32),
        pltpu.VMEM((1, atoms), f32),
        pltpu.VMEM((1, atoms), i32),
        pltpu.VMEM((2, GHOST), i32),
        pltpu.SMEM(paired_partner_lists.shape, i32),
        pltpu.SMEM((cells,), i32),
        pltpu.VMEM((na, 3, 1, atoms), f32),
        pltpu.VMEM((na, depth, 2 * atoms), bf16),
        pltpu.VMEM((na, 16, atoms), f32),
        pltpu.VMEM((na, 16, atoms), f32),
        pltpu.VMEM((na, 16, atoms), f32),
        pltpu.VMEM((na, 16, atoms), f32),
        pltpu.VMEM((wide, depth), f32),
        pltpu.VMEM((wide, depth), bf16),
        pltpu.VMEM((3, wide, depth), bf16),
        pltpu.VMEM((2, 4, edge, depth), bf16),
        pltpu.VMEM((planes, 2, 16, depth), f32),
        pltpu.VMEM((1, atoms), f32),
        pltpu.VMEM((1, atoms), f32),
        pltpu.VMEM((wide, depth), bf16),
        pltpu.VMEM((na, 3, 1, atoms), f32),
        pltpu.VMEM((na, 3, 1, atoms), f32),
        pltpu.VMEM((2, 4, 1, GHOST), f32),
        pltpu.VMEM((4, 1, GHOST), f32),
        pltpu.VMEM((4, 1, GHOST), f32),
        pltpu.VMEM((blocks, 1, CELL), f32),
        pltpu.VMEM((blocks, 1, CELL), f32),
        pltpu.VMEM((blocks, 1, CELL), i32),
        pltpu.VMEM((blocks, 1, CELL), i32),
        pltpu.VMEM((atoms, CELL), f32),
        pltpu.VMEM((atoms, CELL), i32),
        pltpu.VMEM((atoms, CELL), i32),
        pltpu.VMEM((3, atoms, CELL), f32),
        pltpu.VMEM((bricks, 1, CELL), f32),
        pltpu.SemaphoreType.DMA((14,)),
    ]
    for count in (na, 2, 2, 4, 8, na, bricks):
        scratch += [pltpu.SemaphoreType.DMA((count,))] * 2
    tall = lambda v: v.reshape(3, 1, atoms)
    new_positions, new_velocities, deviation = pl.pallas_call(
        functools.partial(kernel, (members, bricks, thick, rows, depth, atoms)),
        out_shape=(
            jax.ShapeDtypeStruct((3, 1, atoms), f32),
            jax.ShapeDtypeStruct((3, 1, atoms), f32),
            jax.ShapeDtypeStruct((thick, rows // members, depth), f32),
        ),
        in_specs=[hbm] * 10 + [smem] + [hbm] * 2,
        out_specs=(vmem, vmem, vmem),
        scratch_shapes=scratch,
        compiler_params=pltpu.CompilerParams(
            collective_id=0, has_side_effects=True, vmem_limit_bytes=40 * 2**20
        ),
        cost_estimate=pl.CostEstimate(
            flops=1_200_000_000, bytes_accessed=400_000, transcendentals=4_000_000
        ),
    )(
        *(
            pltpu.with_memory_space_constraint(v, pltpu.HBM)
            for v in (
                tall(atom_locations),
                tall(atom_speeds_vector),
                inertial_amounts,
                electric_loads,
                scatter_strengths,
                gaussian_spreads_sigma,
                atom_present_flags,
                halo_sender_spots,
                paired_partner_lists,
                cell_usage_tally,
            )
        ),
        target_warmth_levels.reshape(1, 1),
        pltpu.with_memory_space_constraint(observed_volume_values, pltpu.HBM),
        pltpu.with_memory_space_constraint(voxel_reciprocal_spread, pltpu.HBM),
    )
    made = (new_positions, new_velocities, deviation)
    new_positions, new_velocities, deviation = pl.pallas_call(
        functools.partial(write, len(made)),
        out_shape=tuple(jax.ShapeDtypeStruct(v.shape, v.dtype) for v in made),
        in_specs=[vmem] * len(made),
        out_specs=tuple(hbm for _ in made),
        scratch_shapes=[pltpu.SemaphoreType.DMA((len(made),))],
    )(*(pltpu.with_memory_space_constraint(v, pltpu.VMEM) for v in made))
    return (
        new_positions.reshape(1, 3, atoms),
        new_velocities.reshape(1, 3, atoms),
        deviation,
    )


def solution(mesh):
    return jax.shard_map(
        local,
        mesh=mesh,
        in_specs=(
            P("replica", None, "brick"),
            P("replica", None, "brick"),
            P("brick"),
            P("brick"),
            P("brick"),
            P("brick"),
            P("brick"),
            P("brick", None, None),
            P("brick", None, None),
            P("brick", None),
            P("brick"),
            P(None, "brick"),
            P("replica"),
        ),
        out_specs=(
            P("replica", None, "brick"),
            P("replica", None, "brick"),
            P("brick", "replica", None),
        ),
        check_vma=False,
    )
```

```python
import functools
import math

import jax
import jax.numpy as jnp
from jax import lax
from jax.experimental import pallas as pl
from jax.experimental.pallas import tpu as pltpu
from jax.sharding import PartitionSpec as P

MESH = pl.DeviceIdType.MESH

HALO = 2
CELL = 128
GHOST = 256
LOG2E = 1.4426950408889634
B_STEPS = ((0, 0), (0, 1), (1, 0), (1, 1))

restraint = 0.1
coupling = 5.0
softening = 1.0
timestep = 0.5
boltzmann = 0.015
heat_bath_damping = 0.5


def fixed(coord, period):
    scale = 2.0**31 / period
    return (coord * scale).astype(jnp.int32) << 1


def dot_t(a, b):
    return lax.dot_general(a, b, (((1,), (1,)), ((), ())), preferred_element_type=jnp.float32)


def kernel(
    dims,
    loc_at,
    vel_at,
    mass_at,
    load_at,
    strength_at,
    sigma_at,
    flag_at,
    spots_at,
    lists_at,
    tally_at,
    warm,
    obs,
    vrs,
    pos_out,
    vel_out,
    dev_out,
    vel,
    mass_ref,
    load_ref,
    strength_ref,
    sigma_ref,
    flag_ref,
    spots,
    lists,
    tally,
    crd,
    zz,
    gxs,
    gxds,
    gys,
    gyds,
    acc,
    mine,
    rs,
    halo,
    obv,
    amps,
    ivs,
    grd,
    frc,
    frcin,
    gsend,
    glo,
    ghi,
    bx,
    bq,
    by,
    bz,
    colx,
    coly,
    colz,
    pacc,
    kin,
    loc_sem,
    crd_ss,
    crd_rs,
    gh_ss,
    gh_rs,
    ob_ss,
    ob_rs,
    rs_ss,
    rs_rs,
    hl_ss,
    hl_rs,
    fr_ss,
    fr_rs,
    kn_ss,
    kn_rs,
):
    members, bricks, thick, rows, depth, atoms = dims
    half = members // 2
    na = half // 2
    share = rows // members
    planes = thick + 2 * HALO
    wide = planes * 16
    edge = 2 * HALO * 16
    cells = atoms // CELL
    slots = lists.shape[1]
    r = lax.axis_index("replica")
    b = lax.axis_index("brick")
    x, z = r // half, r % half
    zh, zp = z // 2, z % 2
    up, down = (b + 1) % bricks, (b + bricks - 1) % bricks

    def a_peer(d):
        return (x * half + ((zh + d) % na) * 2 + zp, b)

    def b_rep(k):
        dx, dp = B_STEPS[k]
        return ((x + dx) % 2) * half + zh * 2 + (zp + dp) % 2

    def brick_at(n):
        y, xh, core = n // 4, n // 2 % 2, n % 2
        return (b // 4 + y) % (bricks // 4) * 4 + (b // 2 + xh) % 2 * 2 + (b + core) % 2

    far_first = sorted(
        range(1, bricks), key=lambda n: -(min(n // 4, 4 - n // 4) + n // 2 % 2 * 2 + n % 2)
    )

    def nearest(t):
        odd = t % 2
        return odd * ((t + 1) // 2) + (1 - odd) * ((na - t // 2) % na)

    direct = [nearest(t) for t in range(1, na)]
    relayed = {}
    if na == 8:
        direct = direct[:4]
        relayed = {1: (3, 2), 7: (5, 6), 2: (4, 2)}

    barrier = pltpu.get_barrier_semaphore()
    partners = [a_peer(d) for d in reversed(direct)]
    partners += [(r, brick_at(n)) for n in far_first]
    partners += [(b_rep(k), b) for k in range(1, 4)]
    for p in partners:
        pl.semaphore_signal(barrier, inc=1, device_id=p, device_id_type=MESH)

    fetched = {
        "loc": (loc_at, crd.at[0]),
        "flag": (flag_at, flag_ref.at[0]),
        "strength": (strength_at, strength_ref.at[0]),
        "load": (load_at, load_ref.at[0]),
        "sigma": (sigma_at, sigma_ref.at[0]),
        "spots": (spots_at, spots),
        "lists": (lists_at, lists),
        "tally": (tally_at, tally),
        "vel": (vel_at, vel),
        "mass": (mass_at, mass_ref.at[0]),
    }
    for t in range(2):
        tile = pl.ds(pl.multiple_of(t * (rows // 2) + zh * 8, 8), 8)
        for i, src in enumerate((obs, vrs)):
            fetched["map", t, i] = (src.at[:, tile, :], obv.at[pl.ds(HALO, thick), i, pl.ds(8 * t, 8)])
    copies = {
        name: pltpu.make_async_copy(src, dst, loc_sem.at[i])
        for i, (name, (src, dst)) in enumerate(fetched.items())
    }
    for c in copies.values():
        c.start()
    copies["loc"].wait()
    sends = []

    def remote(src, dst, ss, rsem, device):
        return pltpu.make_async_remote_copy(
            src_ref=src, dst_ref=dst, send_sem=ss, recv_sem=rsem, device_id=device, device_id_type=MESH
        )

    def post(*a):
        c = remote(*a)
        c.start()
        sends.append(c)
        return c

    for name in ("flag", "strength", "load", "sigma", "spots"):
        copies[name].wait()
    loc = crd.at[0]
    occ = flag_ref[...].astype(jnp.float32)
    amp = occ * strength_ref[...]
    q = occ * load_ref[...]
    sigma = sigma_ref[...]
    iv = 1.0 / (sigma * sigma)

    four = jnp.concatenate([loc[0], loc[1], loc[2], q], axis=0)
    first = four.astype(jnp.bfloat16).astype(jnp.float32)
    rest = four - first
    second = rest.astype(jnp.bfloat16).astype(jnp.float32)
    third = rest - second
    pieces = jnp.concatenate([first, second, third, jnp.zeros_like(four)], axis=0).astype(jnp.bfloat16)
    slot_of = lax.broadcasted_iota(jnp.int32, (atoms, GHOST), 0)
    for side in range(2):
        chosen = jnp.where(slot_of == spots[side : side + 1, :], 1.0, 0.0).astype(jnp.bfloat16)
        got = jnp.dot(pieces, chosen, preferred_element_type=jnp.float32)
        got = got[0:4] + got[4:8] + got[8:12]
        for i in range(4):
            gsend[side, i] = got[i : i + 1]

    shift_y, shift_z = 32 - int(math.log2(rows)), 32 - int(math.log2(depth))
    unit_y, unit_z = 2.0**-shift_y, 2.0**-shift_z
    amps[...] = amp
    ivs[...] = iv

    def spread(d):
        amp, iv = amps[...], ivs[...]
        ivc = iv * (-0.5 * LOG2E)
        plane_at = (b * thick - HALO + lax.broadcasted_iota(jnp.int32, (16, atoms), 0)).astype(jnp.float32)
        row_in = lax.broadcasted_iota(jnp.int32, (16, atoms), 0)
        row_at = (zh * 8 + (row_in // 8) * (rows // 2) + row_in % 8) << shift_y
        dx = plane_at - crd[d, 0]
        gx = jnp.exp2(dx * dx * ivc)
        gxs[d] = gx
        gxds[d] = dx * iv * gx
        dy = (row_at - fixed(crd[d, 1], rows)).astype(jnp.float32)
        gy = jnp.exp2(dy * dy * (ivc * unit_y**2))
        gys[d] = gy
        gyds[d] = dy * (iv * unit_y) * gy
        level = lax.broadcasted_iota(jnp.int32, (depth, atoms), 0) << shift_z
        dz = (level - fixed(crd[d, 2], depth)).astype(jnp.float32)
        gz = jnp.exp2(dz * dz * (ivc * unit_z**2))
        zz[d, :, atoms:] = (dz * (iv * unit_z) * gz).astype(jnp.bfloat16)
        gzb = gz.astype(jnp.bfloat16)
        zz[d, :, :atoms] = gzb
        left = (amp * gx)[:planes, None, :] * gy[None]
        part = dot_t(left.reshape(wide, atoms).astype(jnp.bfloat16), gzb)
        if isinstance(d, int):
            acc[...] = part
        else:
            acc[...] += part

    spread(0)

    pl.semaphore_wait(barrier, len(partners))
    crd_in = {}
    for d in reversed(direct):
        crd_in[d] = post(crd.at[0], crd.at[d], crd_ss.at[d], crd_rs.at[d], a_peer(d))
    gh_in = [
        post(gsend.at[0], glo, gh_ss.at[0], gh_rs.at[0], (r, up)),
        post(gsend.at[1], ghi, gh_ss.at[1], gh_rs.at[1], (r, down)),
    ]
    for t in range(2):
        for i in range(2):
            copies["map", t, i].wait()
    ob_in = [
        post(obv.at[pl.ds(thick, HALO)], obv.at[pl.ds(0, HALO)], ob_ss.at[0], ob_rs.at[0], (r, up)),
        post(
            obv.at[pl.ds(HALO, HALO)],
            obv.at[pl.ds(thick + HALO, HALO)],
            ob_ss.at[1],
            ob_rs.at[1],
            (r, down),
        ),
    ]


    def column(c, _):
        at = pl.ds(pl.multiple_of(c * CELL, CELL), CELL)
        for i, col in enumerate((colx, coly, colz)):
            v = jnp.broadcast_to(loc[i, :, at], (CELL, CELL)).T
            col[at] = v * 2.0**shift_z if i == 0 else fixed(v, (rows, depth)[i - 1])
        return 0

    lax.fori_loop(0, cells, column, 0)

    scale_x = 2.0**shift_z
    for c in range(cells):
        at = slice(c * CELL, (c + 1) * CELL)
        bx[c] = loc[0, :, at] * scale_x
        by[c] = fixed(loc[1, :, at], rows)
        bz[c] = fixed(loc[2, :, at], depth)
        bq[c] = q[:, at]
    none = cells + 4
    for ref in (bx, bq, by, bz):
        ref[none] = jnp.zeros((1, CELL), ref.dtype)

    def await_crd(d):
        crd_in[d].wait_recv()
        if d in relayed:
            far, to = relayed[d]
            crd_in[far] = post(crd.at[d], crd.at[far], crd_ss.at[far], crd_rs.at[far], a_peer(to))

    early = (1, 7, 2) if na == 8 else ()
    for d in early:
        await_crd(d)

    def collect(t, _):
        d = nearest(t)

        @pl.when(t > len(early))
        def _():
            remote(crd.at[0], crd.at[d], crd_ss.at[d], crd_rs.at[d], a_peer(d)).wait_recv()

        spread(d)
        return 0

    lax.fori_loop(1, na, collect, 0)

    mine[...] = acc[...].astype(jnp.bfloat16)
    for c in gh_in:
        c.wait_recv()

    core = b % 2

    def post_edge(side, k):
        start = pl.multiple_of((1 - side) * (wide - edge), 16)
        at = side * 4 + k
        post(
            mine.at[pl.ds(start, edge)],
            halo.at[side, k],
            hl_ss.at[at],
            hl_rs.at[at],
            (b_rep(k), (b + bricks + 1 - 2 * side) % bricks),
        )

    map_in = []

    def post_map(k):
        map_in.append(post(mine, rs.at[k - 1], rs_ss.at[k], rs_rs.at[k], (b_rep(k), b)))

    for k in (1, 0, 3, 2):
        post_edge(1 - core, k)
    post_map(3)
    for k in (3, 1):
        post_edge(core, k)
    post_map(1)
    post_edge(core, 2)
    post_map(2)
    post_edge(core, 0)
    for side in range(2):
        for k in range(4):
            at = side * 4 + k
            map_in.append(
                remote(mine.at[pl.ds(0, edge)], halo.at[side, k], hl_ss.at[at], hl_rs.at[at], (b_rep(k), up))
            )

    period_x = float(thick * bricks)
    for side, src in enumerate((glo, ghi)):
        if side == 0:
            move = jnp.where(b == 0, -period_x, 0.0)
        else:
            move = jnp.where(b == bricks - 1, period_x, 0.0)
        for g in range(2):
            at = slice(g * CELL, (g + 1) * CELL)
            n = cells + 2 * side + g
            bx[n] = (src[0, :, at] + move) * scale_x
            by[n] = fixed(src[1, :, at], rows)
            bz[n] = fixed(src[2, :, at], depth)
            bq[n] = src[3, :, at]

    part_rows = 32
    parts = CELL // part_rows

    def pair(u, _):
        c = u // parts
        at = pl.ds(pl.multiple_of(u * part_rows, part_rows), part_rows)
        xi, yi, zi = colx[at], coly[at], colz[at]
        total = [jnp.zeros((part_rows, CELL), jnp.float32)] * 3
        for s in range(slots):
            n = jnp.where(s < tally[c], lists[c, s], none)
            dx = xi - bx[n]
            dy = (yi - by[n]).astype(jnp.float32)
            dz = (zi - bz[n]).astype(jnp.float32)
            if shift_y != shift_z:
                dy = dy * 2.0 ** (shift_z - shift_y)
            inv = lax.rsqrt(dx * dx + dy * dy + dz * dz + softening * 4.0**shift_z)
            pull = inv * inv * inv * bq[n]
            total = [total[0] + pull * dx, total[1] + pull * dy, total[2] + pull * dz]
        for i in range(3):
            pacc[i, at] = total[i]
        return 0

    units = cells * parts
    copies["lists"].wait()
    copies["tally"].wait()
    lax.fori_loop(0, units // 2, pair, 0)

    for c in ob_in + map_in:
        c.wait_recv()
    wider = lambda v: v.astype(jnp.float32)
    total = acc[...] + wider(rs[0]) + wider(rs[1]) + wider(rs[2])
    low, high = (
        wider(halo[i, 0]) + wider(halo[i, 1]) + wider(halo[i, 2]) + wider(halo[i, 3]) for i in range(2)
    )
    total = jnp.concatenate(
        [total[:edge] + low, total[edge : wide - edge], total[wide - edge :] + high], axis=0
    ).reshape(planes, 16, depth)
    dev = total / members - obv[:, 0]
    grad = (restraint * obv[:, 1] * dev).astype(jnp.bfloat16)
    grd[...] = grad.reshape(wide, depth)

    lanes = 256

    def force(d):
        for c in range(atoms // lanes):
            at = slice(c * lanes, (c + 1) * lanes)
            after = slice(atoms + c * lanes, atoms + (c + 1) * lanes)
            along = jnp.dot(grd[...], zz[d, :, at], preferred_element_type=jnp.float32)
            slope = jnp.dot(grd[...], zz[d, :, after], preferred_element_type=jnp.float32)
            sums = [0.0, 0.0, 0.0]
            for i in range(planes):
                p = along[16 * i : 16 * i + 16]
                g = gxs[d, i : i + 1, at]
                sums[0] += gxds[d, i : i + 1, at] * p
                sums[1] += g * p
                sums[2] += g * slope[16 * i : 16 * i + 16]
            y = gys[d, :, at]
            f = (y * sums[0], gyds[d, :, at] * sums[1], y * sums[2])
            for i in range(3):
                frc[d, i, :, at] = jnp.sum(f[i], axis=0, keepdims=True)

    def fr_copy(d):
        return remote(frc.at[d], frcin.at[d], fr_ss.at[d], fr_rs.at[d], a_peer((na - d) % na))

    def give(t, _):
        d = nearest(na - 1 - t)
        force(d)

        @pl.when(t < na - 1)
        def _():
            fr_copy(d).start()

        return 0

    lax.fori_loop(0, na, give, 0)

    own = dev[HALO : HALO + thick]
    own = jnp.where(x == 0, own[:, :8], own[:, 8:])
    dev_out[...] = jnp.where(zp == 0, own[:, :share], own[:, share:])

    lax.fori_loop(units // 2, units, pair, 0)
    for name in ("vel", "mass"):
        copies[name].wait()
    mass = mass_ref[...]
    light = timestep / mass
    gain = (coupling * 4.0**shift_z) * q * light
    push = amps[...] * light
    v_half = []
    for i in range(3):
        line = [
            jnp.sum(pacc[i, c * CELL : (c + 1) * CELL].T, axis=0, keepdims=True) for c in range(cells)
        ]
        v_half.append(vel[i] + gain * jnp.concatenate(line, axis=1))

    forces = [frc[0, i] for i in range(3)]
    for d in (nearest(t) for t in range(1, na)):
        fr_copy(d).wait_recv()
        forces = [f + frcin[d, i] for i, f in enumerate(forces)]
    square = jnp.zeros((1, atoms), jnp.float32)
    for i in range(3):
        v_half[i] = v_half[i] - push * forces[i]
        square = square + v_half[i] * v_half[i]
    square = mass * square
    row = square[:, :CELL]
    for c in range(1, cells):
        row = row + square[:, c * CELL : (c + 1) * CELL]
    kin[0] = row
    kn_in = [
        post(kin.at[0], kin.at[n], kn_ss.at[n], kn_rs.at[n], (r, brick_at(n)))
        for n in far_first
    ]
    for c in kn_in:
        c.wait_recv()
    for d in range(1, bricks):
        row = row + kin[d]
    kinetic = jnp.sum(row, axis=1, keepdims=True)
    present = kinetic / (3 * atoms * bricks * boltzmann) + 1e-06
    wanted = jnp.full((1, 1), warm[0, 0].astype(jnp.float32))
    ratio = jnp.sqrt(1.0 + heat_bath_damping * (wanted / present - 1.0))
    for i in range(3):
        v = ratio * v_half[i]
        vel_out[i] = v
        pos_out[i] = loc[i] + timestep * v
    for d in range(1, na):
        fr_copy(d).wait_send()
    for c in sends:
        c.wait_send()


def write(count, *refs):
    sources, targets, sem = refs[:count], refs[count:-1], refs[-1]
    copies = [pltpu.make_async_copy(a, c, sem.at[i]) for i, (a, c) in enumerate(zip(sources, targets))]
    for c in copies:
        c.start()
    for c in copies:
        c.wait()


def local(
    atom_locations,
    atom_speeds_vector,
    inertial_amounts,
    electric_loads,
    scatter_strengths,
    gaussian_spreads_sigma,
    atom_present_flags,
    observed_volume_values,
    voxel_reciprocal_spread,
    paired_partner_lists,
    cell_usage_tally,
    halo_sender_spots,
    target_warmth_levels,
):
    thick, rows, depth = observed_volume_values.shape
    atoms = atom_locations.shape[2]
    members, bricks = lax.axis_size("replica"), lax.axis_size("brick")
    na = members // 4
    planes = thick + 2 * HALO
    wide = planes * 16
    cells = atoms // CELL
    blocks = cells + 5
    f32, bf16, i32 = jnp.float32, jnp.bfloat16, jnp.int32
    vmem = pl.BlockSpec(memory_space=pltpu.VMEM)
    hbm = pl.BlockSpec(memory_space=pltpu.HBM)
    smem = pl.BlockSpec(memory_space=pltpu.SMEM)
    edge = 2 * HALO * 16
    scratch = [
        pltpu.VMEM((3, 1, atoms), f32),
        pltpu.VMEM((1, atoms), f32),
        pltpu.VMEM((1, atoms), f32),
        pltpu.VMEM((1, atoms), f32),
        pltpu.VMEM((1, atoms), f32),
        pltpu.VMEM((1, atoms), i32),
        pltpu.VMEM((2, GHOST), i32),
        pltpu.SMEM(paired_partner_lists.shape, i32),
        pltpu.SMEM((cells,), i32),
        pltpu.VMEM((na, 3, 1, atoms), f32),
        pltpu.VMEM((na, depth, 2 * atoms), bf16),
        pltpu.VMEM((na, 16, atoms), f32),
        pltpu.VMEM((na, 16, atoms), f32),
        pltpu.VMEM((na, 16, atoms), f32),
        pltpu.VMEM((na, 16, atoms), f32),
        pltpu.VMEM((wide, depth), f32),
        pltpu.VMEM((wide, depth), bf16),
        pltpu.VMEM((3, wide, depth), bf16),
        pltpu.VMEM((2, 4, edge, depth), bf16),
        pltpu.VMEM((planes, 2, 16, depth), f32),
        pltpu.VMEM((1, atoms), f32),
        pltpu.VMEM((1, atoms), f32),
        pltpu.VMEM((wide, depth), bf16),
        pltpu.VMEM((na, 3, 1, atoms), f32),
        pltpu.VMEM((na, 3, 1, atoms), f32),
        pltpu.VMEM((2, 4, 1, GHOST), f32),
        pltpu.VMEM((4, 1, GHOST), f32),
        pltpu.VMEM((4, 1, GHOST), f32),
        pltpu.VMEM((blocks, 1, CELL), f32),
        pltpu.VMEM((blocks, 1, CELL), f32),
        pltpu.VMEM((blocks, 1, CELL), i32),
        pltpu.VMEM((blocks, 1, CELL), i32),
        pltpu.VMEM((atoms, CELL), f32),
        pltpu.VMEM((atoms, CELL), i32),
        pltpu.VMEM((atoms, CELL), i32),
        pltpu.VMEM((3, atoms, CELL), f32),
        pltpu.VMEM((bricks, 1, CELL), f32),
        pltpu.SemaphoreType.DMA((14,)),
    ]
    for count in (na, 2, 2, 4, 8, na, bricks):
        scratch += [pltpu.SemaphoreType.DMA((count,))] * 2
    tall = lambda v: v.reshape(3, 1, atoms)
    new_positions, new_velocities, deviation = pl.pallas_call(
        functools.partial(kernel, (members, bricks, thick, rows, depth, atoms)),
        out_shape=(
            jax.ShapeDtypeStruct((3, 1, atoms), f32),
            jax.ShapeDtypeStruct((3, 1, atoms), f32),
            jax.ShapeDtypeStruct((thick, rows // members, depth), f32),
        ),
        in_specs=[hbm] * 10 + [smem] + [hbm] * 2,
        out_specs=(vmem, vmem, vmem),
        scratch_shapes=scratch,
        compiler_params=pltpu.CompilerParams(
            collective_id=0, has_side_effects=True, vmem_limit_bytes=40 * 2**20
        ),
        cost_estimate=pl.CostEstimate(
            flops=1_200_000_000, bytes_accessed=400_000, transcendentals=4_000_000
        ),
    )(
        *(
            pltpu.with_memory_space_constraint(v, pltpu.HBM)
            for v in (
                tall(atom_locations),
                tall(atom_speeds_vector),
                inertial_amounts,
                electric_loads,
                scatter_strengths,
                gaussian_spreads_sigma,
                atom_present_flags,
                halo_sender_spots,
                paired_partner_lists,
                cell_usage_tally,
            )
        ),
        target_warmth_levels.reshape(1, 1),
        pltpu.with_memory_space_constraint(observed_volume_values, pltpu.HBM),
        pltpu.with_memory_space_constraint(voxel_reciprocal_spread, pltpu.HBM),
    )
    made = (new_positions, new_velocities, deviation)
    new_positions, new_velocities, deviation = pl.pallas_call(
        functools.partial(write, len(made)),
        out_shape=tuple(jax.ShapeDtypeStruct(v.shape, v.dtype) for v in made),
        in_specs=[vmem] * len(made),
        out_specs=tuple(hbm for _ in made),
        scratch_shapes=[pltpu.SemaphoreType.DMA((len(made),))],
    )(*(pltpu.with_memory_space_constraint(v, pltpu.VMEM) for v in made))
    return (
        new_positions.reshape(1, 3, atoms),
        new_velocities.reshape(1, 3, atoms),
        deviation,
    )


def solution(mesh):
    return jax.shard_map(
        local,
        mesh=mesh,
        in_specs=(
            P("replica", None, "brick"),
            P("replica", None, "brick"),
            P("brick"),
            P("brick"),
            P("brick"),
            P("brick"),
            P("brick"),
            P("brick", None, None),
            P("brick", None, None),
            P("brick", None),
            P("brick"),
            P(None, "brick"),
            P("replica"),
        ),
        out_specs=(
            P("replica", None, "brick"),
            P("replica", None, "brick"),
            P("brick", "replica", None),
        ),
        check_vma=False,
    )
```
